32 devices in a mesh: grp: 8 (over y, x, core), ep: 4 (over z).
Axes of the slice: x: 2, y: 2, z: 4, core: 2. Of those that a mesh axis runs over, the one named last changes fastest.
Arguments:
- tokens: bfloat16 [128, 197, 512], P(('grp', 'ep')), may hold values from -6 to 6
- routes: int32 [128, 197, 2], P(('grp', 'ep')), may hold values from 0 to 7, all different within a row; in each aligned block of 788 rows (0 to 787, 788 to 1575, ..., all dimensions but the last counted through in order) at most 247 rows name the same one
- gates: float32 [128, 197, 2], P(('grp', 'ep')), may hold values from 0 to 1, as said below
- ln1_gain: float32 [512], replicated, may hold values from 0.5 to 1.5
- ln1_bias: float32 [512], replicated, may hold values from -0.6 to 0.6
- w_qkv: bfloat16 [512, 1536], replicated, may hold values from -0.25 to 0.25
- w_out: bfloat16 [512, 512], replicated, may hold values from -1 to 1
- out_bias: float32 [512], replicated, may hold values from -0.6 to 0.6
- ln2_gain: float32 [512], replicated, may hold values from 0.5 to 1.5
- ln2_bias: float32 [512], replicated, may hold values from -0.6 to 0.6
- w_in: bfloat16 [8, 512, 2048], P('ep'), may hold values from -0.25 to 0.25
- in_bias: float32 [8, 2048], P('ep'), may hold values from -0.6 to 0.6
- w_back: bfloat16 [8, 2048, 512], P('ep'), may hold values from -0.125 to 0.125
- back_bias: float32 [8, 512], P('ep'), may hold values from -0.6 to 0.6
- cotangent: bfloat16 [128, 197, 512], P(('grp', 'ep')), may hold values from -6 to 6
Outputs:
- output: bfloat16 [128, 197, 512], P(('grp', 'ep'))
- grad_tokens: bfloat16 [128, 197, 512], P(('grp', 'ep'))
- grad_ln1_gain: float32 [512], P('ep')
- grad_ln1_bias: float32 [512], P('ep')
- grad_w_qkv: float32 [512, 1536], P('ep')
- grad_w_out: float32 [512, 512], P('ep')
- grad_out_bias: float32 [512], P('ep')
- grad_ln2_gain: float32 [512], P('ep')
- grad_ln2_bias: float32 [512], P('ep')
- grad_w_in: float32 [8, 512, 2048], P('ep')
- grad_in_bias: float32 [8, 2048], P('ep')
- grad_w_back: float32 [8, 2048, 512], P('ep')
- grad_back_bias: float32 [8, 512], P('ep')
The draws below stay inside these ranges and needn't reach their ends.
Inputs may be any that keep to these rules, and one draw needn't show every extreme that they name: `routes`: the two experts of a token differ; no block of 788 tokens names one expert more than 247 times, and some block names some expert exactly 247 times. A token's two gates are positive and sum to one.
All inputs are finite; a program needn't handle non-finite values.
Results may differ from the reference program's by a relative error of at most 0.02.
Values may be sent and summed in bfloat16 or wider, within the bound.
No kernel may reach another device: no remote copies, remote signals or barrier semaphores. Data moves between devices by JAX's collectives and lax.ppermute only.
A program may use at most 192 MiB of HBM per device.

```python
import math
import jax
import jax.numpy as jnp
import numpy as np
from jax import lax

D = 512
HEADS = 8
HD = 64
FF = 2048
SEQ = 197
IMAGES = 128
TOK_DEV = 788
EXPERTS = 8
CAP = 247
N_GRP = 8
N_EP = 4


def draw_gates(key, part):
    key = jax.random.fold_in(key, 7)
    logits = 0.7 * jax.random.normal(key, (IMAGES, SEQ, 2), jnp.float32)
    return jax.nn.softmax(logits, axis=-1)


def steps_of(rng, extent, pieces, low, high):
    level, own = 1.0, jax.random.fold_in(rng, 6)
    for axis_at, parts in pieces:
        steps = jnp.exp(jax.random.uniform(jax.random.fold_in(own, axis_at), (parts,), jnp.float32, low / len(pieces), high / len(pieces)))
        level = level * jnp.repeat(steps, extent[axis_at] // parts).reshape([-1 if axis == axis_at else 1 for axis in range(len(extent))])
    return level


def assign_block(rng, own, number, rows, number_of, top, limit, slope):
    order = jax.random.permutation(rng, number_of)
    packed, common = shares(number_of, rows * top, limit, slope, True), shares(number_of, rows * top, limit, slope, False)
    places = jnp.arange(number_of)

    def named(tallies, rotation):
        used = int((tallies > 0).sum())
        fixed = max(1, used // 4)
        passed = fixed + (places - fixed + rotation * (used - fixed)) % max(1, number_of - fixed)
        return jnp.zeros((number_of,), jnp.int32).at[order[jnp.where(places < fixed, places, passed)]].set(jnp.asarray(tallies, jnp.int32))

    tallies = jnp.where(number % 4 == 0, named(packed, number // 4), named(common, number - number // 4 - 1))
    mixed = jax.random.permutation(jax.random.fold_in(own, 3), number_of)
    source_of, sink = mixed[0:number_of // 2 * 2:2], mixed[1:number_of // 2 * 2:2]
    margin = jnp.minimum(tallies[source_of] - 1, limit - tallies[sink]) // 2
    margin = jnp.where((source_of == order[0]) | (sink == order[0]) | (tallies[sink] == 0), 0, jnp.maximum(margin, 0))
    passed = jax.random.randint(jax.random.fold_in(own, 4), (number_of // 2,), 0, 1 << 20) % (margin + 1)
    tallies = tallies.at[source_of].add(-passed).at[sink].add(passed)
    items = jnp.searchsorted(jnp.cumsum(tallies), jnp.arange(rows * top), side="right").astype(jnp.int32)
    listing = items.reshape(top, rows).T
    listing = listing[jax.random.permutation(jax.random.fold_in(own, 1), rows)]
    rotation = jax.random.randint(jax.random.fold_in(own, 2), (rows, 1), 0, top)
    return jnp.take_along_axis(listing, (jnp.arange(top)[None, :] + rotation) % top, axis=1)


def shares(count, total, most, lean, full):
    portions = [(1 << 20) // math.isqrt(grade ** lean) + 1 for grade in range(1, count + 1)]
    largest = most if full else min(most, max(-(-total // count), total * portions[0] // sum(portions)))
    least = 1 if total - largest >= count - 1 else 0
    given, surplus = [largest] + [least] * (count - 1), total - largest - least * (count - 1)
    while surplus > 0:
        movable = [i for i in range(1, count) if given[i] < largest] or [i for i in range(1, count) if given[i] < most]
        whole, left = sum([portions[i] for i in movable]), surplus
        for i in movable:
            extra = min(most - given[i], max(1, left * portions[i] // whole), surplus)
            given[i] = given[i] + extra
            surplus = surplus - extra
    return np.array(given)


def gaussian(rng, extent, scale, limit, cuts=(), kind=jnp.bfloat16):
    level = steps_of(rng, extent, cuts, -0.22, 0.18) if cuts else 1.0
    entries = jax.random.normal(rng, extent, jnp.float32) * scale * level
    return jnp.minimum(jnp.maximum(entries, -limit), limit).astype(kind)


def setup_inputs(seed: int = 0) -> dict:
    keys = jax.random.split(jax.random.key(seed), 16)
    tokens = gaussian(keys[0], (IMAGES, SEQ, D), 1.0, 6.0, ((0, 32),))
    routes_keys = jax.random.split(jax.random.fold_in(keys[1], 1), IMAGES * SEQ // TOK_DEV)
    routes_turns = jax.random.permutation(jax.random.fold_in(keys[1], 3), IMAGES * SEQ // TOK_DEV)
    routes = jax.vmap(lambda own, number: assign_block(jax.random.fold_in(keys[1], 2), own, number, TOK_DEV, EXPERTS, 2, CAP, 1))(routes_keys, routes_turns).reshape((IMAGES, SEQ, 2))
    gates = draw_gates(jax.random.fold_in(keys[15], 71), 0)
    ln1_gain = jnp.clip(1.0 + 0.1 * jax.random.normal(keys[3], (D,), jnp.float32), 0.5, 1.5)
    ln1_bias = gaussian(keys[4], (D,), 0.1, 0.6, (), jnp.float32)
    w_qkv = gaussian(keys[5], (D, 3 * D), D ** -0.5, 0.25)
    w_out = gaussian(keys[6], (D, D), (D // 16) ** -0.5, 1.0)
    out_bias = gaussian(keys[7], (D,), 0.1, 0.6, (), jnp.float32)
    ln2_gain = jnp.clip(1.0 + 0.1 * jax.random.normal(keys[8], (D,), jnp.float32), 0.5, 1.5)
    ln2_bias = gaussian(keys[9], (D,), 0.1, 0.6, (), jnp.float32)
    w_in = gaussian(keys[10], (EXPERTS, D, FF), D ** -0.5, 0.25, ((0, 4),))
    in_bias = gaussian(keys[11], (EXPERTS, FF), 0.1, 0.6, ((0, 4),), jnp.float32)
    w_back = gaussian(keys[12], (EXPERTS, FF, D), FF ** -0.5, 0.125, ((0, 4),))
    back_bias = gaussian(keys[13], (EXPERTS, D), 0.1, 0.6, ((0, 4),), jnp.float32)
    cotangent = gaussian(keys[14], (IMAGES, SEQ, D), 1.0, 6.0, ((0, 32),))
    return {"tokens": tokens, "routes": routes, "gates": gates, "ln1_gain": ln1_gain, "ln1_bias": ln1_bias, "w_qkv": w_qkv, "w_out": w_out, "out_bias": out_bias, "ln2_gain": ln2_gain, "ln2_bias": ln2_bias, "w_in": w_in, "in_bias": in_bias, "w_back": w_back, "back_bias": back_bias, "cotangent": cotangent}


@jax.custom_vjp
def low(v):
    return lax.optimization_barrier(v.astype(jnp.bfloat16)).astype(jnp.float32)

@jax.custom_vjp
def low_back(v):
    return v

def low_keep(v):
    return (low(v), None)

def low_pass(kept, grad):
    return (grad,)

def back_keep(v):
    return (v, None)

def back_low(kept, grad):
    return (low(grad),)
low.defvjp(low_keep, low_pass)
low_back.defvjp(back_keep, back_low)
NORM_EPS = 1e-06

def exact_dot(left, right):
    return jnp.dot(left, right, precision=lax.Precision.HIGHEST)

def layer_norm(values, gain, bias):
    average = lax.optimization_barrier(jnp.mean(values, axis=-1, keepdims=True))
    centred = values - average
    variance = lax.optimization_barrier(jnp.mean(centred * centred, axis=-1, keepdims=True))
    return centred * lax.rsqrt(variance + NORM_EPS) * gain + bias

def slot_of(route_rows, expert_count):
    flat = route_rows.reshape(-1)
    onehot = (flat[:, None] == jnp.arange(expert_count, dtype=jnp.int32)[None, :]).astype(jnp.int32)
    before = jnp.cumsum(onehot, axis=0).astype(jnp.int32) - onehot
    return lax.optimization_barrier(jnp.sum(before * onehot, axis=1)).astype(jnp.int32).reshape(route_rows.shape)

def forward(inputs, routes, gates, ln1_gain, ln1_bias, w_qkv, w_out, out_bias, ln2_gain, ln2_bias, w_in, in_bias, w_back, back_bias):
    device_count = N_GRP * N_EP
    flat_rows = inputs.reshape(IMAGES * SEQ, D)
    first = low(layer_norm(flat_rows, ln1_gain, ln1_bias))
    qkv = low_back(low(exact_dot(first, w_qkv))).reshape(IMAGES, SEQ, 3, HEADS, HD)
    query, key_rows, value_rows = (qkv[:, :, 0], qkv[:, :, 1], qkv[:, :, 2])
    scores = low_back(jnp.einsum('ishd,ithd->ihst', query, key_rows, precision=lax.Precision.HIGHEST) * HD ** (-0.5))
    attn_prob = low(jax.nn.softmax(scores, axis=-1))
    attended = low_back(low(jnp.einsum('ihst,ithd->ishd', attn_prob, value_rows, precision=lax.Precision.HIGHEST)))
    attended = attended.reshape(IMAGES * SEQ, D)
    branch = low_back(exact_dot(attended, w_out) + out_bias)
    resid = flat_rows + branch
    second = low(layer_norm(resid, ln2_gain, ln2_bias))
    dev_rows = second.reshape(device_count, TOK_DEV, D)
    dev_routes = routes.reshape(device_count, TOK_DEV, 2).astype(jnp.int32)
    slots = jax.vmap(lambda block: slot_of(block, EXPERTS))(dev_routes)
    dev_ids = jnp.broadcast_to(jnp.arange(device_count, dtype=jnp.int32)[:, None, None], slots.shape)
    buffer = jnp.zeros((device_count, EXPERTS, CAP, D), jnp.float32)
    spread = jnp.broadcast_to(dev_rows[:, :, None, :], (device_count, TOK_DEV, 2, D))
    buffer = low_back(buffer.at[dev_ids, dev_routes, slots].set(spread))
    pre_act = low_back(jnp.einsum('necd,edf->necf', buffer, w_in, precision=lax.Precision.HIGHEST) + in_bias[None, :, None, :])
    active = low(jax.nn.gelu(pre_act, approximate=True))
    expert_out = low_back(low(jnp.einsum('necf,efd->necd', active, w_back, precision=lax.Precision.HIGHEST) + back_bias[None, :, None, :]))
    picked = expert_out[dev_ids, dev_routes, slots]
    gate_rows = gates.reshape(device_count, TOK_DEV, 2)
    mixed = lax.optimization_barrier(jnp.sum(picked * gate_rows[:, :, :, None], axis=2)).reshape(IMAGES * SEQ, D)
    return (resid + mixed).reshape(IMAGES, SEQ, D)

def reference(tokens, routes, gates, ln1_gain, ln1_bias, w_qkv, w_out, out_bias, ln2_gain, ln2_bias, w_in, in_bias, w_back, back_bias, cotangent):
    params = (ln1_gain, ln1_bias, w_qkv, w_out, out_bias, ln2_gain, ln2_bias, w_in, in_bias, w_back, back_bias)
    params = tuple((item.astype(jnp.float32) for item in params))
    gate_values = gates.astype(jnp.float32)

    def forward_fn(inputs, *weights):
        return forward(inputs, routes, gate_values, *weights)
    result, pullback = jax.vjp(forward_fn, tokens.astype(jnp.float32), *params)
    grads = pullback(cotangent.astype(jnp.float32))
    return (result.astype(jnp.bfloat16), grads[0].astype(jnp.bfloat16), grads[1], grads[2], grads[3], grads[4], grads[5], grads[6], grads[7], grads[8], grads[9], grads[10], grads[11])
```

```python
import functools

import jax
import jax.numpy as jnp
from jax import lax
from jax.experimental import pallas as pl
from jax.experimental.pallas import tpu as pltpu
from jax.sharding import PartitionSpec as P

HD = 64
NORM_EPS = 1e-06
BF16 = jnp.bfloat16
F32 = jnp.float32
VMEM_LIMIT = 60 * 1024 * 1024
GELU_C = 0.7978845608028654


def dot_nn(a, b):
    return jnp.dot(a, b, preferred_element_type=F32)


def dot_nt(a, b):
    return lax.dot_general(a, b, (((1,), (1,)), ((), ())), preferred_element_type=F32)


def dot_tn(a, b):
    return lax.dot_general(a, b, (((0,), (0,)), ((), ())), preferred_element_type=F32)


def norm_parts(values):
    average = jnp.mean(values, axis=-1, keepdims=True)
    centred = values - average
    inv_std = lax.rsqrt(jnp.mean(centred * centred, axis=-1, keepdims=True) + NORM_EPS)
    return centred * inv_std, inv_std


def norm_back(grad_norm, normed, inv_std, gain):
    scaled = grad_norm * gain
    return inv_std * (
        scaled
        - jnp.mean(scaled, axis=-1, keepdims=True)
        - normed * jnp.mean(scaled * normed, axis=-1, keepdims=True)
    )


def whole(shape):
    zeros = (0,) * len(shape)
    return pl.BlockSpec(tuple(shape), lambda *_: zeros)


def params(*semantics):
    return pltpu.CompilerParams(
        dimension_semantics=semantics or None, vmem_limit_bytes=VMEM_LIMIT
    )


def route_kernel(exp_dev, me_ref, routes_ref, gates_ref, cot_ref, slot_row_ref, slot_col_ref, gate_col_ref, *rest):
    out_refs, scratch = rest[:-1], rest[-1]
    n_img, seq, _ = routes_ref.shape
    experts = slot_row_ref.shape[1]
    capp = out_refs[0].shape[1]
    me = me_ref[0]
    lane = lax.broadcasted_iota(jnp.int32, (seq, 128), 1)
    later = lax.broadcasted_iota(jnp.int32, (seq, seq), 0)
    earlier = lax.broadcasted_iota(jnp.int32, (seq, seq), 1)
    tri = jnp.where(earlier < later, 1.0, 0.0).astype(BF16)
    carry = jnp.zeros((1, 128), F32)
    gate_rows = []
    for i in range(n_img):
        routes = routes_ref[i]
        rel = ((routes // exp_dev) ^ me) * exp_dev + routes % exp_dev
        gates = gates_ref[i]
        hit0 = lane == rel[:, 0:1]
        hit1 = lane == rel[:, 1:2]
        member = jnp.where(hit0 | hit1, 1.0, 0.0)
        slot = jnp.where(member > 0.5, dot_nn(tri, member.astype(BF16)) + carry, -1.0)
        gate = jnp.where(hit0, gates[:, 0:1], 0.0) + jnp.where(hit1, gates[:, 1:2], 0.0)
        carry = carry + jnp.sum(member, axis=0, keepdims=True)
        slot_col_ref[i] = slot[:, :experts]
        gate_col_ref[i] = gate[:, :experts]
        scratch[0, 0:seq, :] = slot
        scratch[1, 0:seq, :] = gate
        slot_row_ref[i] = jnp.transpose(scratch[0])[:experts, :seq]
        gate_rows.append(jnp.transpose(scratch[1])[:experts, :seq])
    place = lax.broadcasted_iota(jnp.int32, (capp, seq), 0).astype(F32)
    for e in range(experts):
        total = jnp.zeros((capp, cot_ref.shape[2]), F32)
        for i in range(n_img):
            pick = jnp.where(place == slot_row_ref[i, e : e + 1, :], gate_rows[i][e : e + 1, :], 0.0)
            total = total + dot_nn(pick.astype(BF16), cot_ref[i])
        out_refs[e // exp_dev][e % exp_dev] = total.astype(BF16)


def route_call(me, routes, gates, cotangent, ep_size, exp_dev, capp):
    n_img, seq, width = cotangent.shape
    experts = ep_size * exp_dev
    seq_pad = -(-seq // 128) * 128
    chunk = jax.ShapeDtypeStruct((exp_dev, capp, width), BF16)
    return pl.pallas_call(
        functools.partial(route_kernel, exp_dev),
        in_specs=[pl.BlockSpec(memory_space=pltpu.SMEM)] + [pl.BlockSpec(memory_space=pltpu.VMEM)] * 3,
        out_specs=[pl.BlockSpec(memory_space=pltpu.VMEM)] * (3 + ep_size),
        out_shape=[
            jax.ShapeDtypeStruct((n_img, experts, seq), F32),
            jax.ShapeDtypeStruct((n_img, seq, experts), F32),
            jax.ShapeDtypeStruct((n_img, seq, experts), F32),
        ]
        + [chunk] * ep_size,
        scratch_shapes=[pltpu.VMEM((2, seq_pad, 128), F32)],
        compiler_params=params(),
        cost_estimate=pl.CostEstimate(
            flops=2 * experts * capp * n_img * seq * width, bytes_accessed=4 * n_img * seq * width * 2, transcendentals=0
        ),
        name="route_and_dispatch_cotangent",
    )(me, routes, gates, cotangent)


def attention_kernel(
    heads, tok_ref, w_qkv_ref, w_out_ref, vec_ref, slot_row_ref, qkv_ref, att_ref, lse_ref, resid_ref, *rest
):
    out_refs, second_ref = rest[:-1], rest[-1]
    img = pl.program_id(0)
    seq, width = tok_ref.shape[1:]
    exp_dev, capp = out_refs[0].shape[:2]
    inputs = tok_ref[0].astype(F32)
    norm_first, _ = norm_parts(inputs)
    first = (norm_first * vec_ref[0:1, :] + vec_ref[1:2, :]).astype(BF16)
    qkv = dot_nn(first, w_qkv_ref[...]).astype(BF16)
    qkv_ref[0] = qkv
    low = lax.broadcasted_iota(jnp.int32, (seq, 2 * HD), 1) < HD
    nothing = jnp.zeros((seq, 2 * HD), BF16)
    lane = lax.broadcasted_iota(jnp.int32, (seq, 128), 1)
    lse_all = jnp.zeros((seq, 128), F32)
    pieces = []
    for pair in range(heads // 2):
        at = pair * 2 * HD
        query = qkv[:, at : at + 2 * HD] * jnp.asarray(HD ** (-0.5), BF16)
        key = qkv[:, width + at : width + at + 2 * HD]
        value = qkv[:, 2 * width + at : 2 * width + at + 2 * HD]
        halves = []
        for half in range(2):
            mine = low if half == 0 else jnp.logical_not(low)
            scores = dot_nt(jnp.where(mine, query, nothing), key)
            top = jnp.max(scores, axis=-1, keepdims=True)
            weight = jnp.exp(scores - top)
            total = jnp.sum(weight, axis=-1, keepdims=True)
            prob = (weight * (1.0 / total)).astype(BF16)
            halves.append(dot_nn(prob, value))
            lse_all = jnp.where(lane == 2 * pair + half, top + jnp.log(total), lse_all)
        pieces.append(jnp.where(low, halves[0], halves[1]).astype(BF16))
    lse_ref[0] = lse_all
    attended = jnp.concatenate(pieces, axis=1)
    att_ref[0] = attended
    resid = inputs + dot_nn(attended, w_out_ref[...]) + vec_ref[2:3, :]
    resid_ref[0] = resid
    norm_second, _ = norm_parts(resid)
    second_ref[img] = (norm_second * vec_ref[3:4, :] + vec_ref[4:5, :]).astype(BF16)

    @pl.when(img == pl.num_programs(0) - 1)
    def _():
        n_img = second_ref.shape[0]
        place = lax.broadcasted_iota(jnp.int32, (capp, seq), 0).astype(F32)
        for e in range(len(out_refs) * exp_dev):
            total = jnp.zeros((capp, width), F32)
            for i in range(n_img):
                pick = jnp.where(place == slot_row_ref[i, e : e + 1, :], 1.0, 0.0)
                total = total + dot_nn(pick.astype(BF16), second_ref[i])
            out_refs[e // exp_dev][e % exp_dev] = total.astype(BF16)


def attention_call(tokens, w_qkv, w_out, vecs, slot_row, ep_size, exp_dev, capp):
    n_img, seq, width = tokens.shape
    chunk = jax.ShapeDtypeStruct((exp_dev, capp, width), BF16)
    image = lambda *tail: pl.BlockSpec((1,) + tail, lambda i: (i, 0, 0))
    return pl.pallas_call(
        functools.partial(attention_kernel, width // HD),
        grid=(n_img,),
        in_specs=[image(seq, width), whole(w_qkv.shape), whole(w_out.shape), whole(vecs.shape), whole(slot_row.shape)],
        out_specs=[image(seq, 3 * width), image(seq, width), image(seq, 128), image(seq, width)]
        + [whole(chunk.shape)] * ep_size,
        out_shape=[
            jax.ShapeDtypeStruct((n_img, seq, 3 * width), BF16),
            jax.ShapeDtypeStruct((n_img, seq, width), BF16),
            jax.ShapeDtypeStruct((n_img, seq, 128), F32),
            jax.ShapeDtypeStruct((n_img, seq, width), F32),
        ]
        + [chunk] * ep_size,
        scratch_shapes=[pltpu.VMEM((n_img, seq, width), BF16)],
        compiler_params=params("arbitrary"),
        cost_estimate=pl.CostEstimate(flops=6 * 10**9, bytes_accessed=10 * 2**20, transcendentals=10**6),
        name="attention_forward_and_dispatch",
    )(tokens, w_qkv, w_out, vecs, slot_row)


def expert_kernel(count, *refs):
    x_refs, g_refs = refs[:count], refs[count : 2 * count]
    w_in_ref, w_back_ref, b_in_ref, b_back_ref = refs[2 * count : 2 * count + 4]
    outs = refs[2 * count + 4 :]
    act_refs, gpre_refs, out_refs, gdis_refs = (outs[k * count : (k + 1) * count] for k in range(4))
    acc_out, acc_dis = outs[4 * count :]
    step = pl.program_id(1)
    w_in = w_in_ref[0]
    w_back = w_back_ref[0]
    for n in range(count):
        pre = dot_nn(x_refs[n][0], w_in) + b_in_ref[0]
        square = pre * pre
        bent = jnp.tanh(pre * (GELU_C + (GELU_C * 0.044715) * square))
        half = 0.5 + 0.5 * bent
        act = (pre * half).astype(BF16)
        slope = half + (pre * (0.5 - 0.5 * bent * bent)) * (GELU_C + (3 * GELU_C * 0.044715) * square)
        gpre = (dot_nt(g_refs[n][0], w_back) * slope).astype(BF16)
        act_refs[n][0] = act
        gpre_refs[n][0] = gpre
        part_dis = dot_nt(gpre, w_in)
        part_out = dot_nn(act, w_back)

        @pl.when(step == 0)
        def _():
            acc_dis[n] = part_dis
            acc_out[n] = part_out + b_back_ref[0]

        @pl.when(step > 0)
        def _():
            acc_dis[n] += part_dis
            acc_out[n] += part_out

        @pl.when(step == pl.num_programs(1) - 1)
        def _():
            gdis_refs[n][0] = acc_dis[n].astype(BF16)
            out_refs[n][0] = acc_out[n].astype(BF16)


def expert_call(xs, gs, w_in, w_back, b_in, b_back, tile):
    count = len(xs)
    exp_dev, capp, width = xs[0].shape
    hidden = w_in.shape[2]
    rows = pl.BlockSpec((1, capp, width), lambda e, f: (e, 0, 0))
    wide = pl.BlockSpec((1, capp, tile), lambda e, f: (e, 0, f))
    narrow = jax.ShapeDtypeStruct((exp_dev, capp, width), BF16)
    broad = jax.ShapeDtypeStruct((exp_dev, capp, hidden), BF16)
    res = pl.pallas_call(
        functools.partial(expert_kernel, count),
        grid=(exp_dev, hidden // tile),
        in_specs=[rows] * (2 * count)
        + [
            pl.BlockSpec((1, width, tile), lambda e, f: (e, 0, f)),
            pl.BlockSpec((1, tile, width), lambda e, f: (e, f, 0)),
            pl.BlockSpec((1, 1, tile), lambda e, f: (e, 0, f)),
            pl.BlockSpec((1, 1, width), lambda e, f: (e, 0, 0)),
        ],
        out_specs=[wide] * (2 * count) + [rows] * (2 * count),
        out_shape=[broad] * (2 * count) + [narrow] * (2 * count),
        scratch_shapes=[pltpu.VMEM((count, capp, width), F32)] * 2,
        compiler_params=params("arbitrary", "arbitrary"),
        cost_estimate=pl.CostEstimate(
            flops=8 * count * exp_dev * capp * width * hidden,
            bytes_accessed=4 * exp_dev * width * hidden + 4 * count * exp_dev * capp * hidden,
            transcendentals=count * exp_dev * capp * hidden,
        ),
        name="experts",
    )(*xs, *gs, w_in, w_back, b_in, b_back)
    return [res[k * count : (k + 1) * count] for k in range(4)]


def weight_kernel(count, left_first, sel_ref, *refs):
    a_refs, b_refs = refs[:count], refs[count : 2 * count]
    out_ref, bias_ref = refs[2 * count :]
    total = dot_tn(a_refs[0][0], b_refs[0][0])
    for n in range(1, count):
        total = total + dot_tn(a_refs[n][0], b_refs[n][0])
    out_ref[0] = total.astype(BF16)
    if left_first:
        @pl.when(pl.program_id(0) == 0)
        def _():
            bias = jnp.sum(b_refs[0][0].astype(F32), axis=0, keepdims=True)
            for n in range(1, count):
                bias = bias + jnp.sum(b_refs[n][0].astype(F32), axis=0, keepdims=True)
            bias_ref[0] = bias
    else:
        bias = jnp.sum(b_refs[0][0].astype(F32), axis=0, keepdims=True)
        for n in range(1, count):
            bias = bias + jnp.sum(b_refs[n][0].astype(F32), axis=0, keepdims=True)
        bias_ref[0] = bias


def weight_call(lefts, rights, which, rel, blocks, left_first):
    count = len(lefts)
    _, capp, m = lefts[0].shape
    n = rights[0].shape[2]
    if left_first:
        m = m // blocks
    else:
        n = n // blocks
    left_at = (lambda r, s: (s[0], 0, r ^ s[1])) if left_first else (lambda r, s: (s[0], 0, 0))
    right_at = (lambda r, s: (s[0], 0, 0)) if left_first else (lambda r, s: (s[0], 0, r ^ s[1]))
    bias_at = (lambda r, s: (0, 0, 0)) if left_first else (lambda r, s: (0, 0, r ^ s[1]))
    return pl.pallas_call(
        functools.partial(weight_kernel, count, left_first),
        grid_spec=pltpu.PrefetchScalarGridSpec(
            num_scalar_prefetch=1,
            grid=(blocks,),
            in_specs=[pl.BlockSpec((1, capp, m), left_at)] * count + [pl.BlockSpec((1, capp, n), right_at)] * count,
            out_specs=[pl.BlockSpec((1, m, n), lambda r, s: (r, 0, 0)), pl.BlockSpec((1, 1, n), bias_at)],
        ),
        out_shape=[
            jax.ShapeDtypeStruct((blocks, m, n), BF16),
            jax.ShapeDtypeStruct((1, 1, rights[0].shape[2]), F32),
        ],
        compiler_params=params("arbitrary"),
        cost_estimate=pl.CostEstimate(
            flops=2 * count * capp * blocks * m * n, bytes_accessed=2 * blocks * m * n, transcendentals=0
        ),
        name="expert_weight_gradient",
    )(which, *lefts, *rights)


def gather_rows(slot_col, value_col, chunk_refs, capp):
    seq = slot_col.shape[0]
    exp_dev = chunk_refs[0].shape[0]
    place = lax.broadcasted_iota(jnp.int32, (seq, capp), 1).astype(F32)
    total = None
    for e in range(len(chunk_refs) * exp_dev):
        value = 1.0 if value_col is None else value_col[:, e : e + 1]
        pick = jnp.where(place == slot_col[:, e : e + 1], value, 0.0).astype(BF16)
        part = dot_nn(pick, chunk_refs[e // exp_dev][e % exp_dev])
        total = part if total is None else total + part
    return total


def backward_kernel(
    heads, ep_size, tok_ref, cot_ref, resid_ref, qkv_ref, att_ref, lse_ref, slot_col_ref, w_qkv_ref, w_out_ref, vec_ref, *rest
):
    chunk_refs = rest[:ep_size]
    gtok_ref, gw_qkv_ref, gw_out_ref, gvec_ref, gqkv_ref = rest[ep_size:]
    img = pl.program_id(0)
    seq, width = tok_ref.shape[1:]
    capp = chunk_refs[0].shape[1]
    grad_second = gather_rows(slot_col_ref[0], None, chunk_refs, capp)
    norm_second, inv_second = norm_parts(resid_ref[0])
    grad_resid = cot_ref[0].astype(F32) + norm_back(grad_second, norm_second, inv_second, vec_ref[3:4, :])
    grad_branch = grad_resid.astype(BF16)
    grad_att = dot_nt(grad_branch, w_out_ref[...]).astype(BF16)
    gw_out = dot_tn(att_ref[0], grad_branch)
    low = lax.broadcasted_iota(jnp.int32, (seq, 2 * HD), 1) < HD
    nothing = jnp.zeros((seq, 2 * HD), BF16)
    scale = jnp.asarray(HD ** (-0.5), BF16)
    for pair in range(heads // 2):
        at = pair * 2 * HD
        query = qkv_ref[0, :, at : at + 2 * HD] * scale
        key = qkv_ref[0, :, width + at : width + at + 2 * HD]
        value = qkv_ref[0, :, 2 * width + at : 2 * width + at + 2 * HD]
        gatt = grad_att[:, at : at + 2 * HD]
        grad_q = grad_k = grad_v = None
        for half in range(2):
            mine = low if half == 0 else jnp.logical_not(low)
            head = 2 * pair + half
            query_h = jnp.where(mine, query, nothing)
            gatt_h = jnp.where(mine, gatt, nothing)
            key_h = jnp.where(mine, key, nothing) * scale
            prob = jnp.exp(dot_nt(query_h, key) - lse_ref[0, :, head : head + 1])
            grad_prob = dot_nt(gatt_h, value)
            mean = jnp.sum(grad_prob * prob, axis=-1, keepdims=True)
            grad_scores = (prob * (grad_prob - mean)).astype(BF16)
            part_v = dot_tn(prob.astype(BF16), gatt_h)
            part_q = dot_nn(grad_scores, key_h)
            part_k = dot_tn(grad_scores, query_h)
            grad_q = part_q if grad_q is None else grad_q + part_q
            grad_k = part_k if grad_k is None else grad_k + part_k
            grad_v = part_v if grad_v is None else grad_v + part_v
        gqkv_ref[:, at : at + 2 * HD] = grad_q.astype(BF16)
        gqkv_ref[:, width + at : width + at + 2 * HD] = grad_k.astype(BF16)
        gqkv_ref[:, 2 * width + at : 2 * width + at + 2 * HD] = grad_v.astype(BF16)
    grad_qkv = gqkv_ref[...]
    norm_first, inv_first = norm_parts(tok_ref[0].astype(F32))
    first = (norm_first * vec_ref[0:1, :] + vec_ref[1:2, :]).astype(BF16)
    gw_qkv = dot_tn(first, grad_qkv)
    grad_first = dot_nt(grad_qkv, w_qkv_ref[...])
    gtok_ref[0] = (grad_resid + norm_back(grad_first, norm_first, inv_first, vec_ref[0:1, :])).astype(BF16)
    sums = [
        grad_first * norm_first,
        grad_first,
        grad_branch.astype(F32),
        grad_second * norm_second,
        grad_second,
    ]
    gvec = jnp.concatenate([jnp.sum(v, axis=0, keepdims=True) for v in sums] + [jnp.zeros((3, width), F32)], axis=0)

    @pl.when(img == 0)
    def _():
        gw_out_ref[...] = gw_out
        gw_qkv_ref[...] = gw_qkv
        gvec_ref[...] = gvec

    @pl.when(img > 0)
    def _():
        gw_out_ref[...] += gw_out
        gw_qkv_ref[...] += gw_qkv
        gvec_ref[...] += gvec


def backward_call(tokens, cotangent, resid, qkv, attended, lse, slot_col, w_qkv, w_out, vecs, chunks):
    n_img, seq, width = tokens.shape
    image = lambda arr: pl.BlockSpec((1,) + arr.shape[1:], lambda i: (i, 0, 0))
    return pl.pallas_call(
        functools.partial(backward_kernel, width // HD, len(chunks)),
        grid=(n_img,),
        in_specs=[image(a) for a in (tokens, cotangent, resid, qkv, attended, lse, slot_col)]
        + [whole(a.shape) for a in (w_qkv, w_out, vecs, *chunks)],
        out_specs=[image(tokens), whole(w_qkv.shape), whole(w_out.shape), whole((8, width))],
        out_shape=[
            jax.ShapeDtypeStruct(tokens.shape, BF16),
            jax.ShapeDtypeStruct(w_qkv.shape, F32),
            jax.ShapeDtypeStruct(w_out.shape, F32),
            jax.ShapeDtypeStruct((8, width), F32),
        ],
        scratch_shapes=[pltpu.VMEM((seq, 3 * width), BF16)],
        compiler_params=params("arbitrary"),
        cost_estimate=pl.CostEstimate(flops=10 * 10**9, bytes_accessed=16 * 2**20, transcendentals=10**6),
        name="attention_backward",
    )(tokens, cotangent, resid, qkv, attended, lse, slot_col, w_qkv, w_out, vecs, *chunks)


def combine_kernel(ep_size, resid_ref, slot_col_ref, gate_col_ref, *rest):
    chunk_refs, out_ref = rest[:ep_size], rest[ep_size]
    mixed = gather_rows(slot_col_ref[0], gate_col_ref[0], chunk_refs, chunk_refs[0].shape[1])
    out_ref[0] = (resid_ref[0] + mixed).astype(BF16)


def combine_call(resid, slot_col, gate_col, chunks):
    n_img, seq, width = resid.shape
    image = lambda arr: pl.BlockSpec((1,) + arr.shape[1:], lambda i: (i, 0, 0))
    return pl.pallas_call(
        functools.partial(combine_kernel, len(chunks)),
        grid=(n_img,),
        in_specs=[image(a) for a in (resid, slot_col, gate_col)] + [whole(c.shape) for c in chunks],
        out_specs=image(resid),
        out_shape=jax.ShapeDtypeStruct(resid.shape, BF16),
        compiler_params=params("arbitrary"),
        cost_estimate=pl.CostEstimate(flops=2 * 10**9, bytes_accessed=5 * 2**20, transcendentals=0),
        name="combine_output",
    )(resid, slot_col, gate_col, *chunks)


def swap(array, axis, size, distance):
    return lax.ppermute(array, axis, [(i, i ^ distance) for i in range(size)])


def local(
    tokens,
    routes,
    gates,
    ln1_gain,
    ln1_bias,
    w_qkv,
    w_out,
    out_bias,
    ln2_gain,
    ln2_bias,
    w_in,
    in_bias,
    w_back,
    back_bias,
    cotangent,
):
    images, seq_len, width = tokens.shape
    ep_size = lax.axis_size("ep")
    exp_dev = w_in.shape[0]
    experts = exp_dev * ep_size
    capacity = (images * seq_len * 10 + 4 * experts - 1) // (4 * experts)
    capp = -(-capacity // 8) * 8
    me = lax.axis_index("ep").astype(jnp.int32).reshape(1)
    vecs = jnp.stack([ln1_gain, ln1_bias, out_bias, ln2_gain, ln2_bias] + [jnp.zeros_like(ln1_gain)] * 3)

    def exchange(chunks):
        return [chunks[0]] + [swap(chunks[d], "ep", ep_size, d) for d in range(1, ep_size)]

    slot_row, slot_col, gate_col, *g_send = route_call(me, routes, gates, cotangent, ep_size, exp_dev, capp)
    g_all = exchange(g_send)
    qkv, attended, lse, resid, *x_send = attention_call(tokens, w_qkv, w_out, vecs, slot_row, ep_size, exp_dev, capp)
    x_all = exchange(x_send)
    b_in, b_back = in_bias[:, None, :], back_bias[:, None, :]
    acts, gpres, outs, gdis = [], [], [], []
    for d in range(ep_size):
        a, p, o, g = expert_call(x_all[d : d + 1], g_all[d : d + 1], w_in, w_back, b_in, b_back, 512)
        acts += a
        gpres += p
        outs += o
        gdis += g
    gdis_back = exchange(gdis)
    outs_back = exchange(outs)
    gw_back, gb_back, gw_in, gb_in = [], [], [], []
    for e in range(exp_dev):
        which = jnp.array([e, 0], jnp.int32)
        w, b = weight_call(acts, g_all, which, None, 4, True)
        gw_back.append(w.reshape(w_back.shape[1:]))
        gb_back.append(b[0, 0])
        w, b = weight_call(x_all, gpres, which, None, 4, False)
        gw_in.append(w.transpose(1, 0, 2).reshape(w_in.shape[1:]))
        gb_in.append(b[0, 0])
    gw_back, gb_back, gw_in, gb_in = (jnp.stack(v) for v in (gw_back, gb_back, gw_in, gb_in))
    grad_tokens, gw_qkv, gw_out, gvec = backward_call(
        tokens, cotangent, resid, qkv, attended, lse, slot_col, w_qkv, w_out, vecs, gdis_back
    )
    output = combine_call(resid, slot_col, gate_col, outs_back)

    def over_grp(v):
        return lax.psum(v.astype(BF16), "grp").astype(F32)

    def over_all(v):
        return over_grp(lax.psum_scatter(v.astype(BF16), "ep", scatter_dimension=0, tiled=True))

    return (
        output,
        grad_tokens,
        over_all(gvec[0]),
        over_all(gvec[1]),
        over_all(gw_qkv),
        over_all(gw_out),
        over_all(gvec[2]),
        over_all(gvec[3]),
        over_all(gvec[4]),
        over_grp(gw_in),
        over_grp(gb_in),
        over_grp(gw_back),
        over_grp(gb_back),
    )


def solution(mesh):
    rows = P(("grp", "ep"), None, None)
    return jax.shard_map(
        local,
        mesh=mesh,
        in_specs=(rows, rows, rows)
        + (P(),) * 7
        + (P("ep", None, None), P("ep", None), P("ep", None, None), P("ep", None), rows),
        out_specs=(rows, rows)
        + (P("ep"), P("ep"), P("ep", None), P("ep", None), P("ep"), P("ep"), P("ep"))
        + (P("ep", None, None), P("ep", None), P("ep", None, None), P("ep", None)),
        check_vma=False,
    )
```

```python
import functools

import jax
import jax.numpy as jnp
from jax import lax
from jax.experimental import pallas as pl
from jax.experimental.pallas import tpu as pltpu
from jax.sharding import PartitionSpec as P

HD = 64
NORM_EPS = 1e-06
BF16 = jnp.bfloat16
F32 = jnp.float32
VMEM_LIMIT = 60 * 1024 * 1024
GELU_C = 0.7978845608028654
COST = pl.CostEstimate(flops=10**6, bytes_accessed=2**12, transcendentals=0)


def dot_nn(a, b):
    return jnp.dot(a, b, preferred_element_type=F32)


def dot_nt(a, b):
    return lax.dot_general(a, b, (((1,), (1,)), ((), ())), preferred_element_type=F32)


def dot_tn(a, b):
    return lax.dot_general(a, b, (((0,), (0,)), ((), ())), preferred_element_type=F32)


def norm_parts(values):
    average = jnp.mean(values, axis=-1, keepdims=True)
    centred = values - average
    inv_std = lax.rsqrt(jnp.mean(centred * centred, axis=-1, keepdims=True) + NORM_EPS)
    return centred * inv_std, inv_std


def norm_back(grad_norm, normed, inv_std, gain):
    scaled = grad_norm * gain
    return inv_std * (
        scaled
        - jnp.mean(scaled, axis=-1, keepdims=True)
        - normed * jnp.mean(scaled * normed, axis=-1, keepdims=True)
    )


def whole(shape):
    zeros = (0,) * len(shape)
    return pl.BlockSpec(tuple(shape), lambda *_: zeros)


def params(*semantics):
    return pltpu.CompilerParams(
        dimension_semantics=semantics or None, vmem_limit_bytes=VMEM_LIMIT
    )


def route_kernel(exp_dev, me_ref, routes_ref, gates_ref, cot_ref, slot_row_ref, slot_col_ref, gate_col_ref, *rest):
    out_refs, scratch = rest[:-1], rest[-1]
    n_img, seq, width = cot_ref.shape
    experts = slot_row_ref.shape[1]
    capp = out_refs[0].shape[1]
    me = me_ref[0]
    expert = lax.broadcasted_iota(jnp.int32, (experts, seq), 0)
    expert = ((expert // exp_dev) ^ me) * exp_dev + expert % exp_dev
    earlier = lax.broadcasted_iota(jnp.int32, (seq, seq), 0)
    later = lax.broadcasted_iota(jnp.int32, (seq, seq), 1)
    tri = jnp.where(earlier < later, 1.0, 0.0).astype(BF16)
    carry = jnp.zeros((experts, 1), F32)
    slots, gate_rows = [], []
    for i in range(n_img):
        hit0 = expert == routes_ref[0, i : i + 1, :]
        hit1 = expert == routes_ref[1, i : i + 1, :]
        member = jnp.where(hit0 | hit1, 1.0, 0.0)
        slot = jnp.where(member > 0.5, dot_nn(member.astype(BF16), tri) + carry, -1.0)
        gate = jnp.where(hit0, gates_ref[0, i : i + 1, :], jnp.where(hit1, gates_ref[1, i : i + 1, :], 0.0))
        carry = carry + jnp.sum(member, axis=1, keepdims=True)
        slots.append(slot)
        gate_rows.append(gate)
        slot_row_ref[i] = slot
        scratch[0, 0:experts, 0:seq] = slot
        scratch[1, 0:experts, 0:seq] = gate
        slot_col_ref[i] = jnp.transpose(scratch[0])[:seq, :experts]
        gate_col_ref[i] = jnp.transpose(scratch[1])[:seq, :experts]
    place = lax.broadcasted_iota(jnp.int32, (capp, seq), 0).astype(F32)
    for e in range(experts):
        total = jnp.zeros((capp, width), F32)
        for i in range(n_img):
            pick = jnp.where(place == slots[i][e : e + 1, :], gate_rows[i][e : e + 1, :], 0.0)
            total = total + dot_nn(pick.astype(BF16), cot_ref[i])
        out_refs[e // exp_dev][e % exp_dev] = total.astype(BF16)


def route_call(me, routes, gates, cotangent, ep_size, exp_dev, capp):
    n_img, seq, width = cotangent.shape
    experts = ep_size * exp_dev
    seq_pad = -(-seq // 128) * 128
    chunk = jax.ShapeDtypeStruct((exp_dev, capp, width), BF16)
    return pl.pallas_call(
        functools.partial(route_kernel, exp_dev),
        in_specs=[pl.BlockSpec(memory_space=pltpu.SMEM)] + [pl.BlockSpec(memory_space=pltpu.VMEM)] * 3,
        out_specs=[pl.BlockSpec(memory_space=pltpu.VMEM)] * (3 + ep_size),
        out_shape=[
            jax.ShapeDtypeStruct((n_img, experts, seq), F32),
            jax.ShapeDtypeStruct((n_img, seq, experts), F32),
            jax.ShapeDtypeStruct((n_img, seq, experts), F32),
        ]
        + [chunk] * ep_size,
        scratch_shapes=[pltpu.VMEM((2, 128, seq_pad), F32)],
        compiler_params=params(),
        cost_estimate=COST,
        name="route_and_dispatch_cotangent",
    )(me, routes.transpose(2, 0, 1), gates.transpose(2, 0, 1), cotangent)


def attention_kernel(
    heads, tok_ref, w_qkv_ref, w_out_ref, vec_ref, slot_row_ref, qkv_ref, att_ref, lse_ref, resid_ref, *rest
):
    out_refs, second_ref = rest[:-1], rest[-1]
    img = pl.program_id(0)
    seq, width = tok_ref.shape[1:]
    exp_dev, capp = out_refs[0].shape[:2]
    inputs = tok_ref[0].astype(F32)
    norm_first, _ = norm_parts(inputs)
    first = (norm_first * vec_ref[0:1, :] + vec_ref[1:2, :]).astype(BF16)
    qkv = dot_nn(first, w_qkv_ref[...]).astype(BF16)
    qkv_ref[0] = qkv
    low = lax.broadcasted_iota(jnp.int32, (seq, 2 * HD), 1) < HD
    nothing = jnp.zeros((seq, 2 * HD), BF16)
    lane = lax.broadcasted_iota(jnp.int32, (seq, 128), 1)
    lse_all = jnp.zeros((seq, 128), F32)
    pieces = []
    for pair in range(heads // 2):
        at = pair * 2 * HD
        query = qkv[:, at : at + 2 * HD] * jnp.asarray(HD ** (-0.5), BF16)
        key = qkv[:, width + at : width + at + 2 * HD]
        value = qkv[:, 2 * width + at : 2 * width + at + 2 * HD]
        halves = []
        for half in range(2):
            mine = low if half == 0 else jnp.logical_not(low)
            scores = dot_nt(jnp.where(mine, query, nothing), key)
            top = jnp.max(scores, axis=-1, keepdims=True)
            weight = jnp.exp(scores - top)
            total = jnp.sum(weight, axis=-1, keepdims=True)
            prob = (weight * (1.0 / total)).astype(BF16)
            halves.append(dot_nn(prob, value))
            lse_all = jnp.where(lane == 2 * pair + half, top + jnp.log(total), lse_all)
        pieces.append(jnp.where(low, halves[0], halves[1]).astype(BF16))
    lse_ref[0] = lse_all
    attended = jnp.concatenate(pieces, axis=1)
    att_ref[0] = attended
    resid = inputs + dot_nn(attended, w_out_ref[...]) + vec_ref[2:3, :]
    resid_ref[0] = resid
    norm_second, _ = norm_parts(resid)
    second_ref[img] = (norm_second * vec_ref[3:4, :] + vec_ref[4:5, :]).astype(BF16)

    @pl.when(img == pl.num_programs(0) - 1)
    def _():
        n_img = second_ref.shape[0]
        place = lax.broadcasted_iota(jnp.int32, (capp, seq), 0).astype(F32)
        for e in range(len(out_refs) * exp_dev):
            total = jnp.zeros((capp, width), F32)
            for i in range(n_img):
                pick = jnp.where(place == slot_row_ref[i, e : e + 1, :], 1.0, 0.0)
                total = total + dot_nn(pick.astype(BF16), second_ref[i])
            out_refs[e // exp_dev][e % exp_dev] = total.astype(BF16)


def attention_call(tokens, w_qkv, w_out, vecs, slot_row, ep_size, exp_dev, capp):
    n_img, seq, width = tokens.shape
    chunk = jax.ShapeDtypeStruct((exp_dev, capp, width), BF16)
    image = lambda *tail: pl.BlockSpec((1,) + tail, lambda i: (i, 0, 0))
    return pl.pallas_call(
        functools.partial(attention_kernel, width // HD),
        grid=(n_img,),
        in_specs=[image(seq, width), whole(w_qkv.shape), whole(w_out.shape), whole(vecs.shape), whole(slot_row.shape)],
        out_specs=[image(seq, 3 * width), image(seq, width), image(seq, 128), image(seq, width)]
        + [whole(chunk.shape)] * ep_size,
        out_shape=[
            jax.ShapeDtypeStruct((n_img, seq, 3 * width), BF16),
            jax.ShapeDtypeStruct((n_img, seq, width), BF16),
            jax.ShapeDtypeStruct((n_img, seq, 128), F32),
            jax.ShapeDtypeStruct((n_img, seq, width), F32),
        ]
        + [chunk] * ep_size,
        scratch_shapes=[pltpu.VMEM((n_img, seq, width), BF16)],
        compiler_params=params("arbitrary"),
        cost_estimate=COST,
        name="attention_forward_and_dispatch",
    )(tokens, w_qkv, w_out, vecs, slot_row)


def expert_kernel(count, *refs):
    x_refs, g_refs = refs[:count], refs[count : 2 * count]
    w_in_ref, w_back_ref, b_in_ref, b_back_ref = refs[2 * count : 2 * count + 4]
    outs = refs[2 * count + 4 :]
    act_refs, gpre_refs, out_refs, gdis_refs = (outs[k * count : (k + 1) * count] for k in range(4))
    acc_out, acc_dis = outs[4 * count :]
    step = pl.program_id(1)
    w_in = w_in_ref[0]
    w_back = w_back_ref[0]
    for n in range(count):
        pre = dot_nn(x_refs[n][0], w_in) + b_in_ref[0]
        square = pre * pre
        bent = jnp.tanh(pre * (GELU_C + (GELU_C * 0.044715) * square))
        half = 0.5 + 0.5 * bent
        act = (pre * half).astype(BF16)
        slope = half + (pre * (0.5 - 0.5 * bent * bent)) * (GELU_C + (3 * GELU_C * 0.044715) * square)
        gpre = (dot_nt(g_refs[n][0], w_back) * slope).astype(BF16)
        act_refs[n][0] = act
        gpre_refs[n][0] = gpre
        part_dis = dot_nt(gpre, w_in)
        part_out = dot_nn(act, w_back)

        @pl.when(step == 0)
        def _():
            acc_dis[n] = part_dis
            acc_out[n] = part_out + b_back_ref[0]

        @pl.when(step > 0)
        def _():
            acc_dis[n] += part_dis
            acc_out[n] += part_out

        @pl.when(step == pl.num_programs(1) - 1)
        def _():
            gdis_refs[n][0] = acc_dis[n].astype(BF16)
            out_refs[n][0] = acc_out[n].astype(BF16)


def expert_call(xs, gs, w_in, w_back, b_in, b_back, tile):
    count = len(xs)
    exp_dev, capp, width = xs[0].shape
    hidden = w_in.shape[2]
    rows = pl.BlockSpec((1, capp, width), lambda e, f: (e, 0, 0))
    wide = pl.BlockSpec((1, capp, tile), lambda e, f: (e, 0, f))
    narrow = jax.ShapeDtypeStruct((exp_dev, capp, width), BF16)
    broad = jax.ShapeDtypeStruct((exp_dev, capp, hidden), BF16)
    res = pl.pallas_call(
        functools.partial(expert_kernel, count),
        grid=(exp_dev, hidden // tile),
        in_specs=[rows] * (2 * count)
        + [
            pl.BlockSpec((1, width, tile), lambda e, f: (e, 0, f)),
            pl.BlockSpec((1, tile, width), lambda e, f: (e, f, 0)),
            pl.BlockSpec((1, 1, tile), lambda e, f: (e, 0, f)),
            pl.BlockSpec((1, 1, width), lambda e, f: (e, 0, 0)),
        ],
        out_specs=[wide] * (2 * count) + [rows] * (2 * count),
        out_shape=[broad] * (2 * count) + [narrow] * (2 * count),
        scratch_shapes=[pltpu.VMEM((count, capp, width), F32)] * 2,
        compiler_params=params("arbitrary", "arbitrary"),
        cost_estimate=COST,
        name="experts",
    )(*xs, *gs, w_in, w_back, b_in, b_back)
    return [res[k * count : (k + 1) * count] for k in range(4)]


def weight_kernel(count, left_first, sel_ref, *refs):
    a_refs, b_refs = refs[:count], refs[count : 2 * count]
    out_ref, bias_ref = refs[2 * count :]
    total = dot_tn(a_refs[0][0], b_refs[0][0])
    for n in range(1, count):
        total = total + dot_tn(a_refs[n][0], b_refs[n][0])
    out_ref[0] = total.astype(BF16)
    if left_first:
        @pl.when(pl.program_id(0) == 0)
        def _():
            bias = jnp.sum(b_refs[0][0].astype(F32), axis=0, keepdims=True)
            for n in range(1, count):
                bias = bias + jnp.sum(b_refs[n][0].astype(F32), axis=0, keepdims=True)
            bias_ref[0] = bias
    else:
        bias = jnp.sum(b_refs[0][0].astype(F32), axis=0, keepdims=True)
        for n in range(1, count):
            bias = bias + jnp.sum(b_refs[n][0].astype(F32), axis=0, keepdims=True)
        bias_ref[0] = bias


def weight_call(lefts, rights, which, blocks, left_first):
    count = len(lefts)
    _, capp, m = lefts[0].shape
    n = rights[0].shape[2]
    if left_first:
        m = m // blocks
    else:
        n = n // blocks
    left_at = (lambda r, s: (s[0], 0, r ^ s[1])) if left_first else (lambda r, s: (s[0], 0, 0))
    right_at = (lambda r, s: (s[0], 0, 0)) if left_first else (lambda r, s: (s[0], 0, r ^ s[1]))
    bias_at = (lambda r, s: (0, 0, 0)) if left_first else (lambda r, s: (0, 0, r ^ s[1]))
    return pl.pallas_call(
        functools.partial(weight_kernel, count, left_first),
        grid_spec=pltpu.PrefetchScalarGridSpec(
            num_scalar_prefetch=1,
            grid=(blocks,),
            in_specs=[pl.BlockSpec((1, capp, m), left_at)] * count + [pl.BlockSpec((1, capp, n), right_at)] * count,
            out_specs=[pl.BlockSpec((1, m, n), lambda r, s: (r, 0, 0)), pl.BlockSpec((1, 1, n), bias_at)],
        ),
        out_shape=[
            jax.ShapeDtypeStruct((blocks, m, n), BF16),
            jax.ShapeDtypeStruct((1, 1, rights[0].shape[2]), F32),
        ],
        compiler_params=params("arbitrary"),
        cost_estimate=COST,
        name="expert_weight_gradient",
    )(which, *lefts, *rights)


def gather_rows(slot_col, value_col, chunk_refs, capp):
    seq = slot_col.shape[0]
    exp_dev = chunk_refs[0].shape[0]
    place = lax.broadcasted_iota(jnp.int32, (seq, capp), 1).astype(F32)
    total = None
    for e in range(len(chunk_refs) * exp_dev):
        value = 1.0 if value_col is None else value_col[:, e : e + 1]
        pick = jnp.where(place == slot_col[:, e : e + 1], value, 0.0).astype(BF16)
        part = dot_nn(pick, chunk_refs[e // exp_dev][e % exp_dev])
        total = part if total is None else total + part
    return total


def backward_kernel(
    heads, ep_size, pack_blocks, place_ref, bias_ref, tok_ref, cot_ref, resid_ref, qkv_ref, att_ref, lse_ref, slot_col_ref, w_qkv_ref, w_out_ref, vec_ref, *rest
):
    chunk_refs = rest[:ep_size]
    packed = len(pack_blocks)
    gtok_ref = rest[ep_size]
    pack_refs = rest[ep_size + 1 : ep_size + 1 + packed]
    gw_qkv_ref, gw_out_ref, gvec_ref, gqkv_ref = rest[ep_size + 1 + packed : ep_size + 5 + packed]
    img = pl.program_id(0)
    seq, width = tok_ref.shape[1:]
    capp = chunk_refs[0].shape[1]
    grad_second = gather_rows(slot_col_ref[0], None, chunk_refs, capp)
    norm_second, inv_second = norm_parts(resid_ref[0])
    grad_resid = cot_ref[0].astype(F32) + norm_back(grad_second, norm_second, inv_second, vec_ref[3:4, :])
    grad_branch = grad_resid.astype(BF16)
    grad_att = dot_nt(grad_branch, w_out_ref[...]).astype(BF16)
    gw_out = dot_tn(att_ref[0], grad_branch)
    low = lax.broadcasted_iota(jnp.int32, (seq, 2 * HD), 1) < HD
    nothing = jnp.zeros((seq, 2 * HD), BF16)
    scale = jnp.asarray(HD ** (-0.5), BF16)
    for pair in range(heads // 2):
        at = pair * 2 * HD
        query = qkv_ref[0, :, at : at + 2 * HD] * scale
        key = qkv_ref[0, :, width + at : width + at + 2 * HD]
        value = qkv_ref[0, :, 2 * width + at : 2 * width + at + 2 * HD]
        gatt = grad_att[:, at : at + 2 * HD]
        grad_q = grad_k = grad_v = None
        for half in range(2):
            mine = low if half == 0 else jnp.logical_not(low)
            head = 2 * pair + half
            query_h = jnp.where(mine, query, nothing)
            gatt_h = jnp.where(mine, gatt, nothing)
            key_h = jnp.where(mine, key, nothing) * scale
            prob = jnp.exp(dot_nt(query_h, key) - lse_ref[0, :, head : head + 1])
            grad_prob = dot_nt(gatt_h, value)
            mean = jnp.sum(grad_prob * prob, axis=-1, keepdims=True)
            grad_scores = (prob * (grad_prob - mean)).astype(BF16)
            part_v = dot_tn(prob.astype(BF16), gatt_h)
            part_q = dot_nn(grad_scores, key_h)
            part_k = dot_tn(grad_scores, query_h)
            grad_q = part_q if grad_q is None else grad_q + part_q
            grad_k = part_k if grad_k is None else grad_k + part_k
            grad_v = part_v if grad_v is None else grad_v + part_v
        gqkv_ref[:, at : at + 2 * HD] = grad_q.astype(BF16)
        gqkv_ref[:, width + at : width + at + 2 * HD] = grad_k.astype(BF16)
        gqkv_ref[:, 2 * width + at : 2 * width + at + 2 * HD] = grad_v.astype(BF16)
    grad_qkv = gqkv_ref[...]
    norm_first, inv_first = norm_parts(tok_ref[0].astype(F32))
    first = (norm_first * vec_ref[0:1, :] + vec_ref[1:2, :]).astype(BF16)
    gw_qkv = dot_tn(first, grad_qkv)
    grad_first = dot_nt(grad_qkv, w_qkv_ref[...])
    gtok_ref[0] = (grad_resid + norm_back(grad_first, norm_first, inv_first, vec_ref[0:1, :])).astype(BF16)
    sums = [
        grad_first * norm_first,
        grad_first,
        grad_branch.astype(F32),
        grad_second * norm_second,
        grad_second,
    ]
    gvec = jnp.concatenate([jnp.sum(v, axis=0, keepdims=True) for v in sums] + [jnp.zeros((3, width), F32)], axis=0)

    @pl.when(img == 0)
    def _():
        gw_out_ref[...] = gw_out
        gw_qkv_ref[...] = gw_qkv
        gvec_ref[...] = gvec

    @pl.when(img > 0)
    def _():
        gw_out_ref[...] += gw_out
        gw_qkv_ref[...] += gw_qkv
        gvec_ref[...] += gvec

    if not packed:
        return

    @pl.when(img == pl.num_programs(0) - 1)
    def _():
        small_ref = rest[-1]
        blocks, per_pack, rows = pack_refs[0].shape[:3]
        per_ep = width // ep_size
        biases = bias_ref.shape[0]
        small_ref[...] = jnp.zeros(small_ref.shape, F32)
        for j in range(ep_size):
            owner = place_ref[0] ^ j
            small_ref[0:8, :] = gvec_ref[:, pl.ds(pl.multiple_of(owner * per_ep, per_ep), per_ep)]
            small_ref[8 : 8 + biases, :] = bias_ref[...] if j == 0 else jnp.zeros(bias_ref.shape, F32)
            for r in range(blocks):
                block = pack_blocks[j // per_pack][r] ^ place_ref[1]
                start = pl.multiple_of(owner * per_ep + block * rows, rows)
                into = pack_refs[j // per_pack]
                into[r, j % per_pack, :, 0 : 3 * width] = gw_qkv_ref[pl.ds(start, rows), :].astype(BF16)
                into[r, j % per_pack, :, 3 * width : 4 * width] = gw_out_ref[pl.ds(start, rows), :].astype(BF16)
                small = small_ref[pl.ds(pl.multiple_of(block * rows, rows), rows), :]
                into[r, j % per_pack, :, 4 * width :] = small.astype(BF16)


def backward_call(tokens, cotangent, resid, qkv, attended, lse, slot_col, w_qkv, w_out, vecs, chunks, place, biases, pack_blocks):
    n_img, seq, width = tokens.shape
    ep_size = len(chunks)
    packed = len(pack_blocks)
    image = lambda arr: pl.BlockSpec((1,) + arr.shape[1:], lambda i: (i, 0, 0))
    sums = [
        jax.ShapeDtypeStruct(w_qkv.shape, F32),
        jax.ShapeDtypeStruct(w_out.shape, F32),
        jax.ShapeDtypeStruct((8, width), F32),
    ]
    scratch = [pltpu.VMEM((seq, 3 * width), BF16)]
    if packed:
        grp_size = len(pack_blocks[0])
        pack = (grp_size, ep_size // 2, width // (ep_size * grp_size), 4 * width + 128)
        outs = [jax.ShapeDtypeStruct(pack, BF16)] * 2
        scratch = [pltpu.VMEM(v.shape, F32) for v in sums] + scratch + [pltpu.VMEM((width // ep_size, 128), F32)]
    else:
        outs = sums
        place, biases = jnp.zeros((2,), jnp.int32), jnp.zeros((8, 128), F32)
    return pl.pallas_call(
        functools.partial(backward_kernel, width // HD, ep_size, pack_blocks),
        grid=(n_img,),
        in_specs=[pl.BlockSpec(memory_space=pltpu.SMEM), whole(biases.shape)]
        + [image(a) for a in (tokens, cotangent, resid, qkv, attended, lse, slot_col)]
        + [whole(a.shape) for a in (w_qkv, w_out, vecs, *chunks)],
        out_specs=[image(tokens)] + [whole(v.shape) for v in outs],
        out_shape=[jax.ShapeDtypeStruct(tokens.shape, BF16)] + outs,
        scratch_shapes=scratch,
        compiler_params=params("arbitrary"),
        cost_estimate=COST,
        name="attention_backward",
    )(place, biases, tokens, cotangent, resid, qkv, attended, lse, slot_col, w_qkv, w_out, vecs, *chunks)


def combine_kernel(ep_size, resid_ref, slot_col_ref, gate_col_ref, *rest):
    chunk_refs, out_ref = rest[:ep_size], rest[ep_size]
    mixed = gather_rows(slot_col_ref[0], gate_col_ref[0], chunk_refs, chunk_refs[0].shape[1])
    out_ref[0] = (resid_ref[0] + mixed).astype(BF16)


def combine_call(resid, slot_col, gate_col, chunks):
    n_img, seq, width = resid.shape
    image = lambda arr: pl.BlockSpec((1,) + arr.shape[1:], lambda i: (i, 0, 0))
    return pl.pallas_call(
        functools.partial(combine_kernel, len(chunks)),
        grid=(n_img,),
        in_specs=[image(a) for a in (resid, slot_col, gate_col)] + [whole(c.shape) for c in chunks],
        out_specs=image(resid),
        out_shape=jax.ShapeDtypeStruct(resid.shape, BF16),
        compiler_params=params("arbitrary"),
        cost_estimate=COST,
        name="combine_output",
    )(resid, slot_col, gate_col, *chunks)


def swap(array, axis, size, distance):
    return lax.ppermute(array, axis, [(i, i ^ distance) for i in range(size)])


def digits(index, bits):
    number = jnp.zeros((), jnp.int32)
    for bit in bits:
        number = number * 2 + (index >> bit) % 2
    return number


def scatter_sums(arrays, orders, size):
    for step in range(len(orders[0])):
        halves = [a.shape[0] // 2 for a in arrays]
        came = [swap(a[h:], "grp", size, 1 << o[step]) for a, h, o in zip(arrays, halves, orders)]
        arrays = [a[:h] + c for a, h, c in zip(arrays, halves, came)]
    return arrays


def gather_sums(block, order, size):
    pieces = [block]
    for bit in reversed(order):
        pieces = pieces + [swap(p, "grp", size, 1 << bit) for p in pieces]
    return pieces


def widen_kernel(exp_dev, count, place_ref, *refs):
    piece_refs, out_ref = refs[: exp_dev * count], refs[-1]
    for e in range(exp_dev):
        for r in range(count):
            @pl.when((pl.program_id(0) == e) & (pl.program_id(1) == r))
            def _():
                out_ref[0] = piece_refs[e * count + r][0].astype(F32)


def widen_call(own, other, place, axis, shape):
    count = len(own)
    _, m, n = own[0].shape
    at = (lambda l, r, s: (l ^ s[0], r ^ s[1], 0)) if axis == 0 else (lambda l, r, s: (l ^ s[0], 0, r ^ s[1]))
    return pl.pallas_call(
        functools.partial(widen_kernel, 2, count),
        grid_spec=pltpu.PrefetchScalarGridSpec(
            num_scalar_prefetch=1,
            grid=(2, count),
            in_specs=[pl.BlockSpec((1, m, n), lambda l, r, s: (0, 0, 0))] * (2 * count),
            out_specs=pl.BlockSpec((1, m, n), at),
        ),
        out_shape=jax.ShapeDtypeStruct(shape, F32),
        compiler_params=params("arbitrary", "arbitrary"),
        cost_estimate=COST,
        name="expert_gradient_result",
    )(place, *own, *other)


def unpack_kernel(width, exp_dev, hidden, offsets, place_ref, *refs):
    piece_refs = refs[: len(offsets)]
    gw_qkv_ref, gw_out_ref, vec_ref, b_in_ref, b_back_ref, small_ref = refs[len(offsets) :]
    rows = piece_refs[0].shape[0]
    for piece_ref, offset in zip(piece_refs, offsets):
        at = pl.ds(pl.multiple_of((place_ref[0] ^ offset) * rows, rows), rows)
        gw_qkv_ref[at, :] = piece_ref[:, 0 : 3 * width].astype(F32)
        gw_out_ref[at, :] = piece_ref[:, 3 * width : 4 * width].astype(F32)
        small_ref[at, :] = piece_ref[:, 4 * width :].astype(F32)
    vec_ref[...] = small_ref[0:8, :]
    row = 8
    for ref, length in ((b_in_ref, hidden), (b_back_ref, width)):
        for e in range(exp_dev):
            for at in range(0, length, 128):
                ref[e : e + 1, at : at + 128] = small_ref[row : row + 1, :]
                row += 1


def unpack_call(pieces, offsets, place, width, exp_dev, hidden):
    rows = pieces[0].shape[0] * len(pieces)
    shapes = [(rows, 3 * width), (rows, width), (8, 128), (exp_dev, hidden), (exp_dev, width)]
    return pl.pallas_call(
        functools.partial(unpack_kernel, width, exp_dev, hidden, offsets),
        in_specs=[pl.BlockSpec(memory_space=pltpu.SMEM)] + [pl.BlockSpec(memory_space=pltpu.VMEM)] * len(pieces),
        out_specs=[pl.BlockSpec(memory_space=pltpu.VMEM)] * len(shapes),
        out_shape=[jax.ShapeDtypeStruct(v, F32) for v in shapes],
        scratch_shapes=[pltpu.VMEM((rows, 128), F32)],
        compiler_params=params(),
        cost_estimate=COST,
        name="parameter_gradient_results",
    )(place, *pieces)


def after(arrays, *others):
    return lax.optimization_barrier((list(arrays), others))[0]


def local(
    tokens,
    routes,
    gates,
    ln1_gain,
    ln1_bias,
    w_qkv,
    w_out,
    out_bias,
    ln2_gain,
    ln2_bias,
    w_in,
    in_bias,
    w_back,
    back_bias,
    cotangent,
):
    images, seq_len, width = tokens.shape
    ep_size = lax.axis_size("ep")
    exp_dev = w_in.shape[0]
    experts = exp_dev * ep_size
    capacity = (images * seq_len * 10 + 4 * experts - 1) // (4 * experts)
    capp = -(-capacity // 8) * 8
    me = lax.axis_index("ep").astype(jnp.int32).reshape(1)
    vecs = jnp.stack([ln1_gain, ln1_bias, out_bias, ln2_gain, ln2_bias] + [jnp.zeros_like(ln1_gain)] * 3)

    def exchange(chunks):
        return [chunks[0]] + [swap(chunks[d], "ep", ep_size, d) for d in range(1, ep_size)]

    slot_row, slot_col, gate_col, *g_send = route_call(me, routes, gates, cotangent, ep_size, exp_dev, capp)
    g_all = exchange(g_send)
    qkv, attended, lse, resid, *x_send = attention_call(tokens, w_qkv, w_out, vecs, slot_row, ep_size, exp_dev, capp)
    x_all = exchange(x_send)
    b_in, b_back = in_bias[:, None, :], back_bias[:, None, :]
    acts, gpres, outs, gdis = [], [], [], []
    for d in range(ep_size):
        a, p, o, g = expert_call(x_all[d : d + 1], g_all[d : d + 1], w_in, w_back, b_in, b_back, 512)
        acts += a
        gpres += p
        outs += o
        gdis += g
    gdis_back = exchange(gdis)
    outs_back = exchange(outs)
    grp_size = lax.axis_size("grp")
    grp = lax.axis_index("grp").astype(jnp.int32)
    bits = list(range(grp_size.bit_length() - 1))
    order_a, order_b = bits[1:], bits[:0:-1]
    blocks = grp_size // 2
    core = grp % 2
    place_a = jnp.stack([core, digits(grp, order_a)])
    place_b = jnp.stack([core, digits(grp, order_b)])
    flip = jnp.array([1, 0], jnp.int32)
    gwb_far, gbb_far = weight_call(acts, g_all, place_a ^ flip, blocks, True)
    gwi_far, gbi_far = weight_call(x_all, gpres, place_b ^ flip, blocks, False)
    gwb_far = swap(gwb_far, "grp", grp_size, 1)
    gwi_far = swap(gwi_far, "grp", grp_size, 1)
    gwb, gbb = weight_call(acts, g_all, place_a, blocks, True)
    gwi, gbi = weight_call(x_all, gpres, place_b, blocks, False)
    sum_b, sum_i = scatter_sums([gwb + gwb_far, gwi + gwi_far], [order_a, order_b], grp_size)
    all_b, all_i = gather_sums(sum_b, order_a, grp_size), gather_sums(sum_i, order_b, grp_size)
    oth_b = [swap(p, "grp", grp_size, 1) for p in all_b]
    oth_i = [swap(p, "grp", grp_size, 1) for p in all_i]
    gw_back = widen_call(all_b, oth_b, place_a, 0, w_back.shape)
    gw_in = widen_call(all_i, oth_i, place_b, 1, w_in.shape)

    def by_expert(near, far):
        return jnp.where(core == 0, jnp.concatenate([near, far]), jnp.concatenate([far, near]))[:, 0]

    gb_in, gb_back = by_expert(gbi, gbi_far), by_expert(gbb, gbb_far)
    hidden = w_in.shape[2]
    packed = width // ep_size == 128 and 128 % (16 * grp_size) == 0
    place, biases, pack_blocks = None, None, ()
    if packed:
        order_p, order_q = [0] + order_a, [0] + order_b
        pack_blocks = tuple(
            tuple(sum((r >> (len(o) - 1 - k)) % 2 << bit for k, bit in enumerate(o)) for r in range(grp_size))
            for o in (order_p, order_q)
        )
        place = jnp.stack([me[0], grp])
        biases = jnp.concatenate([gb_in.reshape(-1, 128), gb_back.reshape(-1, 128)])
    grad_tokens, *grads = backward_call(
        tokens, cotangent, resid, qkv, attended, lse, slot_col, w_qkv, w_out, vecs, gdis_back, place, biases, pack_blocks
    )
    output = combine_call(resid, slot_col, gate_col, outs_back)
    if packed:
        near, far = scatter_sums(grads, [order_p, order_q], grp_size)
        parts = [near[0, d] for d in range(ep_size // 2)] + [far[0, d] for d in range(ep_size // 2)]
        parts = exchange(parts)
        total = parts[0].astype(F32)
        for part in parts[1:]:
            total = total + part.astype(F32)
        pieces, offsets = [total.astype(BF16)], [0]
        for bit in reversed(bits):
            pieces = pieces + [swap(p, "grp", grp_size, 1 << bit) for p in pieces]
            offsets = offsets + [o ^ (1 << bit) for o in offsets]
        gw_qkv, gw_out, gvec, gb_in, gb_back = unpack_call(pieces, offsets, grp.reshape(1), width, exp_dev, hidden)
        gvec = [gvec[k] for k in range(5)]
    else:
        def over_grp(v):
            return lax.psum(v.astype(BF16), "grp").astype(F32)

        def over_all(v):
            return over_grp(lax.psum_scatter(v.astype(BF16), "ep", scatter_dimension=0, tiled=True))

        gw_qkv, gw_out, gvec = grads
        gw_qkv, gw_out, gb_in, gb_back = over_all(gw_qkv), over_all(gw_out), over_grp(gb_in), over_grp(gb_back)
        gvec = [over_all(gvec[k]) for k in range(5)]
    return (output, grad_tokens, gvec[0], gvec[1], gw_qkv, gw_out, gvec[2], gvec[3], gvec[4], gw_in, gb_in, gw_back, gb_back)


def solution(mesh):
    rows = P(("grp", "ep"), None, None)
    return jax.shard_map(
        local,
        mesh=mesh,
        in_specs=(rows, rows, rows)
        + (P(),) * 7
        + (P("ep", None, None), P("ep", None), P("ep", None, None), P("ep", None), rows),
        out_specs=(rows, rows)
        + (P("ep"), P("ep"), P("ep", None), P("ep", None), P("ep"), P("ep"), P("ep"))
        + (P("ep", None, None), P("ep", None), P("ep", None, None), P("ep", None)),
        check_vma=False,
    )
```

```python
import functools

import jax
import jax.numpy as jnp
from jax import lax
from jax.experimental import pallas as pl
from jax.experimental.pallas import tpu as pltpu
from jax.sharding import PartitionSpec as P

HD = 64
NORM_EPS = 1e-06
BF16 = jnp.bfloat16
F32 = jnp.float32
VMEM_LIMIT = 60 * 1024 * 1024
GELU_C = 0.7978845608028654


def cost(microseconds):
    return pl.CostEstimate(flops=int(microseconds * 10**9), bytes_accessed=2**12, transcendentals=0)


def dot_nn(a, b):
    return jnp.dot(a, b, preferred_element_type=F32)


def dot_nt(a, b):
    return lax.dot_general(a, b, (((1,), (1,)), ((), ())), preferred_element_type=F32)


def dot_tn(a, b):
    return lax.dot_general(a, b, (((0,), (0,)), ((), ())), preferred_element_type=F32)


def norm_parts(values):
    average = jnp.mean(values, axis=-1, keepdims=True)
    centred = values - average
    inv_std = lax.rsqrt(jnp.mean(centred * centred, axis=-1, keepdims=True) + NORM_EPS)
    return centred * inv_std, inv_std


def norm_back(grad_norm, normed, inv_std, gain):
    scaled = grad_norm * gain
    return inv_std * (
        scaled
        - jnp.mean(scaled, axis=-1, keepdims=True)
        - normed * jnp.mean(scaled * normed, axis=-1, keepdims=True)
    )


def whole(shape):
    zeros = (0,) * len(shape)
    return pl.BlockSpec(tuple(shape), lambda *_: zeros)


def params(*semantics):
    return pltpu.CompilerParams(
        dimension_semantics=semantics or None, vmem_limit_bytes=VMEM_LIMIT
    )


def dispatch_rows(place, slots, values, source_refs, e):
    total = None
    for i, source in enumerate(source_refs):
        value = 1.0 if values is None else values[i][e : e + 1, :]
        pick = jnp.where(place == slots[i][e : e + 1, :], value, 0.0).astype(BF16)
        part = dot_nn(pick, source[...])
        total = part if total is None else total + part
    return total.astype(BF16)


def slot_places(capp, seq):
    return lax.broadcasted_iota(jnp.int32, (capp, seq), 0).astype(F32)


def route_kernel(exp_dev, me_ref, routes_ref, gates_ref, cot_ref, info_ref, slot_col_ref, gate_col_ref, *rest):
    out_refs, scratch = rest[:-1], rest[-1]
    n_img, seq, width = cot_ref.shape
    experts = info_ref.shape[2]
    capp = out_refs[0].shape[1]
    me = me_ref[0]
    expert = lax.broadcasted_iota(jnp.int32, (experts, seq), 0)
    expert = ((expert // exp_dev) ^ me) * exp_dev + expert % exp_dev
    earlier = lax.broadcasted_iota(jnp.int32, (seq, seq), 0)
    later = lax.broadcasted_iota(jnp.int32, (seq, seq), 1)
    tri = jnp.where(earlier < later, 1.0, 0.0).astype(BF16)
    carry = jnp.zeros((experts, 1), F32)
    slots, gate_rows = [], []
    for i in range(n_img):
        hit0 = expert == routes_ref[0, i : i + 1, :]
        hit1 = expert == routes_ref[1, i : i + 1, :]
        member = jnp.where(hit0 | hit1, 1.0, 0.0)
        slot = jnp.where(member > 0.5, dot_nn(member.astype(BF16), tri) + carry, -1.0)
        gate = jnp.where(hit0, gates_ref[0, i : i + 1, :], jnp.where(hit1, gates_ref[1, i : i + 1, :], 0.0))
        carry = carry + jnp.sum(member, axis=1, keepdims=True)
        slots.append(slot)
        gate_rows.append(gate)
        info_ref[0, i] = slot
        info_ref[1, i] = gate
        scratch[0, 0:experts, 0:seq] = slot
        scratch[1, 0:experts, 0:seq] = gate
        slot_col_ref[i] = jnp.transpose(scratch[0])[:seq, :experts]
        gate_col_ref[i] = jnp.transpose(scratch[1])[:seq, :experts]
    place = slot_places(capp, seq)
    sources = [cot_ref.at[i] for i in range(n_img)]
    for e in range(len(out_refs) * exp_dev):
        out_refs[e // exp_dev][e % exp_dev] = dispatch_rows(place, slots, gate_rows, sources, e)


def route_call(me, routes, gates, cotangent, ep_size, exp_dev, capp):
    n_img, seq, width = cotangent.shape
    experts = ep_size * exp_dev
    seq_pad = -(-seq // 128) * 128
    chunk = jax.ShapeDtypeStruct((exp_dev, capp, width), BF16)
    return pl.pallas_call(
        functools.partial(route_kernel, exp_dev),
        in_specs=[pl.BlockSpec(memory_space=pltpu.SMEM)] + [pl.BlockSpec(memory_space=pltpu.VMEM)] * 3,
        out_specs=[pl.BlockSpec(memory_space=pltpu.VMEM)] * (3 + ep_size // 2),
        out_shape=[
            jax.ShapeDtypeStruct((2, n_img, experts, seq), F32),
            jax.ShapeDtypeStruct((n_img, seq, experts), F32),
            jax.ShapeDtypeStruct((n_img, seq, experts), F32),
        ]
        + [chunk] * (ep_size // 2),
        scratch_shapes=[pltpu.VMEM((2, 128, seq_pad), F32)],
        compiler_params=params(),
        cost_estimate=cost(4),
        name="route_and_dispatch_cotangent",
    )(me, routes.transpose(2, 0, 1), gates.transpose(2, 0, 1), cotangent)


def gateway_kernel(exp_dev, info_ref, cot_ref, *out_refs):
    n_img, seq, width = cot_ref.shape
    capp = out_refs[0].shape[1]
    place = slot_places(capp, seq)
    slots = [info_ref[0, i] for i in range(n_img)]
    gate_rows = [info_ref[1, i] for i in range(n_img)]
    sources = [cot_ref.at[i] for i in range(n_img)]
    half = len(out_refs)
    for j in range(half):
        for k in range(exp_dev):
            out_refs[j][k] = dispatch_rows(place, slots, gate_rows, sources, (half ^ j) * exp_dev + k)


def gateway_call(info, cotangent, ep_size, exp_dev, capp):
    chunk = jax.ShapeDtypeStruct((exp_dev, capp, cotangent.shape[2]), BF16)
    return pl.pallas_call(
        functools.partial(gateway_kernel, exp_dev),
        in_specs=[pl.BlockSpec(memory_space=pltpu.VMEM)] * 2,
        out_specs=[pl.BlockSpec(memory_space=pltpu.VMEM)] * (ep_size // 2),
        out_shape=[chunk] * (ep_size // 2),
        compiler_params=params(),
        cost_estimate=cost(3),
        name="dispatch_far_cotangent",
    )(info, cotangent)


def attention_kernel(
    heads, tok_ref, w_qkv_ref, w_out_ref, vec_ref, info_ref, qkv_ref, att_ref, lse_ref, resid_ref, *rest
):
    out_refs, second_ref = rest[:-1], rest[-1]
    img = pl.program_id(0)
    seq, width = tok_ref.shape[1:]
    exp_dev, capp = out_refs[0].shape[:2]
    inputs = tok_ref[0].astype(F32)
    norm_first, _ = norm_parts(inputs)
    first = (norm_first * vec_ref[0:1, :] + vec_ref[1:2, :]).astype(BF16)
    qkv = dot_nn(first, w_qkv_ref[...]).astype(BF16)
    qkv_ref[0] = qkv
    low = lax.broadcasted_iota(jnp.int32, (seq, 2 * HD), 1) < HD
    nothing = jnp.zeros((seq, 2 * HD), BF16)
    lane = lax.broadcasted_iota(jnp.int32, (seq, 128), 1)
    lse_all = jnp.zeros((seq, 128), F32)
    pieces = []
    for pair in range(heads // 2):
        at = pair * 2 * HD
        query = qkv[:, at : at + 2 * HD] * jnp.asarray(HD ** (-0.5), BF16)
        key = qkv[:, width + at : width + at + 2 * HD]
        value = qkv[:, 2 * width + at : 2 * width + at + 2 * HD]
        halves = []
        for half in range(2):
            mine = low if half == 0 else jnp.logical_not(low)
            scores = dot_nt(jnp.where(mine, query, nothing), key)
            top = jnp.max(scores, axis=-1, keepdims=True)
            weight = jnp.exp(scores - top)
            total = jnp.sum(weight, axis=-1, keepdims=True)
            prob = (weight * (1.0 / total)).astype(BF16)
            halves.append(dot_nn(prob, value))
            lse_all = jnp.where(lane == 2 * pair + half, top + jnp.log(total), lse_all)
        pieces.append(jnp.where(low, halves[0], halves[1]).astype(BF16))
    lse_ref[0] = lse_all
    attended = jnp.concatenate(pieces, axis=1)
    att_ref[0] = attended
    resid = inputs + dot_nn(attended, w_out_ref[...]) + vec_ref[2:3, :]
    resid_ref[0] = resid
    norm_second, _ = norm_parts(resid)
    second_ref[img] = (norm_second * vec_ref[3:4, :] + vec_ref[4:5, :]).astype(BF16)

    @pl.when(img == pl.num_programs(0) - 1)
    def _():
        n_img = second_ref.shape[0]
        place = slot_places(capp, seq)
        slots = [info_ref[0, i] for i in range(n_img)]
        sources = [second_ref.at[i] for i in range(n_img)]
        for e in range(len(out_refs) * exp_dev):
            out_refs[e // exp_dev][e % exp_dev] = dispatch_rows(place, slots, None, sources, e)


def attention_call(tokens, w_qkv, w_out, vecs, info, ep_size, exp_dev, capp):
    n_img, seq, width = tokens.shape
    chunk = jax.ShapeDtypeStruct((exp_dev, capp, width), BF16)
    image = lambda *tail: pl.BlockSpec((1,) + tail, lambda i: (i, 0, 0))
    return pl.pallas_call(
        functools.partial(attention_kernel, width // HD),
        grid=(n_img,),
        in_specs=[image(seq, width), whole(w_qkv.shape), whole(w_out.shape), whole(vecs.shape), whole(info.shape)],
        out_specs=[image(seq, 3 * width), image(seq, width), image(seq, 128), image(seq, width)]
        + [whole(chunk.shape)] * ep_size,
        out_shape=[
            jax.ShapeDtypeStruct((n_img, seq, 3 * width), BF16),
            jax.ShapeDtypeStruct((n_img, seq, width), BF16),
            jax.ShapeDtypeStruct((n_img, seq, 128), F32),
            jax.ShapeDtypeStruct((n_img, seq, width), F32),
        ]
        + [chunk] * ep_size,
        scratch_shapes=[pltpu.VMEM((n_img, seq, width), BF16)],
        compiler_params=params("arbitrary"),
        cost_estimate=cost(14),
        name="attention_forward_and_dispatch",
    )(tokens, w_qkv, w_out, vecs, info)


def expert_kernel(count, carried, blocks, tile, sel_ref, *refs):
    x_refs, g_refs = refs[:count], refs[count : 2 * count]
    w_in_hbm, w_back_hbm, b_in_ref, b_back_ref = refs[2 * count : 2 * count + 4]
    before = refs[2 * count + 4 : 2 * count + 4 + carried]
    outs = refs[2 * count + 4 + carried :]
    out_refs, gdis_refs = outs[:count], outs[count : 2 * count]
    sums, (gb_in_ref, gb_back_ref) = outs[2 * count : 2 * count + 4], outs[2 * count + 4 : 2 * count + 6]
    w_in_buf, w_back_buf, back_buf, in_buf, acc_out, acc_dis, load_sem, sum_sem, store_sem = outs[2 * count + 6 :]
    exp_dev, _, hidden = w_in_buf.shape
    block = hidden // blocks
    steps = [(l, t) for l in range(exp_dev) for t in range(hidden // tile)]

    def loads(l, t):
        e = sel_ref[0] ^ l
        span = pl.ds(t * tile, tile)
        return [
            pltpu.make_async_copy(w_in_hbm.at[e, :, span], w_in_buf.at[l, :, span], load_sem.at[l, t, 0]),
            pltpu.make_async_copy(w_back_hbm.at[e, span, :], w_back_buf.at[l, span, :], load_sem.at[l, t, 1]),
        ]

    def blocks_of(t):
        return range(t * tile // block, (t + 1) * tile // block)

    def sum_loads(l, t):
        return [
            copy
            for b in blocks_of(t)
            for copy in (
                pltpu.make_async_copy(before[2 * l].at[b ^ sel_ref[1]], back_buf.at[l, b], sum_sem.at[l, b, 0]),
                pltpu.make_async_copy(before[2 * l + 1].at[b ^ sel_ref[2]], in_buf.at[l, b], sum_sem.at[l, b, 1]),
            )
        ]

    def stores(l, t):
        return [
            copy
            for b in blocks_of(t)
            for copy in (
                pltpu.make_async_copy(back_buf.at[l, b], sums[2 * l].at[b ^ sel_ref[1]], store_sem.at[l, b, 0]),
                pltpu.make_async_copy(in_buf.at[l, b], sums[2 * l + 1].at[b ^ sel_ref[2]], store_sem.at[l, b, 1]),
            )
        ]

    for l, t in steps:
        for copy in loads(l, t):
            copy.start()
    if carried:
        for l, t in steps:
            for copy in sum_loads(l, t):
                copy.start()
    for l, t in steps:
        e = sel_ref[0] ^ l
        span = slice(t * tile, (t + 1) * tile)
        for copy in loads(l, t):
            copy.wait()
        w_in, w_back = w_in_buf[l, :, span], w_back_buf[l, span, :]
        gw_back = gw_in = gb_in = None
        for n in range(count):
            x, g = x_refs[n][e], g_refs[n][e]
            pre = dot_nn(x, w_in) + b_in_ref[e, :, span]
            square = pre * pre
            bent = jnp.tanh(pre * (GELU_C + (GELU_C * 0.044715) * square))
            half = 0.5 + 0.5 * bent
            act = (pre * half).astype(BF16)
            slope = half + (pre * (0.5 - 0.5 * bent * bent)) * (GELU_C + (3 * GELU_C * 0.044715) * square)
            gpre = (dot_nt(g, w_back) * slope).astype(BF16)
            part_dis, part_out = dot_nt(gpre, w_in), dot_nn(act, w_back)
            if t == 0:
                part_out = part_out + b_back_ref[e]
            else:
                part_dis, part_out = part_dis + acc_dis[n], part_out + acc_out[n]
            if span.stop == hidden:
                gdis_refs[n][e] = part_dis.astype(BF16)
                out_refs[n][e] = part_out.astype(BF16)
            else:
                acc_dis[n] = part_dis
                acc_out[n] = part_out
            one = (dot_tn(act, g), dot_tn(x, gpre), jnp.sum(gpre.astype(F32), axis=0, keepdims=True))
            gw_back = one[0] if n == 0 else gw_back + one[0]
            gw_in = one[1] if n == 0 else gw_in + one[1]
            gb_in = one[2] if n == 0 else gb_in + one[2]
        gb_in_ref[e, :, span] = gb_in
        if carried:
            for copy in sum_loads(l, t):
                copy.wait()
        for b in blocks_of(t):
            at = slice(b * block - t * tile, (b + 1) * block - t * tile)
            back, into = gw_back[at, :], gw_in[:, at]
            if carried:
                back, into = back + back_buf[l, b].astype(F32), into + in_buf[l, b].astype(F32)
            back_buf[l, b] = back.astype(BF16)
            in_buf[l, b] = into.astype(BF16)
        for copy in stores(l, t):
            copy.start()
    for e in range(exp_dev):
        total = jnp.sum(g_refs[0][e].astype(F32), axis=0, keepdims=True)
        for n in range(1, count):
            total = total + jnp.sum(g_refs[n][e].astype(F32), axis=0, keepdims=True)
        gb_back_ref[e] = total
    for l, t in steps:
        for copy in stores(l, t):
            copy.wait()


def expert_call(xs, gs, w_in, w_back, b_in, b_back, place, blocks, before, microseconds):
    count = len(xs)
    exp_dev, capp, width = xs[0].shape
    hidden = w_in.shape[2]
    block = hidden // blocks
    tile = max(block, min(hidden, 512))
    narrow = jax.ShapeDtypeStruct((exp_dev, capp, width), BF16)
    shapes = [jax.ShapeDtypeStruct((blocks, block, width), BF16), jax.ShapeDtypeStruct((blocks, width, block), BF16)] * 2
    held = pl.BlockSpec(memory_space=pltpu.VMEM)
    remote = pl.BlockSpec(memory_space=pl.ANY)
    res = pl.pallas_call(
        functools.partial(expert_kernel, count, len(before), blocks, tile),
        in_specs=[pl.BlockSpec(memory_space=pltpu.SMEM)]
        + [held] * (2 * count)
        + [remote] * 2
        + [held] * 2
        + [remote] * len(before),
        out_specs=[held] * (2 * count) + [remote] * 4 + [held] * 2,
        out_shape=[narrow] * (2 * count)
        + shapes
        + [jax.ShapeDtypeStruct((exp_dev, 1, hidden), F32), jax.ShapeDtypeStruct((exp_dev, 1, width), F32)],
        scratch_shapes=[
            pltpu.VMEM((exp_dev, width, hidden), BF16),
            pltpu.VMEM((exp_dev, hidden, width), BF16),
            pltpu.VMEM((exp_dev, blocks, block, width), BF16),
            pltpu.VMEM((exp_dev, blocks, width, block), BF16),
            pltpu.VMEM((count, capp, width), F32),
            pltpu.VMEM((count, capp, width), F32),
            pltpu.SemaphoreType.DMA((exp_dev, blocks, 2)),
            pltpu.SemaphoreType.DMA((exp_dev, blocks, 2)),
            pltpu.SemaphoreType.DMA((exp_dev, blocks, 2)),
        ],
        compiler_params=params(),
        cost_estimate=cost(microseconds),
        name="experts",
    )(place, *xs, *gs, w_in, w_back, b_in, b_back, *before)
    return res[:count], res[count : 2 * count], res[2 * count : 2 * count + 4], res[2 * count + 4 :]


def gather_rows(slot_col, value_col, chunk_refs, capp):
    seq = slot_col.shape[0]
    exp_dev = chunk_refs[0].shape[0]
    place = lax.broadcasted_iota(jnp.int32, (seq, capp), 1).astype(F32)
    total = None
    for e in range(len(chunk_refs) * exp_dev):
        value = 1.0 if value_col is None else value_col[:, e : e + 1]
        pick = jnp.where(place == slot_col[:, e : e + 1], value, 0.0).astype(BF16)
        part = dot_nn(pick, chunk_refs[e // exp_dev][e % exp_dev])
        total = part if total is None else total + part
    return total


def backward_kernel(
    heads, ep_size, pack_blocks, place_ref, bias_ref, tok_ref, cot_ref, resid_ref, qkv_ref, att_ref, lse_ref, slot_col_ref, w_qkv_ref, w_out_ref, vec_ref, *rest
):
    chunk_refs = rest[:ep_size]
    packed = len(pack_blocks)
    gtok_ref = rest[ep_size]
    pack_refs = rest[ep_size + 1 : ep_size + 1 + packed]
    gw_qkv_ref, gw_out_ref, gvec_ref, gqkv_ref = rest[ep_size + 1 + packed : ep_size + 5 + packed]
    img = pl.program_id(0)
    seq, width = tok_ref.shape[1:]
    capp = chunk_refs[0].shape[1]
    grad_second = gather_rows(slot_col_ref[0], None, chunk_refs, capp)
    norm_second, inv_second = norm_parts(resid_ref[0])
    grad_resid = cot_ref[0].astype(F32) + norm_back(grad_second, norm_second, inv_second, vec_ref[3:4, :])
    grad_branch = grad_resid.astype(BF16)
    grad_att = dot_nt(grad_branch, w_out_ref[...]).astype(BF16)
    gw_out = dot_tn(att_ref[0], grad_branch)
    low = lax.broadcasted_iota(jnp.int32, (seq, 2 * HD), 1) < HD
    nothing = jnp.zeros((seq, 2 * HD), BF16)
    scale = jnp.asarray(HD ** (-0.5), BF16)
    for pair in range(heads // 2):
        at = pair * 2 * HD
        query = qkv_ref[0, :, at : at + 2 * HD] * scale
        key = qkv_ref[0, :, width + at : width + at + 2 * HD]
        value = qkv_ref[0, :, 2 * width + at : 2 * width + at + 2 * HD]
        gatt = grad_att[:, at : at + 2 * HD]
        grad_q = grad_k = grad_v = None
        for half in range(2):
            mine = low if half == 0 else jnp.logical_not(low)
            head = 2 * pair + half
            query_h = jnp.where(mine, query, nothing)
            gatt_h = jnp.where(mine, gatt, nothing)
            key_h = jnp.where(mine, key, nothing) * scale
            prob = jnp.exp(dot_nt(query_h, key) - lse_ref[0, :, head : head + 1])
            grad_prob = dot_nt(gatt_h, value)
            mean = jnp.sum(grad_prob * prob, axis=-1, keepdims=True)
            grad_scores = (prob * (grad_prob - mean)).astype(BF16)
            part_v = dot_tn(prob.astype(BF16), gatt_h)
            part_q = dot_nn(grad_scores, key_h)
            part_k = dot_tn(grad_scores, query_h)
            grad_q = part_q if grad_q is None else grad_q + part_q
            grad_k = part_k if grad_k is None else grad_k + part_k
            grad_v = part_v if grad_v is None else grad_v + part_v
        gqkv_ref[:, at : at + 2 * HD] = grad_q.astype(BF16)
        gqkv_ref[:, width + at : width + at + 2 * HD] = grad_k.astype(BF16)
        gqkv_ref[:, 2 * width + at : 2 * width + at + 2 * HD] = grad_v.astype(BF16)
    grad_qkv = gqkv_ref[...]
    norm_first, inv_first = norm_parts(tok_ref[0].astype(F32))
    first = (norm_first * vec_ref[0:1, :] + vec_ref[1:2, :]).astype(BF16)
    gw_qkv = dot_tn(first, grad_qkv)
    grad_first = dot_nt(grad_qkv, w_qkv_ref[...])
    gtok_ref[0] = (grad_resid + norm_back(grad_first, norm_first, inv_first, vec_ref[0:1, :])).astype(BF16)
    sums = [
        grad_first * norm_first,
        grad_first,
        grad_branch.astype(F32),
        grad_second * norm_second,
        grad_second,
    ]
    gvec = jnp.concatenate([jnp.sum(v, axis=0, keepdims=True) for v in sums] + [jnp.zeros((3, width), F32)], axis=0)

    @pl.when(img == 0)
    def _():
        gw_out_ref[...] = gw_out
        gw_qkv_ref[...] = gw_qkv
        gvec_ref[...] = gvec

    @pl.when(img > 0)
    def _():
        gw_out_ref[...] += gw_out
        gw_qkv_ref[...] += gw_qkv
        gvec_ref[...] += gvec

    if not packed:
        return

    @pl.when(img == pl.num_programs(0) - 1)
    def _():
        small_ref = rest[-1]
        blocks, per_pack, rows = pack_refs[0].shape[:3]
        per_ep = width // ep_size
        biases = bias_ref.shape[0]
        small_ref[...] = jnp.zeros(small_ref.shape, F32)
        for j in range(ep_size):
            owner = place_ref[0] ^ j
            small_ref[0:8, :] = gvec_ref[:, pl.ds(pl.multiple_of(owner * per_ep, per_ep), per_ep)]
            small_ref[8 : 8 + biases, :] = bias_ref[...] if j == 0 else jnp.zeros(bias_ref.shape, F32)
            for r in range(blocks):
                block = pack_blocks[j // per_pack][r] ^ place_ref[1]
                start = pl.multiple_of(owner * per_ep + block * rows, rows)
                into = pack_refs[j // per_pack]
                into[r, j % per_pack, :, 0 : 3 * width] = gw_qkv_ref[pl.ds(start, rows), :].astype(BF16)
                into[r, j % per_pack, :, 3 * width : 4 * width] = gw_out_ref[pl.ds(start, rows), :].astype(BF16)
                small = small_ref[pl.ds(pl.multiple_of(block * rows, rows), rows), :]
                into[r, j % per_pack, :, 4 * width :] = small.astype(BF16)


def backward_call(tokens, cotangent, resid, qkv, attended, lse, slot_col, w_qkv, w_out, vecs, chunks, place, biases, pack_blocks):
    n_img, seq, width = tokens.shape
    ep_size = len(chunks)
    packed = len(pack_blocks)
    image = lambda arr: pl.BlockSpec((1,) + arr.shape[1:], lambda i: (i, 0, 0))
    sums = [
        jax.ShapeDtypeStruct(w_qkv.shape, F32),
        jax.ShapeDtypeStruct(w_out.shape, F32),
        jax.ShapeDtypeStruct((8, width), F32),
    ]
    scratch = [pltpu.VMEM((seq, 3 * width), BF16)]
    if packed:
        grp_size = len(pack_blocks[0])
        pack = (grp_size, ep_size // 2, width // (ep_size * grp_size), 4 * width + 128)
        outs = [jax.ShapeDtypeStruct(pack, BF16)] * 2
        scratch = [pltpu.VMEM(v.shape, F32) for v in sums] + scratch + [pltpu.VMEM((width // ep_size, 128), F32)]
    else:
        outs = sums
        place, biases = jnp.zeros((2,), jnp.int32), jnp.zeros((8, 128), F32)
    return pl.pallas_call(
        functools.partial(backward_kernel, width // HD, ep_size, pack_blocks),
        grid=(n_img,),
        in_specs=[pl.BlockSpec(memory_space=pltpu.SMEM), whole(biases.shape)]
        + [image(a) for a in (tokens, cotangent, resid, qkv, attended, lse, slot_col)]
        + [whole(a.shape) for a in (w_qkv, w_out, vecs, *chunks)],
        out_specs=[image(tokens)] + [whole(v.shape) for v in outs],
        out_shape=[jax.ShapeDtypeStruct(tokens.shape, BF16)] + outs,
        scratch_shapes=scratch,
        compiler_params=params("arbitrary"),
        cost_estimate=cost(25),
        name="attention_backward",
    )(place, biases, tokens, cotangent, resid, qkv, attended, lse, slot_col, w_qkv, w_out, vecs, *chunks)


def combine_kernel(ep_size, resid_ref, slot_col_ref, gate_col_ref, *rest):
    chunk_refs, out_ref = rest[:ep_size], rest[ep_size]
    mixed = gather_rows(slot_col_ref[0], gate_col_ref[0], chunk_refs, chunk_refs[0].shape[1])
    out_ref[0] = (resid_ref[0] + mixed).astype(BF16)


def combine_call(resid, slot_col, gate_col, chunks):
    n_img, seq, width = resid.shape
    image = lambda arr: pl.BlockSpec((1,) + arr.shape[1:], lambda i: (i, 0, 0))
    return pl.pallas_call(
        functools.partial(combine_kernel, len(chunks)),
        grid=(n_img,),
        in_specs=[image(a) for a in (resid, slot_col, gate_col)] + [whole(c.shape) for c in chunks],
        out_specs=image(resid),
        out_shape=jax.ShapeDtypeStruct(resid.shape, BF16),
        compiler_params=params("arbitrary"),
        cost_estimate=cost(5),
        name="combine_output",
    )(resid, slot_col, gate_col, *chunks)


def swap(array, axis, size, distance):
    return lax.ppermute(array, axis, [(i, i ^ distance) for i in range(size)])


def digits(index, bits):
    number = jnp.zeros((), jnp.int32)
    for bit in bits:
        number = number * 2 + (index >> bit) % 2
    return number


def scatter_step(arrays, bits, size):
    halves = [a.shape[0] // 2 for a in arrays]
    came = [swap(a[h:], "grp", size, 1 << bit) for a, h, bit in zip(arrays, halves, bits)]
    return [a[:h] + c for a, h, c in zip(arrays, halves, came)]


def gather_sums(block, order, size):
    pieces = [block]
    for bit in reversed(order):
        pieces = pieces + [swap(p, "grp", size, 1 << bit) for p in pieces]
    return pieces


def widen_kernel(exp_dev, count, place_ref, *refs):
    piece_refs, out_ref = refs[: exp_dev * count], refs[-1]
    for e in range(exp_dev):
        for r in range(count):
            @pl.when((pl.program_id(0) == e) & (pl.program_id(1) == r))
            def _():
                out_ref[0] = piece_refs[e * count + r][0].astype(F32)


def widen_call(own, other, place, axis, shape):
    count = len(own)
    _, m, n = own[0].shape
    at = (lambda l, r, s: (l ^ s[0], r ^ s[1], 0)) if axis == 0 else (lambda l, r, s: (l ^ s[0], 0, r ^ s[1]))
    return pl.pallas_call(
        functools.partial(widen_kernel, 2, count),
        grid_spec=pltpu.PrefetchScalarGridSpec(
            num_scalar_prefetch=1,
            grid=(2, count),
            in_specs=[pl.BlockSpec((1, m, n), lambda l, r, s: (0, 0, 0))] * (2 * count),
            out_specs=pl.BlockSpec((1, m, n), at),
        ),
        out_shape=jax.ShapeDtypeStruct(shape, F32),
        compiler_params=params("arbitrary", "arbitrary"),
        cost_estimate=cost(5),
        name="expert_gradient_result",
    )(place, *own, *other)


def unpack_kernel(width, exp_dev, hidden, offsets, place_ref, *refs):
    piece_refs = refs[: len(offsets)]
    gw_qkv_ref, gw_out_ref, vec_ref, b_in_ref, b_back_ref, small_ref = refs[len(offsets) :]
    rows = piece_refs[0].shape[0]
    for piece_ref, offset in zip(piece_refs, offsets):
        at = pl.ds(pl.multiple_of((place_ref[0] ^ offset) * rows, rows), rows)
        gw_qkv_ref[at, :] = piece_ref[:, 0 : 3 * width].astype(F32)
        gw_out_ref[at, :] = piece_ref[:, 3 * width : 4 * width].astype(F32)
        small_ref[at, :] = piece_ref[:, 4 * width :].astype(F32)
    vec_ref[...] = small_ref[0:8, :]
    row = 8
    for ref, length in ((b_in_ref, hidden), (b_back_ref, width)):
        for e in range(exp_dev):
            for at in range(0, length, 128):
                ref[e : e + 1, at : at + 128] = small_ref[row : row + 1, :]
                row += 1


def unpack_call(pieces, offsets, place, width, exp_dev, hidden):
    rows = pieces[0].shape[0] * len(pieces)
    shapes = [(rows, 3 * width), (rows, width), (8, 128), (exp_dev, hidden), (exp_dev, width)]
    return pl.pallas_call(
        functools.partial(unpack_kernel, width, exp_dev, hidden, offsets),
        in_specs=[pl.BlockSpec(memory_space=pltpu.SMEM)] + [pl.BlockSpec(memory_space=pltpu.VMEM)] * len(pieces),
        out_specs=[pl.BlockSpec(memory_space=pltpu.VMEM)] * len(shapes),
        out_shape=[jax.ShapeDtypeStruct(v, F32) for v in shapes],
        scratch_shapes=[pltpu.VMEM((rows, 128), F32)],
        compiler_params=params(),
        cost_estimate=cost(5),
        name="parameter_gradient_results",
    )(place, *pieces)


def after(arrays, *others):
    return lax.optimization_barrier((list(arrays), others))[0]


def local(
    tokens,
    routes,
    gates,
    ln1_gain,
    ln1_bias,
    w_qkv,
    w_out,
    out_bias,
    ln2_gain,
    ln2_bias,
    w_in,
    in_bias,
    w_back,
    back_bias,
    cotangent,
):
    images, seq_len, width = tokens.shape
    ep_size = lax.axis_size("ep")
    exp_dev = w_in.shape[0]
    experts = exp_dev * ep_size
    capacity = (images * seq_len * 10 + 4 * experts - 1) // (4 * experts)
    capp = -(-capacity // 8) * 8
    me = lax.axis_index("ep").astype(jnp.int32).reshape(1)
    vecs = jnp.stack([ln1_gain, ln1_bias, out_bias, ln2_gain, ln2_bias] + [jnp.zeros_like(ln1_gain)] * 3)

    grp_size = lax.axis_size("grp")
    grp = lax.axis_index("grp").astype(jnp.int32)
    bits = list(range(grp_size.bit_length() - 1))
    order_a, order_b = bits[1:], bits[:0:-1]
    blocks = grp_size // 2
    core = grp % 2
    block_a, block_b = digits(grp, order_a), digits(grp, order_b)
    half = ep_size // 2

    def over_ep(array, distance):
        return swap(array, "ep", ep_size, distance)

    cot_far = over_ep(cotangent, half)
    info, slot_col, gate_col, *g_all = route_call(me, routes, gates, cotangent, ep_size, exp_dev, capp)
    info_far = over_ep(info, half)
    g_all = [g_all[0]] + [over_ep(g_all[d], d) for d in range(1, half)]
    qkv, attended, lse, resid, *x_send = attention_call(tokens, w_qkv, w_out, vecs, info, ep_size, exp_dev, capp)
    x_all = [x_send[0]]
    for d in range(1, ep_size):
        send, = after([x_send[d]], *([cot_far] if d == half else [x_all[-1]] if d > half else []))
        x_all.append(over_ep(send, d))
    far = gateway_call(info_far, cot_far, ep_size, exp_dev, capp)
    g_all = g_all + [far[0]] + [over_ep(far[j], j) for j in range(1, half)]
    g_all[0], = after(g_all[:1], *far)
    b_in, b_back = in_bias[:, None, :], back_bias[:, None, :]
    place_e = jnp.stack([1 - core, block_a, block_b])
    steps = [list(range(half))] + [[d] for d in range(half, ep_size)]
    outs, gdis, gdis_back, sums, bias_sums = [], [], [], (), None
    for number, step in enumerate(steps):
        xs, gs = [x_all[d] for d in step], [g_all[d] for d in step]
        if number == len(steps) - 1:
            xs = after(xs, *gdis_back[:half])
        o, g, sums, sums_b = expert_call(xs, gs, w_in, w_back, b_in, b_back, place_e, blocks, tuple(sums), 4 + 6 * len(step))
        outs, gdis = outs + list(o), gdis + list(g)
        for d in step:
            send, = after([gdis[d]], *([x_all[-1]] if d >= half else []))
            gdis_back.append(over_ep(send, d) if d else send)
        bias_sums = sums_b if number == 0 else [a + b for a, b in zip(bias_sums, sums_b)]
    gb_in, gb_back = bias_sums[0][:, 0], bias_sums[1][:, 0]
    far_b, far_i, near_b, near_i = sums
    state = [near_b + swap(far_b, "grp", grp_size, 1), near_i + swap(far_i, "grp", grp_size, 1)]
    stages = [state]
    for step in range(len(order_a)):
        state = scatter_step(state, [order_a[step], order_b[step]], grp_size)
        stages.append(state)
    sum_b, sum_i = state
    resid_late, = after([resid], *stages[len(stages) // 2])
    all_b, all_i = gather_sums(sum_b, order_a, grp_size), gather_sums(sum_i, order_b, grp_size)
    oth_b = [swap(p, "grp", grp_size, 1) for p in all_b]
    oth_i = [swap(p, "grp", grp_size, 1) for p in all_i]
    gw_back = widen_call(all_b, oth_b, jnp.stack([core, block_a]), 0, w_back.shape)
    gw_in = widen_call(all_i, oth_i, jnp.stack([core, block_b]), 1, w_in.shape)
    hidden = w_in.shape[2]
    packed = width // ep_size == 128 and 128 % (16 * grp_size) == 0
    place, biases, pack_blocks = None, None, ()
    if packed:
        order_p, order_q = [0] + order_a, [0] + order_b
        pack_blocks = tuple(
            tuple(sum((r >> (len(o) - 1 - k)) % 2 << bit for k, bit in enumerate(o)) for r in range(grp_size))
            for o in (order_p, order_q)
        )
        place = jnp.stack([me[0], grp])
        biases = jnp.concatenate([gb_in.reshape(-1, 128), gb_back.reshape(-1, 128)])
    grad_tokens, *grads = backward_call(
        tokens, cotangent, resid_late, qkv, attended, lse, slot_col, w_qkv, w_out, vecs, gdis_back, place, biases, pack_blocks
    )
    outs_back = [outs[0]]
    for d in range(1, ep_size):
        send, = after([outs[d]], *gdis_back, *([outs_back[-1]] if d > half else []))
        outs_back.append(over_ep(send, d))
    output = combine_call(resid, slot_col, gate_col, outs_back)
    grads = after(grads, sum_b, sum_i, *outs_back[: half + 1])
    if packed:
        for bits_now in zip(order_p, order_q):
            grads = scatter_step(grads, bits_now, grp_size)
        near, far = after(grads, *outs_back)
        parts = [near[0, d] for d in range(ep_size // 2)] + [far[0, d] for d in range(ep_size // 2)]
        total = parts[0].astype(F32)
        for d in range(1, ep_size):
            total = total + over_ep(parts[d], d).astype(F32)
        pieces, offsets = [total.astype(BF16)], [0]
        for bit in reversed(bits):
            pieces = pieces + [swap(p, "grp", grp_size, 1 << bit) for p in pieces]
            offsets = offsets + [o ^ (1 << bit) for o in offsets]
        gw_qkv, gw_out, gvec, gb_in, gb_back = unpack_call(pieces, offsets, grp.reshape(1), width, exp_dev, hidden)
        gvec = [gvec[k] for k in range(5)]
    else:
        def over_grp(v):
            return lax.psum(v.astype(BF16), "grp").astype(F32)

        def over_all(v):
            return over_grp(lax.psum_scatter(v.astype(BF16), "ep", scatter_dimension=0, tiled=True))

        gw_qkv, gw_out, gvec = grads
        gw_qkv, gw_out, gb_in, gb_back = over_all(gw_qkv), over_all(gw_out), over_grp(gb_in), over_grp(gb_back)
        gvec = [over_all(gvec[k]) for k in range(5)]
    return (output, grad_tokens, gvec[0], gvec[1], gw_qkv, gw_out, gvec[2], gvec[3], gvec[4], gw_in, gb_in, gw_back, gb_back)


def solution(mesh):
    rows = P(("grp", "ep"), None, None)
    return jax.shard_map(
        local,
        mesh=mesh,
        in_specs=(rows, rows, rows)
        + (P(),) * 7
        + (P("ep", None, None), P("ep", None), P("ep", None, None), P("ep", None), rows),
        out_specs=(rows, rows)
        + (P("ep"), P("ep"), P("ep", None), P("ep", None), P("ep"), P("ep"), P("ep"))
        + (P("ep", None, None), P("ep", None), P("ep", None, None), P("ep", None)),
        check_vma=False,
    )
```

```python
import functools

import jax
import jax.numpy as jnp
from jax import lax
from jax.experimental import pallas as pl
from jax.experimental.pallas import tpu as pltpu
from jax.sharding import PartitionSpec as P

HD = 64
NORM_EPS = 1e-06
BF16 = jnp.bfloat16
F32 = jnp.float32
VMEM_LIMIT = 64 * 1024 * 1024
GELU_C = 0.7978845608028654


def cost(microseconds):
    return pl.CostEstimate(flops=int(microseconds * 10**9), bytes_accessed=2**12, transcendentals=0)


def dot_nn(a, b):
    return jnp.dot(a, b, preferred_element_type=F32)


def dot_nt(a, b):
    return lax.dot_general(a, b, (((1,), (1,)), ((), ())), preferred_element_type=F32)


def dot_tn(a, b):
    return lax.dot_general(a, b, (((0,), (0,)), ((), ())), preferred_element_type=F32)


def norm_parts(values):
    average = jnp.mean(values, axis=-1, keepdims=True)
    centred = values - average
    inv_std = lax.rsqrt(jnp.mean(centred * centred, axis=-1, keepdims=True) + NORM_EPS)
    return centred * inv_std, inv_std


def norm_back(grad_norm, normed, inv_std, gain):
    scaled = grad_norm * gain
    return inv_std * (
        scaled
        - jnp.mean(scaled, axis=-1, keepdims=True)
        - normed * jnp.mean(scaled * normed, axis=-1, keepdims=True)
    )


def whole(shape):
    zeros = (0,) * len(shape)
    return pl.BlockSpec(tuple(shape), lambda *_: zeros)


def params(*semantics):
    return pltpu.CompilerParams(
        dimension_semantics=semantics or None, vmem_limit_bytes=VMEM_LIMIT
    )


def dispatch_rows(place, slots, values, source_refs, e):
    total = None
    for i, source in enumerate(source_refs):
        value = 1.0 if values is None else values[i][e : e + 1, :]
        pick = jnp.where(place == slots[i][e : e + 1, :], value, 0.0).astype(BF16)
        part = dot_nn(pick, source[...])
        total = part if total is None else total + part
    return total.astype(BF16)


def slot_places(capp, seq):
    return lax.broadcasted_iota(jnp.int32, (capp, seq), 0).astype(F32)


def route_kernel(exp_dev, me_ref, routes_ref, gates_ref, cot_ref, info_ref, slot_col_ref, gate_col_ref, *rest):
    out_refs, scratch = rest[:-1], rest[-1]
    n_img, seq, width = cot_ref.shape
    experts = info_ref.shape[2]
    capp = out_refs[0].shape[1]
    me = me_ref[0]
    expert = lax.broadcasted_iota(jnp.int32, (experts, seq), 0)
    expert = ((expert // exp_dev) ^ me) * exp_dev + expert % exp_dev
    earlier = lax.broadcasted_iota(jnp.int32, (seq, seq), 0)
    later = lax.broadcasted_iota(jnp.int32, (seq, seq), 1)
    tri = jnp.where(earlier < later, 1.0, 0.0).astype(BF16)
    carry = jnp.zeros((experts, 1), F32)
    slots, gate_rows = [], []
    for i in range(n_img):
        hit0 = expert == routes_ref[i, 0:1, :]
        hit1 = expert == routes_ref[i, 1:2, :]
        member = jnp.where(hit0 | hit1, 1.0, 0.0)
        slot = jnp.where(member > 0.5, dot_nn(member.astype(BF16), tri) + carry, -1.0)
        gate = jnp.where(hit0, gates_ref[i, 0:1, :], jnp.where(hit1, gates_ref[i, 1:2, :], 0.0))
        carry = carry + jnp.sum(member, axis=1, keepdims=True)
        slots.append(slot)
        gate_rows.append(gate)
        info_ref[0, i] = slot
        info_ref[1, i] = gate
        scratch[0, 0:experts, 0:seq] = slot
        scratch[1, 0:experts, 0:seq] = gate
        slot_col_ref[i] = jnp.transpose(scratch[0])[:seq, :experts]
        gate_col_ref[i] = jnp.transpose(scratch[1])[:seq, :experts]
    place = slot_places(capp, seq)
    sources = [cot_ref.at[i] for i in range(n_img)]
    for e in range(len(out_refs) * exp_dev):
        out_refs[e // exp_dev][e % exp_dev] = dispatch_rows(place, slots, gate_rows, sources, e)


def route_call(me, routes, gates, cotangent, ep_size, exp_dev, capp):
    n_img, seq, width = cotangent.shape
    experts = ep_size * exp_dev
    seq_pad = -(-seq // 128) * 128
    chunk = jax.ShapeDtypeStruct((exp_dev, capp, width), BF16)
    return pl.pallas_call(
        functools.partial(route_kernel, exp_dev),
        in_specs=[pl.BlockSpec(memory_space=pltpu.SMEM)] + [pl.BlockSpec(memory_space=pltpu.VMEM)] * 3,
        out_specs=[pl.BlockSpec(memory_space=pltpu.VMEM)] * (3 + ep_size // 2),
        out_shape=[
            jax.ShapeDtypeStruct((2, n_img, experts, seq), F32),
            jax.ShapeDtypeStruct((n_img, seq, experts), F32),
            jax.ShapeDtypeStruct((n_img, seq, experts), F32),
        ]
        + [chunk] * (ep_size // 2),
        scratch_shapes=[pltpu.VMEM((2, 128, seq_pad), F32)],
        compiler_params=params(),
        cost_estimate=cost(4),
        name="route_and_dispatch_cotangent",
    )(me, routes.transpose(0, 2, 1), gates.transpose(0, 2, 1), cotangent)


def gateway_kernel(exp_dev, info_ref, cot_ref, *out_refs):
    n_img, seq, width = cot_ref.shape
    capp = out_refs[0].shape[1]
    place = slot_places(capp, seq)
    slots = [info_ref[0, i] for i in range(n_img)]
    gate_rows = [info_ref[1, i] for i in range(n_img)]
    sources = [cot_ref.at[i] for i in range(n_img)]
    half = len(out_refs)
    for j in range(half):
        for k in range(exp_dev):
            out_refs[j][k] = dispatch_rows(place, slots, gate_rows, sources, (half ^ j) * exp_dev + k)


def gateway_call(info, cotangent, ep_size, exp_dev, capp):
    chunk = jax.ShapeDtypeStruct((exp_dev, capp, cotangent.shape[2]), BF16)
    return pl.pallas_call(
        functools.partial(gateway_kernel, exp_dev),
        in_specs=[pl.BlockSpec(memory_space=pltpu.VMEM)] * 2,
        out_specs=[pl.BlockSpec(memory_space=pltpu.VMEM)] * (ep_size // 2),
        out_shape=[chunk] * (ep_size // 2),
        compiler_params=params(),
        cost_estimate=cost(3),
        name="dispatch_far_cotangent",
    )(info, cotangent)


def attention_kernel(
    heads, tok_ref, w_qkv_ref, w_out_ref, vec_ref, info_ref, qkv_ref, att_ref, lse_ref, resid_ref, *rest
):
    out_refs, second_ref = rest[:-1], rest[-1]
    img = pl.program_id(0)
    seq, width = tok_ref.shape[1:]
    exp_dev, capp = out_refs[0].shape[:2]
    inputs = tok_ref[0].astype(F32)
    norm_first, _ = norm_parts(inputs)
    first = (norm_first * vec_ref[0:1, :] + vec_ref[1:2, :]).astype(BF16)
    qkv = dot_nn(first, w_qkv_ref[...]).astype(BF16)
    qkv_ref[0] = qkv
    low = lax.broadcasted_iota(jnp.int32, (seq, 2 * HD), 1) < HD
    nothing = jnp.zeros((seq, 2 * HD), BF16)
    lane = lax.broadcasted_iota(jnp.int32, (seq, 128), 1)
    lse_all = jnp.zeros((seq, 128), F32)
    pieces = []
    for pair in range(heads // 2):
        at = pair * 2 * HD
        query = qkv[:, at : at + 2 * HD] * jnp.asarray(HD ** (-0.5), BF16)
        key = qkv[:, width + at : width + at + 2 * HD]
        value = qkv[:, 2 * width + at : 2 * width + at + 2 * HD]
        halves = []
        for half in range(2):
            mine = low if half == 0 else jnp.logical_not(low)
            scores = dot_nt(jnp.where(mine, query, nothing), key)
            top = jnp.max(scores, axis=-1, keepdims=True)
            weight = jnp.exp(scores - top)
            total = jnp.sum(weight, axis=-1, keepdims=True)
            prob = (weight * (1.0 / total)).astype(BF16)
            halves.append(dot_nn(prob, value))
            lse_all = jnp.where(lane == 2 * pair + half, top + jnp.log(total), lse_all)
        pieces.append(jnp.where(low, halves[0], halves[1]).astype(BF16))
    lse_ref[0] = lse_all
    attended = jnp.concatenate(pieces, axis=1)
    att_ref[0] = attended
    resid = inputs + dot_nn(attended, w_out_ref[...]) + vec_ref[2:3, :]
    resid_ref[0] = resid
    norm_second, _ = norm_parts(resid)
    second_ref[img] = (norm_second * vec_ref[3:4, :] + vec_ref[4:5, :]).astype(BF16)

    @pl.when(img == pl.num_programs(0) - 1)
    def _():
        n_img = second_ref.shape[0]
        place = slot_places(capp, seq)
        slots = [info_ref[0, i] for i in range(n_img)]
        sources = [second_ref.at[i] for i in range(n_img)]
        for e in range(len(out_refs) * exp_dev):
            out_refs[e // exp_dev][e % exp_dev] = dispatch_rows(place, slots, None, sources, e)


def attention_call(tokens, w_qkv, w_out, vecs, info, ep_size, exp_dev, capp):
    n_img, seq, width = tokens.shape
    chunk = jax.ShapeDtypeStruct((exp_dev, capp, width), BF16)
    image = lambda *tail: pl.BlockSpec((1,) + tail, lambda i: (i, 0, 0))
    return pl.pallas_call(
        functools.partial(attention_kernel, width // HD),
        grid=(n_img,),
        in_specs=[image(seq, width), whole(w_qkv.shape), whole(w_out.shape), whole(vecs.shape), whole(info.shape)],
        out_specs=[image(seq, 3 * width), image(seq, width), image(seq, 128), image(seq, width)]
        + [whole(chunk.shape)] * ep_size,
        out_shape=[
            jax.ShapeDtypeStruct((n_img, seq, 3 * width), BF16),
            jax.ShapeDtypeStruct((n_img, seq, width), BF16),
            jax.ShapeDtypeStruct((n_img, seq, 128), F32),
            jax.ShapeDtypeStruct((n_img, seq, width), F32),
        ]
        + [chunk] * ep_size,
        scratch_shapes=[pltpu.VMEM((n_img, seq, width), BF16)],
        compiler_params=params("arbitrary"),
        cost_estimate=cost(14),
        name="attention_forward_and_dispatch",
    )(tokens, w_qkv, w_out, vecs, info)


def expert_kernel(count, carried, blocks, tile, sel_ref, *refs):
    x_refs, g_refs = refs[:count], refs[count : 2 * count]
    w_in_hbm, w_back_hbm, b_in_ref, b_back_ref = refs[2 * count : 2 * count + 4]
    before = refs[2 * count + 4 : 2 * count + 4 + carried]
    outs = refs[2 * count + 4 + carried :]
    out_refs, gdis_refs = outs[:count], outs[count : 2 * count]
    sums, (gb_in_ref, gb_back_ref) = outs[2 * count : 2 * count + 4], outs[2 * count + 4 : 2 * count + 6]
    w_in_buf, w_back_buf, back_buf, in_buf, acc_out, acc_dis, load_sem, sum_sem, store_sem = outs[2 * count + 6 :]
    exp_dev, _, hidden = w_in_buf.shape
    block = hidden // blocks
    steps = [(l, t) for l in range(exp_dev) for t in range(hidden // tile)]

    def loads(l, t):
        e = sel_ref[0] ^ l
        span = pl.ds(t * tile, tile)
        return [
            pltpu.make_async_copy(w_in_hbm.at[e, :, span], w_in_buf.at[l, :, span], load_sem.at[l, t, 0]),
            pltpu.make_async_copy(w_back_hbm.at[e, span, :], w_back_buf.at[l, span, :], load_sem.at[l, t, 1]),
        ]

    def blocks_of(t):
        return range(t * tile // block, (t + 1) * tile // block)

    def sum_loads(l, t):
        return [
            copy
            for b in blocks_of(t)
            for copy in (
                pltpu.make_async_copy(before[2 * l].at[b ^ sel_ref[1]], back_buf.at[l, b], sum_sem.at[l, b, 0]),
                pltpu.make_async_copy(before[2 * l + 1].at[b ^ sel_ref[2]], in_buf.at[l, b], sum_sem.at[l, b, 1]),
            )
        ]

    def stores(l, t):
        return [
            copy
            for b in blocks_of(t)
            for copy in (
                pltpu.make_async_copy(back_buf.at[l, b], sums[2 * l].at[b ^ sel_ref[1]], store_sem.at[l, b, 0]),
                pltpu.make_async_copy(in_buf.at[l, b], sums[2 * l + 1].at[b ^ sel_ref[2]], store_sem.at[l, b, 1]),
            )
        ]

    for l, t in steps:
        for copy in loads(l, t):
            copy.start()
    if carried:
        for l, t in steps:
            for copy in sum_loads(l, t):
                copy.start()
    for l, t in steps:
        e = sel_ref[0] ^ l
        span = slice(t * tile, (t + 1) * tile)
        for copy in loads(l, t):
            copy.wait()
        w_in, w_back = w_in_buf[l, :, span], w_back_buf[l, span, :]
        gw_back = gw_in = gb_in = None
        for n in range(count):
            x, g = x_refs[n][e], g_refs[n][e]
            pre = dot_nn(x, w_in) + b_in_ref[e, :, span]
            square = pre * pre
            bent = jnp.tanh(pre * (GELU_C + (GELU_C * 0.044715) * square))
            half = 0.5 + 0.5 * bent
            value = pre * half
            act = value.astype(BF16)
            slope = half + (value - value * half) * (2 * GELU_C + (6 * GELU_C * 0.044715) * square)
            gpre = (dot_nt(g, w_back) * slope).astype(BF16)
            part_dis, part_out = dot_nt(gpre, w_in), dot_nn(act, w_back)
            if t == 0:
                part_out = part_out + b_back_ref[e]
            else:
                part_dis, part_out = part_dis + acc_dis[n], part_out + acc_out[n]
            if span.stop == hidden:
                gdis_refs[n][e] = part_dis.astype(BF16)
                out_refs[n][e] = part_out.astype(BF16)
            else:
                acc_dis[n] = part_dis
                acc_out[n] = part_out
            one = (dot_tn(act, g), dot_tn(x, gpre), jnp.sum(gpre.astype(F32), axis=0, keepdims=True))
            gw_back = one[0] if n == 0 else gw_back + one[0]
            gw_in = one[1] if n == 0 else gw_in + one[1]
            gb_in = one[2] if n == 0 else gb_in + one[2]
        gb_in_ref[e, :, span] = gb_in
        if carried:
            for copy in sum_loads(l, t):
                copy.wait()
        for b in blocks_of(t):
            at = slice(b * block - t * tile, (b + 1) * block - t * tile)
            back, into = gw_back[at, :], gw_in[:, at]
            if carried:
                back, into = back + back_buf[l, b].astype(F32), into + in_buf[l, b].astype(F32)
            back_buf[l, b] = back.astype(BF16)
            in_buf[l, b] = into.astype(BF16)
        for copy in stores(l, t):
            copy.start()
    for e in range(exp_dev):
        total = jnp.sum(g_refs[0][e].astype(F32), axis=0, keepdims=True)
        for n in range(1, count):
            total = total + jnp.sum(g_refs[n][e].astype(F32), axis=0, keepdims=True)
        gb_back_ref[e] = total
    for l, t in steps:
        for copy in stores(l, t):
            copy.wait()


def expert_call(xs, gs, w_in, w_back, b_in, b_back, place, blocks, before, microseconds):
    count = len(xs)
    exp_dev, capp, width = xs[0].shape
    hidden = w_in.shape[2]
    block = hidden // blocks
    tile = max(block, min(hidden, 512))
    narrow = jax.ShapeDtypeStruct((exp_dev, capp, width), BF16)
    shapes = [jax.ShapeDtypeStruct((blocks, block, width), BF16), jax.ShapeDtypeStruct((blocks, width, block), BF16)] * 2
    held = pl.BlockSpec(memory_space=pltpu.VMEM)
    remote = pl.BlockSpec(memory_space=pl.ANY)
    res = pl.pallas_call(
        functools.partial(expert_kernel, count, len(before), blocks, tile),
        in_specs=[pl.BlockSpec(memory_space=pltpu.SMEM)]
        + [held] * (2 * count)
        + [remote] * 2
        + [held] * 2
        + [remote] * len(before),
        out_specs=[held] * (2 * count) + [remote] * 4 + [held] * 2,
        out_shape=[narrow] * (2 * count)
        + shapes
        + [jax.ShapeDtypeStruct((exp_dev, 1, hidden), F32), jax.ShapeDtypeStruct((exp_dev, 1, width), F32)],
        scratch_shapes=[
            pltpu.VMEM((exp_dev, width, hidden), BF16),
            pltpu.VMEM((exp_dev, hidden, width), BF16),
            pltpu.VMEM((exp_dev, blocks, block, width), BF16),
            pltpu.VMEM((exp_dev, blocks, width, block), BF16),
            pltpu.VMEM((count, capp, width), F32),
            pltpu.VMEM((count, capp, width), F32),
            pltpu.SemaphoreType.DMA((exp_dev, blocks, 2)),
            pltpu.SemaphoreType.DMA((exp_dev, blocks, 2)),
            pltpu.SemaphoreType.DMA((exp_dev, blocks, 2)),
        ],
        compiler_params=params(),
        cost_estimate=cost(microseconds),
        name="experts",
    )(place, *xs, *gs, w_in, w_back, b_in, b_back, *before)
    return res[:count], res[count : 2 * count], res[2 * count : 2 * count + 4], res[2 * count + 4 :]


def gather_rows(slot_col, value_col, chunk_refs, capp):
    seq = slot_col.shape[0]
    exp_dev = chunk_refs[0].shape[0]
    place = lax.broadcasted_iota(jnp.int32, (seq, capp), 1).astype(F32)
    total = None
    for e in range(len(chunk_refs) * exp_dev):
        value = 1.0 if value_col is None else value_col[:, e : e + 1]
        pick = jnp.where(place == slot_col[:, e : e + 1], value, 0.0).astype(BF16)
        part = dot_nn(pick, chunk_refs[e // exp_dev][e % exp_dev])
        total = part if total is None else total + part
    return total


def backward_kernel(
    heads, ep_size, pack_blocks, place_ref, bias_ref, tok_ref, cot_ref, resid_ref, qkv_ref, att_ref, lse_ref, slot_col_ref, w_qkv_ref, w_out_ref, vec_ref, *rest
):
    chunk_refs = rest[:ep_size]
    packed = len(pack_blocks)
    gtok_ref = rest[ep_size]
    pack_refs = rest[ep_size + 1 : ep_size + 1 + packed]
    gw_qkv_ref, gw_out_ref, gvec_ref, gqkv_ref = rest[ep_size + 1 + packed : ep_size + 5 + packed]
    img = pl.program_id(0)
    seq, width = tok_ref.shape[1:]
    capp = chunk_refs[0].shape[1]
    grad_second = gather_rows(slot_col_ref[0], None, chunk_refs, capp)
    norm_second, inv_second = norm_parts(resid_ref[0])
    grad_resid = cot_ref[0].astype(F32) + norm_back(grad_second, norm_second, inv_second, vec_ref[3:4, :])
    grad_branch = grad_resid.astype(BF16)
    grad_att = dot_nt(grad_branch, w_out_ref[...]).astype(BF16)
    gw_out = dot_tn(att_ref[0], grad_branch)
    low = lax.broadcasted_iota(jnp.int32, (seq, 2 * HD), 1) < HD
    nothing = jnp.zeros((seq, 2 * HD), BF16)
    scale = jnp.asarray(HD ** (-0.5), BF16)
    for pair in range(heads // 2):
        at = pair * 2 * HD
        query = qkv_ref[0, :, at : at + 2 * HD] * scale
        key = qkv_ref[0, :, width + at : width + at + 2 * HD]
        value = qkv_ref[0, :, 2 * width + at : 2 * width + at + 2 * HD]
        gatt = grad_att[:, at : at + 2 * HD]
        grad_q = grad_k = grad_v = None
        for half in range(2):
            mine = low if half == 0 else jnp.logical_not(low)
            head = 2 * pair + half
            query_h = jnp.where(mine, query, nothing)
            gatt_h = jnp.where(mine, gatt, nothing)
            key_h = jnp.where(mine, key, nothing) * scale
            prob = jnp.exp(dot_nt(query_h, key) - lse_ref[0, :, head : head + 1])
            grad_prob = dot_nt(gatt_h, value)
            mean = jnp.sum(grad_prob * prob, axis=-1, keepdims=True)
            grad_scores = (prob * (grad_prob - mean)).astype(BF16)
            part_v = dot_tn(prob.astype(BF16), gatt_h)
            part_q = dot_nn(grad_scores, key_h)
            part_k = dot_tn(grad_scores, query_h)
            grad_q = part_q if grad_q is None else grad_q + part_q
            grad_k = part_k if grad_k is None else grad_k + part_k
            grad_v = part_v if grad_v is None else grad_v + part_v
        gqkv_ref[:, at : at + 2 * HD] = grad_q.astype(BF16)
        gqkv_ref[:, width + at : width + at + 2 * HD] = grad_k.astype(BF16)
        gqkv_ref[:, 2 * width + at : 2 * width + at + 2 * HD] = grad_v.astype(BF16)
    grad_qkv = gqkv_ref[...]
    norm_first, inv_first = norm_parts(tok_ref[0].astype(F32))
    first = (norm_first * vec_ref[0:1, :] + vec_ref[1:2, :]).astype(BF16)
    gw_qkv = dot_tn(first, grad_qkv)
    grad_first = dot_nt(grad_qkv, w_qkv_ref[...])
    gtok_ref[0] = (grad_resid + norm_back(grad_first, norm_first, inv_first, vec_ref[0:1, :])).astype(BF16)
    sums = [
        grad_first * norm_first,
        grad_first,
        grad_branch.astype(F32),
        grad_second * norm_second,
        grad_second,
    ]
    gvec = jnp.concatenate([jnp.sum(v, axis=0, keepdims=True) for v in sums] + [jnp.zeros((3, width), F32)], axis=0)

    @pl.when(img == 0)
    def _():
        gw_out_ref[...] = gw_out
        gw_qkv_ref[...] = gw_qkv
        gvec_ref[...] = gvec

    @pl.when(img > 0)
    def _():
        gw_out_ref[...] += gw_out
        gw_qkv_ref[...] += gw_qkv
        gvec_ref[...] += gvec

    if not packed:
        return

    @pl.when(img == pl.num_programs(0) - 1)
    def _():
        small_ref = rest[-1]
        blocks, per_pack, rows = pack_refs[0].shape[:3]
        per_ep = width // ep_size
        biases = bias_ref.shape[0]
        small_ref[...] = jnp.zeros(small_ref.shape, F32)
        for j in range(ep_size):
            owner = place_ref[0] ^ j
            small_ref[0:8, :] = gvec_ref[:, pl.ds(pl.multiple_of(owner * per_ep, per_ep), per_ep)]
            small_ref[8 : 8 + biases, :] = bias_ref[...] if j == 0 else jnp.zeros(bias_ref.shape, F32)
            for r in range(blocks):
                block = pack_blocks[j // per_pack][r] ^ place_ref[1]
                start = pl.multiple_of(owner * per_ep + block * rows, rows)
                into = pack_refs[j // per_pack]
                into[r, j % per_pack, :, 0 : 3 * width] = gw_qkv_ref[pl.ds(start, rows), :].astype(BF16)
                into[r, j % per_pack, :, 3 * width : 4 * width] = gw_out_ref[pl.ds(start, rows), :].astype(BF16)
                small = small_ref[pl.ds(pl.multiple_of(block * rows, rows), rows), :]
                into[r, j % per_pack, :, 4 * width :] = small.astype(BF16)


def backward_call(tokens, cotangent, resid, qkv, attended, lse, slot_col, w_qkv, w_out, vecs, chunks, place, biases, pack_blocks):
    n_img, seq, width = tokens.shape
    ep_size = len(chunks)
    packed = len(pack_blocks)
    image = lambda arr: pl.BlockSpec((1,) + arr.shape[1:], lambda i: (i, 0, 0))
    sums = [
        jax.ShapeDtypeStruct(w_qkv.shape, F32),
        jax.ShapeDtypeStruct(w_out.shape, F32),
        jax.ShapeDtypeStruct((8, width), F32),
    ]
    scratch = [pltpu.VMEM((seq, 3 * width), BF16)]
    if packed:
        grp_size = len(pack_blocks[0])
        pack = (grp_size, ep_size // 2, width // (ep_size * grp_size), 4 * width + 128)
        outs = [jax.ShapeDtypeStruct(pack, BF16)] * 2
        scratch = [pltpu.VMEM(v.shape, F32) for v in sums] + scratch + [pltpu.VMEM((width // ep_size, 128), F32)]
    else:
        outs = sums
        place, biases = jnp.zeros((2,), jnp.int32), jnp.zeros((8, 128), F32)
    return pl.pallas_call(
        functools.partial(backward_kernel, width // HD, ep_size, pack_blocks),
        grid=(n_img,),
        in_specs=[pl.BlockSpec(memory_space=pltpu.SMEM), whole(biases.shape)]
        + [image(a) for a in (tokens, cotangent, resid, qkv, attended, lse, slot_col)]
        + [whole(a.shape) for a in (w_qkv, w_out, vecs, *chunks)],
        out_specs=[image(tokens)] + [whole(v.shape) for v in outs],
        out_shape=[jax.ShapeDtypeStruct(tokens.shape, BF16)] + outs,
        scratch_shapes=scratch,
        compiler_params=params("arbitrary"),
        cost_estimate=cost(25),
        name="attention_backward",
    )(place, biases, tokens, cotangent, resid, qkv, attended, lse, slot_col, w_qkv, w_out, vecs, *chunks)


def combine_kernel(ep_size, resid_ref, slot_col_ref, gate_col_ref, *rest):
    chunk_refs, out_ref = rest[:ep_size], rest[ep_size]
    mixed = gather_rows(slot_col_ref[0], gate_col_ref[0], chunk_refs, chunk_refs[0].shape[1])
    out_ref[0] = (resid_ref[0] + mixed).astype(BF16)


def combine_call(resid, slot_col, gate_col, chunks):
    n_img, seq, width = resid.shape
    image = lambda arr: pl.BlockSpec((1,) + arr.shape[1:], lambda i: (i, 0, 0))
    return pl.pallas_call(
        functools.partial(combine_kernel, len(chunks)),
        grid=(n_img,),
        in_specs=[image(a) for a in (resid, slot_col, gate_col)] + [whole(c.shape) for c in chunks],
        out_specs=image(resid),
        out_shape=jax.ShapeDtypeStruct(resid.shape, BF16),
        compiler_params=params("arbitrary"),
        cost_estimate=cost(5),
        name="combine_output",
    )(resid, slot_col, gate_col, *chunks)


def swap(array, axis, size, distance):
    return lax.ppermute(array, axis, [(i, i ^ distance) for i in range(size)])


def digits(index, bits):
    number = jnp.zeros((), jnp.int32)
    for bit in bits:
        number = number * 2 + (index >> bit) % 2
    return number


def scatter_step(arrays, bits, size):
    halves = [a.shape[0] // 2 for a in arrays]
    came = [swap(a[h:], "grp", size, 1 << bit) for a, h, bit in zip(arrays, halves, bits)]
    return [a[:h] + c for a, h, c in zip(arrays, halves, came)]


def gather_sums(block, order, size):
    pieces = [block]
    for bit in reversed(order):
        pieces = pieces + [swap(p, "grp", size, 1 << bit) for p in pieces]
    return pieces


def widen_kernel(count, place_ref, *refs):
    piece_refs, out_ref = refs[:count], refs[-1]
    for r in range(count):
        @pl.when(pl.program_id(0) == r)
        def _():
            out_ref[0] = piece_refs[r][0].astype(F32)


def widen_call(pieces, expert, first, axis, shape, base):
    count = len(pieces)
    _, m, n = pieces[0].shape
    at = (lambda r, s: (s[0], r ^ s[1], 0)) if axis == 0 else (lambda r, s: (s[0], 0, r ^ s[1]))
    extra = [] if base is None else [base]
    return pl.pallas_call(
        functools.partial(widen_kernel, count),
        grid_spec=pltpu.PrefetchScalarGridSpec(
            num_scalar_prefetch=1,
            grid=(count,),
            in_specs=[pl.BlockSpec((1, m, n), lambda r, s: (0, 0, 0))] * count
            + [pl.BlockSpec(memory_space=pl.ANY)] * len(extra),
            out_specs=pl.BlockSpec((1, m, n), at),
        ),
        out_shape=jax.ShapeDtypeStruct(shape, F32),
        input_output_aliases={1 + count: 0} if extra else {},
        compiler_params=params("arbitrary"),
        cost_estimate=cost(4),
        name="expert_gradient_result",
    )(jnp.stack([expert, first]), *pieces, *extra)


def unpack_kernel(width, exp_dev, hidden, offsets, place_ref, *refs):
    piece_refs = refs[: len(offsets)]
    gw_qkv_ref, gw_out_ref, vec_ref, b_in_ref, b_back_ref, small_ref = refs[len(offsets) :]
    rows = piece_refs[0].shape[0]
    for piece_ref, offset in zip(piece_refs, offsets):
        at = pl.ds(pl.multiple_of((place_ref[0] ^ offset) * rows, rows), rows)
        gw_qkv_ref[at, :] = piece_ref[:, 0 : 3 * width].astype(F32)
        gw_out_ref[at, :] = piece_ref[:, 3 * width : 4 * width].astype(F32)
        small_ref[at, :] = piece_ref[:, 4 * width :].astype(F32)
    vec_ref[...] = small_ref[0:8, :]
    row = 8
    for ref, length in ((b_in_ref, hidden), (b_back_ref, width)):
        for e in range(exp_dev):
            for at in range(0, length, 128):
                ref[e : e + 1, at : at + 128] = small_ref[row : row + 1, :]
                row += 1


def unpack_call(pieces, offsets, place, width, exp_dev, hidden):
    rows = pieces[0].shape[0] * len(pieces)
    shapes = [(rows, 3 * width), (rows, width), (8, 128), (exp_dev, hidden), (exp_dev, width)]
    return pl.pallas_call(
        functools.partial(unpack_kernel, width, exp_dev, hidden, offsets),
        in_specs=[pl.BlockSpec(memory_space=pltpu.SMEM)] + [pl.BlockSpec(memory_space=pltpu.VMEM)] * len(pieces),
        out_specs=[pl.BlockSpec(memory_space=pltpu.VMEM)] * len(shapes),
        out_shape=[jax.ShapeDtypeStruct(v, F32) for v in shapes],
        scratch_shapes=[pltpu.VMEM((rows, 128), F32)],
        compiler_params=params(),
        cost_estimate=cost(5),
        name="parameter_gradient_results",
    )(place, *pieces)


def after(arrays, *others):
    return lax.optimization_barrier((list(arrays), others))[0]


def local(
    tokens,
    routes,
    gates,
    ln1_gain,
    ln1_bias,
    w_qkv,
    w_out,
    out_bias,
    ln2_gain,
    ln2_bias,
    w_in,
    in_bias,
    w_back,
    back_bias,
    cotangent,
):
    images, seq_len, width = tokens.shape
    ep_size = lax.axis_size("ep")
    exp_dev = w_in.shape[0]
    experts = exp_dev * ep_size
    capacity = (images * seq_len * 10 + 4 * experts - 1) // (4 * experts)
    capp = -(-capacity // 8) * 8
    me = lax.axis_index("ep").astype(jnp.int32).reshape(1)
    vecs = jnp.stack([ln1_gain, ln1_bias, out_bias, ln2_gain, ln2_bias] + [jnp.zeros_like(ln1_gain)] * 3)

    grp_size = lax.axis_size("grp")
    grp = lax.axis_index("grp").astype(jnp.int32)
    bits = list(range(grp_size.bit_length() - 1))
    order_a, order_b = bits[1:], bits[:0:-1]
    blocks = grp_size // 2
    core = grp % 2
    block_a, block_b = digits(grp, order_a), digits(grp, order_b)
    half = ep_size // 2

    def over_ep(array, distance):
        return swap(array, "ep", ep_size, distance)

    cot_far = over_ep(cotangent, half)
    info, slot_col, gate_col, *g_all = route_call(me, routes, gates, cotangent, ep_size, exp_dev, capp)
    info_far = over_ep(info, half)
    g_all = [g_all[0]] + [over_ep(g_all[d], d) for d in range(1, half)]
    qkv, attended, lse, resid, *x_send = attention_call(tokens, w_qkv, w_out, vecs, info, ep_size, exp_dev, capp)
    b_in, b_back = in_bias[:, None, :], back_bias[:, None, :]
    place_e = jnp.stack([1 - core, block_a, block_b])
    x_all = [x_send[0]] + [over_ep(x_send[d], d) for d in range(1, half + 1)]
    groups = [[0], list(range(1, half + 1))] + [[d] for d in range(half + 1, ep_size)]
    outs, gdis, gdis_back, sums, bias_sums = [], [], [], (), None
    for number, group in enumerate(groups):
        if number == 1:
            info_far, = after([info_far], sums[0])
            far = gateway_call(info_far, cot_far, ep_size, exp_dev, capp)
            g_all = g_all + [far[0]] + [over_ep(far[j], j) for j in range(1, half)]
            for d in range(half + 1, ep_size):
                send, = after([x_send[d]], *far, *x_all[1:d])
                x_all.append(over_ep(send, d))
        xs, gs = [x_all[d] for d in group], [g_all[d] for d in group]
        if number == 0:
            xs = after(xs, *g_all[1:])
        o, g, sums, sums_b = expert_call(xs, gs, w_in, w_back, b_in, b_back, place_e, blocks, tuple(sums), 10 * len(group))
        outs, gdis = outs + list(o), gdis + list(g)
        for d in group:
            send, = after([gdis[d]], *([x_all[-1]] if d >= half else []))
            gdis_back.append(over_ep(send, d) if d else send)
        bias_sums = sums_b if number == 0 else [a + b for a, b in zip(bias_sums, sums_b)]
    gb_in, gb_back = bias_sums[0][:, 0], bias_sums[1][:, 0]
    far_b, far_i, near_b, near_i = sums
    far_i, = after([far_i], gdis_back[half])
    state = [near_b + swap(far_b, "grp", grp_size, 1), near_i + swap(far_i, "grp", grp_size, 1)]
    stages = [state]
    for step in range(len(order_a)):
        state = scatter_step(state, [order_a[step], order_b[step]], grp_size)
        stages.append(state)
    sum_b, sum_i = state
    early = stages[len(stages) // 2]
    resid_late, = after([resid], *early)
    all_b, all_i = gather_sums(sum_b, order_a, grp_size), gather_sums(sum_i, order_b, grp_size)
    oth_b = [swap(p, "grp", grp_size, 1) for p in all_b]
    oth_i = [swap(p, "grp", grp_size, 1) for p in all_i]
    gw_back = widen_call(all_b, core, block_a, 0, w_back.shape, None)
    gw_in = widen_call(all_i, core, block_b, 1, w_in.shape, None)
    gw_back = widen_call(oth_b, 1 - core, block_a, 0, w_back.shape, gw_back)
    gw_in = widen_call(oth_i, 1 - core, block_b, 1, w_in.shape, gw_in)
    hidden = w_in.shape[2]
    packed = width // ep_size == 128 and 128 % (16 * grp_size) == 0
    place, biases, pack_blocks = None, None, ()
    if packed:
        order_p, order_q = [0] + order_a, [0] + order_b
        pack_blocks = tuple(
            tuple(sum((r >> (len(o) - 1 - k)) % 2 << bit for k, bit in enumerate(o)) for r in range(grp_size))
            for o in (order_p, order_q)
        )
        place = jnp.stack([me[0], grp])
        biases = jnp.concatenate([gb_in.reshape(-1, 128), gb_back.reshape(-1, 128)])
    grad_tokens, *grads = backward_call(
        tokens, cotangent, resid_late, qkv, attended, lse, slot_col, w_qkv, w_out, vecs, gdis_back, place, biases, pack_blocks
    )
    outs_back = [outs[0]]
    for d in range(1, ep_size):
        send, = after([outs[d]], *early, *gdis_back, *([outs_back[-1]] if d > half else []))
        outs_back.append(over_ep(send, d))
    output = combine_call(resid, slot_col, gate_col, outs_back)
    grads = after(grads, sum_b, sum_i, *outs_back[: half + 1])
    if packed:
        for bits_now in zip(order_p, order_q):
            grads = scatter_step(grads, bits_now, grp_size)
        near, far = after(grads, *outs_back)
        parts = [near[0, d] for d in range(ep_size // 2)] + [far[0, d] for d in range(ep_size // 2)]
        total = parts[0].astype(F32)
        for d in range(1, ep_size):
            total = total + over_ep(parts[d], d).astype(F32)
        pieces, offsets = [total.astype(BF16)], [0]
        for bit in reversed(bits):
            pieces = pieces + [swap(p, "grp", grp_size, 1 << bit) for p in pieces]
            offsets = offsets + [o ^ (1 << bit) for o in offsets]
        gw_qkv, gw_out, gvec, gb_in, gb_back = unpack_call(pieces, offsets, grp.reshape(1), width, exp_dev, hidden)
        gvec = [gvec[k] for k in range(5)]
    else:
        def over_grp(v):
            return lax.psum(v.astype(BF16), "grp").astype(F32)

        def over_all(v):
            return over_grp(lax.psum_scatter(v.astype(BF16), "ep", scatter_dimension=0, tiled=True))

        gw_qkv, gw_out, gvec = grads
        gw_qkv, gw_out, gb_in, gb_back = over_all(gw_qkv), over_all(gw_out), over_grp(gb_in), over_grp(gb_back)
        gvec = [over_all(gvec[k]) for k in range(5)]
    return (output, grad_tokens, gvec[0], gvec[1], gw_qkv, gw_out, gvec[2], gvec[3], gvec[4], gw_in, gb_in, gw_back, gb_back)


def solution(mesh):
    rows = P(("grp", "ep"), None, None)
    return jax.shard_map(
        local,
        mesh=mesh,
        in_specs=(rows, rows, rows)
        + (P(),) * 7
        + (P("ep", None, None), P("ep", None), P("ep", None, None), P("ep", None), rows),
        out_specs=(rows, rows)
        + (P("ep"), P("ep"), P("ep", None), P("ep", None), P("ep"), P("ep"), P("ep"))
        + (P("ep", None, None), P("ep", None), P("ep", None, None), P("ep", None)),
        check_vma=False,
    )
```

```python
import functools

import jax
import jax.numpy as jnp
from jax import lax
from jax.experimental import pallas as pl
from jax.experimental.pallas import tpu as pltpu
from jax.sharding import PartitionSpec as P

HD = 64
NORM_EPS = 1e-06
BF16 = jnp.bfloat16
F32 = jnp.float32
MIB = 1024 * 1024
GELU_C = 0.7978845608028654


def cost(microseconds):
    return pl.CostEstimate(flops=int(microseconds * 10**9), bytes_accessed=2**12, transcendentals=0)


def dot_nn(a, b):
    return jnp.dot(a, b, preferred_element_type=F32)


def dot_nt(a, b):
    return lax.dot_general(a, b, (((1,), (1,)), ((), ())), preferred_element_type=F32)


def dot_tn(a, b):
    return lax.dot_general(a, b, (((0,), (0,)), ((), ())), preferred_element_type=F32)


def norm_parts(values):
    average = jnp.mean(values, axis=-1, keepdims=True)
    centred = values - average
    inv_std = lax.rsqrt(jnp.mean(centred * centred, axis=-1, keepdims=True) + NORM_EPS)
    return centred * inv_std, inv_std


def norm_back(grad_norm, normed, inv_std, gain):
    scaled = grad_norm * gain
    return inv_std * (
        scaled
        - jnp.mean(scaled, axis=-1, keepdims=True)
        - normed * jnp.mean(scaled * normed, axis=-1, keepdims=True)
    )


def whole(shape):
    zeros = (0,) * len(shape)
    return pl.BlockSpec(tuple(shape), lambda *_: zeros)


def params(mebibytes, *semantics):
    return pltpu.CompilerParams(dimension_semantics=semantics or None, vmem_limit_bytes=mebibytes * MIB)


def dispatch_rows(place, slots, values, source_refs, e):
    total = None
    for i, source in enumerate(source_refs):
        value = 1.0 if values is None else values[i][e : e + 1, :]
        pick = jnp.where(place == slots[i][e : e + 1, :], value, 0.0).astype(BF16)
        part = dot_nn(pick, source[...])
        total = part if total is None else total + part
    return total.astype(BF16)


def slot_places(capp, seq):
    return lax.broadcasted_iota(jnp.int32, (capp, seq), 0).astype(F32)


def route_kernel(exp_dev, me_ref, routes_ref, gates_ref, cot_ref, info_ref, slot_col_ref, gate_col_ref, *rest):
    out_refs, scratch = rest[:-1], rest[-1]
    n_img, seq, width = cot_ref.shape
    experts = info_ref.shape[2]
    capp = out_refs[0].shape[1]
    me = me_ref[0]
    expert = lax.broadcasted_iota(jnp.int32, (experts, seq), 0)
    expert = ((expert // exp_dev) ^ me) * exp_dev + expert % exp_dev
    earlier = lax.broadcasted_iota(jnp.int32, (seq, seq), 0)
    later = lax.broadcasted_iota(jnp.int32, (seq, seq), 1)
    tri = jnp.where(earlier < later, 1.0, 0.0).astype(BF16)
    carry = jnp.zeros((experts, 1), F32)
    slots, gate_rows = [], []
    for i in range(n_img):
        hit0 = expert == routes_ref[i, 0:1, :]
        hit1 = expert == routes_ref[i, 1:2, :]
        member = jnp.where(hit0 | hit1, 1.0, 0.0)
        slot = jnp.where(member > 0.5, dot_nn(member.astype(BF16), tri) + carry, -1.0)
        gate = jnp.where(hit0, gates_ref[i, 0:1, :], jnp.where(hit1, gates_ref[i, 1:2, :], 0.0))
        carry = carry + jnp.sum(member, axis=1, keepdims=True)
        slots.append(slot)
        gate_rows.append(gate)
        info_ref[0, i] = slot
        info_ref[1, i] = gate
        scratch[0, 0:experts, 0:seq] = slot
        scratch[1, 0:experts, 0:seq] = gate
        slot_col_ref[i] = jnp.transpose(scratch[0])[:seq, :experts]
        gate_col_ref[i] = jnp.transpose(scratch[1])[:seq, :experts]
    place = slot_places(capp, seq)
    sources = [cot_ref.at[i] for i in range(n_img)]
    for e in range(len(out_refs) * exp_dev):
        out_refs[e // exp_dev][e % exp_dev] = dispatch_rows(place, slots, gate_rows, sources, e)


def route_call(me, routes, gates, cotangent, ep_size, exp_dev, capp):
    n_img, seq, width = cotangent.shape
    experts = ep_size * exp_dev
    seq_pad = -(-seq // 128) * 128
    chunk = jax.ShapeDtypeStruct((exp_dev, capp, width), BF16)
    return pl.pallas_call(
        functools.partial(route_kernel, exp_dev),
        in_specs=[pl.BlockSpec(memory_space=pltpu.SMEM)] + [pl.BlockSpec(memory_space=pltpu.VMEM)] * 3,
        out_specs=[pl.BlockSpec(memory_space=pltpu.VMEM)] * (3 + ep_size // 2),
        out_shape=[
            jax.ShapeDtypeStruct((2, n_img, experts, seq), F32),
            jax.ShapeDtypeStruct((n_img, seq, experts), F32),
            jax.ShapeDtypeStruct((n_img, seq, experts), F32),
        ]
        + [chunk] * (ep_size // 2),
        scratch_shapes=[pltpu.VMEM((2, 128, seq_pad), F32)],
        compiler_params=params(16),
        cost_estimate=cost(4),
        name="route_and_dispatch_cotangent",
    )(me, routes.transpose(0, 2, 1), gates.transpose(0, 2, 1), cotangent)


def gateway_kernel(exp_dev, info_ref, cot_ref, *out_refs):
    n_img, seq, width = cot_ref.shape
    capp = out_refs[0].shape[1]
    place = slot_places(capp, seq)
    slots = [info_ref[0, i] for i in range(n_img)]
    gate_rows = [info_ref[1, i] for i in range(n_img)]
    sources = [cot_ref.at[i] for i in range(n_img)]
    half = len(out_refs)
    for j in range(half):
        for k in range(exp_dev):
            out_refs[j][k] = dispatch_rows(place, slots, gate_rows, sources, (half ^ j) * exp_dev + k)


def gateway_call(info, cotangent, ep_size, exp_dev, capp):
    chunk = jax.ShapeDtypeStruct((exp_dev, capp, cotangent.shape[2]), BF16)
    return pl.pallas_call(
        functools.partial(gateway_kernel, exp_dev),
        in_specs=[pl.BlockSpec(memory_space=pltpu.VMEM)] * 2,
        out_specs=[pl.BlockSpec(memory_space=pltpu.VMEM)] * (ep_size // 2),
        out_shape=[chunk] * (ep_size // 2),
        compiler_params=params(16),
        cost_estimate=cost(3),
        name="dispatch_far_cotangent",
    )(info, cotangent)


def attention_kernel(
    heads, tok_ref, w_qkv_ref, w_out_ref, vec_ref, info_ref, qkv_ref, att_ref, lse_ref, resid_ref, *rest
):
    out_refs, second_ref = rest[:-1], rest[-1]
    img = pl.program_id(0)
    seq, width = tok_ref.shape[1:]
    exp_dev, capp = out_refs[0].shape[:2]
    inputs = tok_ref[0].astype(F32)
    norm_first, _ = norm_parts(inputs)
    first = (norm_first * vec_ref[0:1, :] + vec_ref[1:2, :]).astype(BF16)
    qkv = dot_nn(first, w_qkv_ref[...]).astype(BF16)
    qkv_ref[0] = qkv
    low = lax.broadcasted_iota(jnp.int32, (seq, 2 * HD), 1) < HD
    nothing = jnp.zeros((seq, 2 * HD), BF16)
    lane = lax.broadcasted_iota(jnp.int32, (seq, 128), 1)
    lse_all = jnp.zeros((seq, 128), F32)
    pieces = []
    for pair in range(heads // 2):
        at = pair * 2 * HD
        query = qkv[:, at : at + 2 * HD] * jnp.asarray(HD ** (-0.5), BF16)
        key = qkv[:, width + at : width + at + 2 * HD]
        value = qkv[:, 2 * width + at : 2 * width + at + 2 * HD]
        halves = []
        for half in range(2):
            mine = low if half == 0 else jnp.logical_not(low)
            scores = dot_nt(jnp.where(mine, query, nothing), key)
            top = jnp.max(scores, axis=-1, keepdims=True)
            weight = jnp.exp(scores - top)
            total = jnp.sum(weight, axis=-1, keepdims=True)
            prob = (weight * (1.0 / total)).astype(BF16)
            halves.append(dot_nn(prob, value))
            lse_all = jnp.where(lane == 2 * pair + half, top + jnp.log(total), lse_all)
        pieces.append(jnp.where(low, halves[0], halves[1]).astype(BF16))
    lse_ref[0] = lse_all
    attended = jnp.concatenate(pieces, axis=1)
    att_ref[0] = attended
    resid = inputs + dot_nn(attended, w_out_ref[...]) + vec_ref[2:3, :]
    resid_ref[0] = resid
    norm_second, _ = norm_parts(resid)
    second_ref[img] = (norm_second * vec_ref[3:4, :] + vec_ref[4:5, :]).astype(BF16)

    @pl.when(img == pl.num_programs(0) - 1)
    def _():
        n_img = second_ref.shape[0]
        place = slot_places(capp, seq)
        slots = [info_ref[0, i] for i in range(n_img)]
        sources = [second_ref.at[i] for i in range(n_img)]
        for e in range(len(out_refs) * exp_dev):
            out_refs[e // exp_dev][e % exp_dev] = dispatch_rows(place, slots, None, sources, e)


def attention_call(tokens, w_qkv, w_out, vecs, info, ep_size, exp_dev, capp):
    n_img, seq, width = tokens.shape
    chunk = jax.ShapeDtypeStruct((exp_dev, capp, width), BF16)
    image = lambda *tail: pl.BlockSpec((1,) + tail, lambda i: (i, 0, 0))
    return pl.pallas_call(
        functools.partial(attention_kernel, width // HD),
        grid=(n_img,),
        in_specs=[image(seq, width), whole(w_qkv.shape), whole(w_out.shape), whole(vecs.shape), whole(info.shape)],
        out_specs=[image(seq, 3 * width), image(seq, width), image(seq, 128), image(seq, width)]
        + [whole(chunk.shape)] * ep_size,
        out_shape=[
            jax.ShapeDtypeStruct((n_img, seq, 3 * width), BF16),
            jax.ShapeDtypeStruct((n_img, seq, width), BF16),
            jax.ShapeDtypeStruct((n_img, seq, 128), F32),
            jax.ShapeDtypeStruct((n_img, seq, width), F32),
        ]
        + [chunk] * ep_size,
        scratch_shapes=[pltpu.VMEM((n_img, seq, width), BF16)],
        compiler_params=params(32, "arbitrary"),
        cost_estimate=cost(14),
        name="attention_forward_and_dispatch",
    )(tokens, w_qkv, w_out, vecs, info)


def expert_kernel(count, carried, blocks, tile, sel_ref, *refs):
    x_refs, g_refs = refs[:count], refs[count : 2 * count]
    w_in_ref, w_back_ref, b_in_ref, b_back_ref = refs[2 * count : 2 * count + 4]
    before = refs[2 * count + 4 : 2 * count + 4 + carried]
    outs = refs[2 * count + 4 + carried :]
    out_refs, gdis_refs = outs[:count], outs[count : 2 * count]
    sums, (gb_in_ref, gb_back_ref) = outs[2 * count : 2 * count + 4], outs[2 * count + 4 : 2 * count + 6]
    acc_out, acc_dis = outs[2 * count + 6 :]
    exp_dev, _, hidden = w_in_ref.shape
    block = hidden // blocks
    for l in range(exp_dev):
        e = sel_ref[0] ^ l
        own = pl.ds(e, 1)
        for t in range(hidden // tile):
            span = slice(t * tile, (t + 1) * tile)
            w_in, w_back = w_in_ref[e, :, span], w_back_ref[e, span, :]
            gw_back = gw_in = gb_in = None
            for n in range(count):
                x, g = x_refs[n][e], g_refs[n][e]
                pre = dot_nn(x, w_in) + b_in_ref[own, span]
                square = pre * pre
                bent = jnp.tanh(pre * (GELU_C + (GELU_C * 0.044715) * square))
                half = 0.5 + 0.5 * bent
                value = pre * half
                act = value.astype(BF16)
                slope = half + (value - value * half) * (2 * GELU_C + (6 * GELU_C * 0.044715) * square)
                gpre = (dot_nt(g, w_back) * slope).astype(BF16)
                part_dis, part_out = dot_nt(gpre, w_in), dot_nn(act, w_back)
                if t == 0:
                    part_out = part_out + b_back_ref[own, :]
                else:
                    part_dis, part_out = part_dis + acc_dis[n], part_out + acc_out[n]
                if span.stop == hidden:
                    gdis_refs[n][e] = part_dis.astype(BF16)
                    out_refs[n][e] = part_out.astype(BF16)
                else:
                    acc_dis[n] = part_dis
                    acc_out[n] = part_out
                one = (dot_tn(act, g), dot_tn(x, gpre), jnp.sum(gpre.astype(F32), axis=0, keepdims=True))
                gw_back = one[0] if n == 0 else gw_back + one[0]
                gw_in = one[1] if n == 0 else gw_in + one[1]
                gb_in = one[2] if n == 0 else gb_in + one[2]
            gb_in_ref[own, span] = gb_in
            for b in range(t * tile // block, (t + 1) * tile // block):
                at = slice(b * block - t * tile, (b + 1) * block - t * tile)
                at_back, at_in = b ^ sel_ref[1], b ^ sel_ref[2]
                back, into = gw_back[at, :], gw_in[:, at]
                if carried:
                    back = back + before[2 * l][at_back].astype(F32)
                    into = into + before[2 * l + 1][at_in].astype(F32)
                sums[2 * l][at_back] = back.astype(BF16)
                sums[2 * l + 1][at_in] = into.astype(BF16)
        total = jnp.sum(g_refs[0][e].astype(F32), axis=0, keepdims=True)
        for n in range(1, count):
            total = total + jnp.sum(g_refs[n][e].astype(F32), axis=0, keepdims=True)
        gb_back_ref[own, :] = total


def expert_call(xs, gs, w_in, w_back, b_in, b_back, place, blocks, before, microseconds):
    count = len(xs)
    exp_dev, capp, width = xs[0].shape
    hidden = w_in.shape[2]
    block = hidden // blocks
    tile = max(block, min(hidden, 1024))
    narrow = jax.ShapeDtypeStruct((exp_dev, capp, width), BF16)
    shapes = [jax.ShapeDtypeStruct((blocks, block, width), BF16), jax.ShapeDtypeStruct((blocks, width, block), BF16)] * 2
    held = pl.BlockSpec(memory_space=pltpu.VMEM)
    first = 1 + 2 * count + 4
    res = pl.pallas_call(
        functools.partial(expert_kernel, count, len(before), blocks, tile),
        in_specs=[pl.BlockSpec(memory_space=pltpu.SMEM)] + [held] * (2 * count + 4 + len(before)),
        out_specs=[held] * (2 * count + 6),
        out_shape=[narrow] * (2 * count)
        + shapes
        + [jax.ShapeDtypeStruct(b_in.shape, F32), jax.ShapeDtypeStruct(b_back.shape, F32)],
        scratch_shapes=[pltpu.VMEM((count, capp, width), F32)] * 2,
        input_output_aliases={first + k: 2 * count + k for k in range(len(before))},
        compiler_params=params(30),
        cost_estimate=cost(microseconds),
        name="experts",
    )(place, *xs, *gs, w_in, w_back, b_in, b_back, *before)
    return res[:count], res[count : 2 * count], res[2 * count : 2 * count + 4], res[2 * count + 4 :]


def gather_rows(slot_col, value_col, chunk_refs, capp):
    seq = slot_col.shape[0]
    exp_dev = chunk_refs[0].shape[0]
    place = lax.broadcasted_iota(jnp.int32, (seq, capp), 1).astype(F32)
    total = None
    for e in range(len(chunk_refs) * exp_dev):
        value = 1.0 if value_col is None else value_col[:, e : e + 1]
        pick = jnp.where(place == slot_col[:, e : e + 1], value, 0.0).astype(BF16)
        part = dot_nn(pick, chunk_refs[e // exp_dev][e % exp_dev])
        total = part if total is None else total + part
    return total


def backward_kernel(
    heads, ep_size, pack_blocks, place_ref, bias_ref, tok_ref, cot_ref, resid_ref, qkv_ref, att_ref, lse_ref, slot_col_ref, w_qkv_ref, w_out_ref, vec_ref, *rest
):
    chunk_refs = rest[:ep_size]
    packed = len(pack_blocks)
    gtok_ref = rest[ep_size]
    pack_refs = rest[ep_size + 1 : ep_size + 1 + packed]
    gw_qkv_ref, gw_out_ref, gvec_ref, gqkv_ref = rest[ep_size + 1 + packed : ep_size + 5 + packed]
    img = pl.program_id(0)
    seq, width = tok_ref.shape[1:]
    capp = chunk_refs[0].shape[1]
    grad_second = gather_rows(slot_col_ref[0], None, chunk_refs, capp)
    norm_second, inv_second = norm_parts(resid_ref[0])
    grad_resid = cot_ref[0].astype(F32) + norm_back(grad_second, norm_second, inv_second, vec_ref[3:4, :])
    grad_branch = grad_resid.astype(BF16)
    grad_att = dot_nt(grad_branch, w_out_ref[...]).astype(BF16)
    gw_out = dot_tn(att_ref[0], grad_branch)
    low = lax.broadcasted_iota(jnp.int32, (seq, 2 * HD), 1) < HD
    nothing = jnp.zeros((seq, 2 * HD), BF16)
    scale = jnp.asarray(HD ** (-0.5), BF16)
    for pair in range(heads // 2):
        at = pair * 2 * HD
        query = qkv_ref[0, :, at : at + 2 * HD] * scale
        key = qkv_ref[0, :, width + at : width + at + 2 * HD]
        value = qkv_ref[0, :, 2 * width + at : 2 * width + at + 2 * HD]
        gatt = grad_att[:, at : at + 2 * HD]
        grad_q = grad_k = grad_v = None
        for half in range(2):
            mine = low if half == 0 else jnp.logical_not(low)
            head = 2 * pair + half
            query_h = jnp.where(mine, query, nothing)
            gatt_h = jnp.where(mine, gatt, nothing)
            key_h = jnp.where(mine, key, nothing) * scale
            prob = jnp.exp(dot_nt(query_h, key) - lse_ref[0, :, head : head + 1])
            grad_prob = dot_nt(gatt_h, value)
            mean = jnp.sum(grad_prob * prob, axis=-1, keepdims=True)
            grad_scores = (prob * (grad_prob - mean)).astype(BF16)
            part_v = dot_tn(prob.astype(BF16), gatt_h)
            part_q = dot_nn(grad_scores, key_h)
            part_k = dot_tn(grad_scores, query_h)
            grad_q = part_q if grad_q is None else grad_q + part_q
            grad_k = part_k if grad_k is None else grad_k + part_k
            grad_v = part_v if grad_v is None else grad_v + part_v
        gqkv_ref[:, at : at + 2 * HD] = grad_q.astype(BF16)
        gqkv_ref[:, width + at : width + at + 2 * HD] = grad_k.astype(BF16)
        gqkv_ref[:, 2 * width + at : 2 * width + at + 2 * HD] = grad_v.astype(BF16)
    grad_qkv = gqkv_ref[...]
    norm_first, inv_first = norm_parts(tok_ref[0].astype(F32))
    first = (norm_first * vec_ref[0:1, :] + vec_ref[1:2, :]).astype(BF16)
    gw_qkv = dot_tn(first, grad_qkv)
    grad_first = dot_nt(grad_qkv, w_qkv_ref[...])
    gtok_ref[0] = (grad_resid + norm_back(grad_first, norm_first, inv_first, vec_ref[0:1, :])).astype(BF16)
    sums = [
        grad_first * norm_first,
        grad_first,
        grad_branch.astype(F32),
        grad_second * norm_second,
        grad_second,
    ]
    gvec = jnp.concatenate([jnp.sum(v, axis=0, keepdims=True) for v in sums] + [jnp.zeros((3, width), F32)], axis=0)

    @pl.when(img == 0)
    def _():
        gw_out_ref[...] = gw_out
        gw_qkv_ref[...] = gw_qkv
        gvec_ref[...] = gvec

    @pl.when(img > 0)
    def _():
        gw_out_ref[...] += gw_out
        gw_qkv_ref[...] += gw_qkv
        gvec_ref[...] += gvec

    if not packed:
        return

    @pl.when(img == pl.num_programs(0) - 1)
    def _():
        small_ref = rest[-1]
        blocks, per_pack, rows = pack_refs[0].shape[:3]
        per_ep = width // ep_size
        biases = bias_ref.shape[0]
        small_ref[...] = jnp.zeros(small_ref.shape, F32)
        for j in range(ep_size):
            owner = place_ref[0] ^ j
            small_ref[0:8, :] = gvec_ref[:, pl.ds(pl.multiple_of(owner * per_ep, per_ep), per_ep)]
            small_ref[8 : 8 + biases, :] = bias_ref[...] if j == 0 else jnp.zeros(bias_ref.shape, F32)
            for r in range(blocks):
                block = pack_blocks[j // per_pack][r] ^ place_ref[1]
                start = pl.multiple_of(owner * per_ep + block * rows, rows)
                into = pack_refs[j // per_pack]
                into[r, j % per_pack, :, 0 : 3 * width] = gw_qkv_ref[pl.ds(start, rows), :].astype(BF16)
                into[r, j % per_pack, :, 3 * width : 4 * width] = gw_out_ref[pl.ds(start, rows), :].astype(BF16)
                small = small_ref[pl.ds(pl.multiple_of(block * rows, rows), rows), :]
                into[r, j % per_pack, :, 4 * width :] = small.astype(BF16)


def backward_call(tokens, cotangent, resid, qkv, attended, lse, slot_col, w_qkv, w_out, vecs, chunks, place, biases, pack_blocks):
    n_img, seq, width = tokens.shape
    ep_size = len(chunks)
    packed = len(pack_blocks)
    image = lambda arr: pl.BlockSpec((1,) + arr.shape[1:], lambda i: (i, 0, 0))
    sums = [
        jax.ShapeDtypeStruct(w_qkv.shape, F32),
        jax.ShapeDtypeStruct(w_out.shape, F32),
        jax.ShapeDtypeStruct((8, width), F32),
    ]
    scratch = [pltpu.VMEM((seq, 3 * width), BF16)]
    if packed:
        grp_size = len(pack_blocks[0])
        pack = (grp_size, ep_size // 2, width // (ep_size * grp_size), 4 * width + 128)
        outs = [jax.ShapeDtypeStruct(pack, BF16)] * 2
        scratch = [pltpu.VMEM(v.shape, F32) for v in sums] + scratch + [pltpu.VMEM((width // ep_size, 128), F32)]
    else:
        outs = sums
        place, biases = jnp.zeros((2,), jnp.int32), jnp.zeros((8, 128), F32)
    return pl.pallas_call(
        functools.partial(backward_kernel, width // HD, ep_size, pack_blocks),
        grid=(n_img,),
        in_specs=[pl.BlockSpec(memory_space=pltpu.SMEM), whole(biases.shape)]
        + [image(a) for a in (tokens, cotangent, resid, qkv, attended, lse, slot_col)]
        + [whole(a.shape) for a in (w_qkv, w_out, vecs, *chunks)],
        out_specs=[image(tokens)] + [whole(v.shape) for v in outs],
        out_shape=[jax.ShapeDtypeStruct(tokens.shape, BF16)] + outs,
        scratch_shapes=scratch,
        compiler_params=params(40, "arbitrary"),
        cost_estimate=cost(25),
        name="attention_backward",
    )(place, biases, tokens, cotangent, resid, qkv, attended, lse, slot_col, w_qkv, w_out, vecs, *chunks)


def combine_kernel(ep_size, resid_ref, slot_col_ref, gate_col_ref, *rest):
    chunk_refs, out_ref = rest[:ep_size], rest[ep_size]
    mixed = gather_rows(slot_col_ref[0], gate_col_ref[0], chunk_refs, chunk_refs[0].shape[1])
    out_ref[0] = (resid_ref[0] + mixed).astype(BF16)


def combine_call(resid, slot_col, gate_col, chunks):
    n_img, seq, width = resid.shape
    image = lambda arr: pl.BlockSpec((1,) + arr.shape[1:], lambda i: (i, 0, 0))
    return pl.pallas_call(
        functools.partial(combine_kernel, len(chunks)),
        grid=(n_img,),
        in_specs=[image(a) for a in (resid, slot_col, gate_col)] + [whole(c.shape) for c in chunks],
        out_specs=image(resid),
        out_shape=jax.ShapeDtypeStruct(resid.shape, BF16),
        compiler_params=params(16, "arbitrary"),
        cost_estimate=cost(5),
        name="combine_output",
    )(resid, slot_col, gate_col, *chunks)


def swap(array, axis, size, distance):
    return lax.ppermute(array, axis, [(i, i ^ distance) for i in range(size)])


def digits(index, bits):
    number = jnp.zeros((), jnp.int32)
    for bit in bits:
        number = number * 2 + (index >> bit) % 2
    return number


def scatter_step(arrays, bits, size):
    halves = [a.shape[0] // 2 for a in arrays]
    came = [swap(a[h:], "grp", size, 1 << bit) for a, h, bit in zip(arrays, halves, bits)]
    return [a[:h] + c for a, h, c in zip(arrays, halves, came)]


def gather_sums(block, order, size):
    pieces = [block]
    for bit in reversed(order):
        pieces = pieces + [swap(p, "grp", size, 1 << bit) for p in pieces]
    return pieces


def widen_kernel(count, place_ref, *refs):
    piece_refs, out_ref = refs[:count], refs[-1]
    for r in range(count):
        @pl.when(pl.program_id(0) == r)
        def _():
            out_ref[0] = piece_refs[r][0].astype(F32)


def widen_call(pieces, expert, first, axis, shape, base):
    count = len(pieces)
    _, m, n = pieces[0].shape
    at = (lambda r, s: (s[0], r ^ s[1], 0)) if axis == 0 else (lambda r, s: (s[0], 0, r ^ s[1]))
    extra = [] if base is None else [base]
    return pl.pallas_call(
        functools.partial(widen_kernel, count),
        grid_spec=pltpu.PrefetchScalarGridSpec(
            num_scalar_prefetch=1,
            grid=(count,),
            in_specs=[pl.BlockSpec((1, m, n), lambda r, s: (0, 0, 0))] * count
            + [pl.BlockSpec(memory_space=pl.ANY)] * len(extra),
            out_specs=pl.BlockSpec((1, m, n), at),
        ),
        out_shape=jax.ShapeDtypeStruct(shape, F32),
        input_output_aliases={1 + count: 0} if extra else {},
        compiler_params=params(16, "arbitrary"),
        cost_estimate=cost(4),
        name="expert_gradient_result",
    )(jnp.stack([expert, first]), *pieces, *extra)


def unpack_kernel(width, exp_dev, hidden, offsets, place_ref, *refs):
    piece_refs = refs[: len(offsets)]
    gw_qkv_ref, gw_out_ref, vec_ref, b_in_ref, b_back_ref, small_ref = refs[len(offsets) :]
    rows = piece_refs[0].shape[0]
    for piece_ref, offset in zip(piece_refs, offsets):
        at = pl.ds(pl.multiple_of((place_ref[0] ^ offset) * rows, rows), rows)
        gw_qkv_ref[at, :] = piece_ref[:, 0 : 3 * width].astype(F32)
        gw_out_ref[at, :] = piece_ref[:, 3 * width : 4 * width].astype(F32)
        small_ref[at, :] = piece_ref[:, 4 * width :].astype(F32)
    vec_ref[...] = small_ref[0:8, :]
    row = 8
    for ref, length in ((b_in_ref, hidden), (b_back_ref, width)):
        for e in range(exp_dev):
            for at in range(0, length, 128):
                ref[e : e + 1, at : at + 128] = small_ref[row : row + 1, :]
                row += 1


def unpack_call(pieces, offsets, place, width, exp_dev, hidden):
    rows = pieces[0].shape[0] * len(pieces)
    shapes = [(rows, 3 * width), (rows, width), (8, 128), (exp_dev, hidden), (exp_dev, width)]
    return pl.pallas_call(
        functools.partial(unpack_kernel, width, exp_dev, hidden, offsets),
        in_specs=[pl.BlockSpec(memory_space=pltpu.SMEM)] + [pl.BlockSpec(memory_space=pltpu.VMEM)] * len(pieces),
        out_specs=[pl.BlockSpec(memory_space=pltpu.VMEM)] * len(shapes),
        out_shape=[jax.ShapeDtypeStruct(v, F32) for v in shapes],
        scratch_shapes=[pltpu.VMEM((rows, 128), F32)],
        compiler_params=params(16),
        cost_estimate=cost(5),
        name="parameter_gradient_results",
    )(place, *pieces)


def after(arrays, *others):
    return lax.optimization_barrier((list(arrays), others))[0]


def local(
    tokens,
    routes,
    gates,
    ln1_gain,
    ln1_bias,
    w_qkv,
    w_out,
    out_bias,
    ln2_gain,
    ln2_bias,
    w_in,
    in_bias,
    w_back,
    back_bias,
    cotangent,
):
    images, seq_len, width = tokens.shape
    ep_size = lax.axis_size("ep")
    exp_dev = w_in.shape[0]
    experts = exp_dev * ep_size
    capacity = (images * seq_len * 10 + 4 * experts - 1) // (4 * experts)
    capp = -(-capacity // 8) * 8
    me = lax.axis_index("ep").astype(jnp.int32).reshape(1)
    vecs = jnp.stack([ln1_gain, ln1_bias, out_bias, ln2_gain, ln2_bias] + [jnp.zeros_like(ln1_gain)] * 3)

    grp_size = lax.axis_size("grp")
    grp = lax.axis_index("grp").astype(jnp.int32)
    bits = list(range(grp_size.bit_length() - 1))
    order_a, order_b = bits[1:], bits[:0:-1]
    blocks = grp_size // 2
    core = grp % 2
    block_a, block_b = digits(grp, order_a), digits(grp, order_b)
    half = ep_size // 2

    def over_ep(array, distance):
        return swap(array, "ep", ep_size, distance)

    cot_far = over_ep(cotangent, half)
    info, slot_col, gate_col, *g_all = route_call(me, routes, gates, cotangent, ep_size, exp_dev, capp)
    info_far = over_ep(info, half)
    g_all = [g_all[0]] + [over_ep(g_all[d], d) for d in range(1, half)]
    qkv, attended, lse, resid, *x_send = attention_call(tokens, w_qkv, w_out, vecs, info, ep_size, exp_dev, capp)
    place_e = jnp.stack([1 - core, block_a, block_b])
    x_all = [x_send[0]] + [over_ep(x_send[d], d) for d in range(1, half + 1)]
    groups = [[0]] + [list(range(d, min(d + 2, half + 1))) for d in range(1, half + 1, 2)] + [[d] for d in range(half + 1, ep_size)]
    outs, gdis, gdis_back, sums, bias_sums = [], [], [], (), None
    for number, group in enumerate(groups):
        if number == 1:
            info_far, = after([info_far], sums[0])
            far = gateway_call(info_far, cot_far, ep_size, exp_dev, capp)
            g_all = g_all + [far[0]] + [over_ep(far[j], j) for j in range(1, half)]
            for d in range(half + 1, ep_size):
                send, = after([x_send[d]], *far, *x_all[1:d])
                x_all.append(over_ep(send, d))
        xs, gs = [x_all[d] for d in group], [g_all[d] for d in group]
        if number == 0:
            xs = after(xs, *g_all[1:])
        o, g, sums, sums_b = expert_call(xs, gs, w_in, w_back, in_bias, back_bias, place_e, blocks, tuple(sums), 10 * len(group))
        outs, gdis = outs + list(o), gdis + list(g)
        for d in group:
            send, = after([gdis[d]], *([x_all[-1]] if d >= half else []))
            gdis_back.append(over_ep(send, d) if d else send)
        bias_sums = sums_b if number == 0 else [a + b for a, b in zip(bias_sums, sums_b)]
    gb_in, gb_back = bias_sums
    far_b, far_i, near_b, near_i = sums
    far_i, = after([far_i], gdis_back[half])
    state = [near_b + swap(far_b, "grp", grp_size, 1), near_i + swap(far_i, "grp", grp_size, 1)]
    stages = [state]
    for step in range(len(order_a)):
        state = scatter_step(state, [order_a[step], order_b[step]], grp_size)
        stages.append(state)
    sum_b, sum_i = state
    early = stages[len(stages) // 2]
    resid_late, = after([resid], *early)
    all_b, all_i = gather_sums(sum_b, order_a, grp_size), gather_sums(sum_i, order_b, grp_size)
    oth_b = [swap(p, "grp", grp_size, 1) for p in all_b]
    oth_i = [swap(p, "grp", grp_size, 1) for p in all_i]
    gw_back = widen_call(all_b, core, block_a, 0, w_back.shape, None)
    gw_in = widen_call(all_i, core, block_b, 1, w_in.shape, None)
    gw_back = widen_call(oth_b, 1 - core, block_a, 0, w_back.shape, gw_back)
    gw_in = widen_call(oth_i, 1 - core, block_b, 1, w_in.shape, gw_in)
    hidden = w_in.shape[2]
    packed = width // ep_size == 128 and 128 % (16 * grp_size) == 0
    place, biases, pack_blocks = None, None, ()
    if packed:
        order_p, order_q = [0] + order_a, [0] + order_b
        pack_blocks = tuple(
            tuple(sum((r >> (len(o) - 1 - k)) % 2 << bit for k, bit in enumerate(o)) for r in range(grp_size))
            for o in (order_p, order_q)
        )
        place = jnp.stack([me[0], grp])
        biases = jnp.concatenate([gb_in.reshape(-1, 128), gb_back.reshape(-1, 128)])
    grad_tokens, *grads = backward_call(
        tokens, cotangent, resid_late, qkv, attended, lse, slot_col, w_qkv, w_out, vecs, gdis_back, place, biases, pack_blocks
    )
    outs_back = [outs[0]]
    for d in range(1, ep_size):
        send, = after([outs[d]], *early, *gdis_back, *([outs_back[-1]] if d > half else []))
        outs_back.append(over_ep(send, d))
    output = combine_call(resid, slot_col, gate_col, outs_back)
    grads = after(grads, sum_b, sum_i, *outs_back[: half + 1])
    if packed:
        for bits_now in zip(order_p, order_q):
            grads = scatter_step(grads, bits_now, grp_size)
        near, far = after(grads, *outs_back)
        parts = [near[0, d] for d in range(ep_size // 2)] + [far[0, d] for d in range(ep_size // 2)]
        total = parts[0].astype(F32)
        for d in range(1, ep_size):
            total = total + over_ep(parts[d], d).astype(F32)
        pieces, offsets = [total.astype(BF16)], [0]
        for bit in reversed(bits):
            pieces = pieces + [swap(p, "grp", grp_size, 1 << bit) for p in pieces]
            offsets = offsets + [o ^ (1 << bit) for o in offsets]
        gw_qkv, gw_out, gvec, gb_in, gb_back = unpack_call(pieces, offsets, grp.reshape(1), width, exp_dev, hidden)
        gvec = [gvec[k] for k in range(5)]
    else:
        def over_grp(v):
            return lax.psum(v.astype(BF16), "grp").astype(F32)

        def over_all(v):
            return over_grp(lax.psum_scatter(v.astype(BF16), "ep", scatter_dimension=0, tiled=True))

        gw_qkv, gw_out, gvec = grads
        gw_qkv, gw_out, gb_in, gb_back = over_all(gw_qkv), over_all(gw_out), over_grp(gb_in), over_grp(gb_back)
        gvec = [over_all(gvec[k]) for k in range(5)]
    return (output, grad_tokens, gvec[0], gvec[1], gw_qkv, gw_out, gvec[2], gvec[3], gvec[4], gw_in, gb_in, gw_back, gb_back)


def solution(mesh):
    rows = P(("grp", "ep"), None, None)
    return jax.shard_map(
        local,
        mesh=mesh,
        in_specs=(rows, rows, rows)
        + (P(),) * 7
        + (P("ep", None, None), P("ep", None), P("ep", None, None), P("ep", None), rows),
        out_specs=(rows, rows)
        + (P("ep"), P("ep"), P("ep", None), P("ep", None), P("ep"), P("ep"), P("ep"))
        + (P("ep", None, None), P("ep", None), P("ep", None, None), P("ep", None)),
        check_vma=False,
    )
```

```python
import functools

import jax
import jax.numpy as jnp
from jax import lax
from jax.experimental import pallas as pl
from jax.experimental.pallas import tpu as pltpu
from jax.sharding import PartitionSpec as P

HD = 64
NORM_EPS = 1e-06
BF16 = jnp.bfloat16
F32 = jnp.float32
MIB = 1024 * 1024
GELU_C = 0.7978845608028654


def cost(microseconds):
    return pl.CostEstimate(flops=int(microseconds * 10**9), bytes_accessed=2**12, transcendentals=0)


def dot_nn(a, b):
    return jnp.dot(a, b, preferred_element_type=F32)


def dot_nt(a, b):
    return lax.dot_general(a, b, (((1,), (1,)), ((), ())), preferred_element_type=F32)


def dot_tn(a, b):
    return lax.dot_general(a, b, (((0,), (0,)), ((), ())), preferred_element_type=F32)


def norm_parts(values):
    average = jnp.mean(values, axis=-1, keepdims=True)
    centred = values - average
    inv_std = lax.rsqrt(jnp.mean(centred * centred, axis=-1, keepdims=True) + NORM_EPS)
    return centred * inv_std, inv_std


def norm_back(grad_norm, normed, inv_std, gain):
    scaled = grad_norm * gain
    return inv_std * (
        scaled
        - jnp.mean(scaled, axis=-1, keepdims=True)
        - normed * jnp.mean(scaled * normed, axis=-1, keepdims=True)
    )


def whole(shape):
    zeros = (0,) * len(shape)
    return pl.BlockSpec(tuple(shape), lambda *_: zeros)


def params(mebibytes, *semantics):
    return pltpu.CompilerParams(dimension_semantics=semantics or None, vmem_limit_bytes=mebibytes * MIB)


def dispatch_rows(place, slots, values, source_refs, e):
    total = None
    for i, source in enumerate(source_refs):
        value = 1.0 if values is None else values[i][e : e + 1, :]
        pick = jnp.where(place == slots[i][e : e + 1, :], value, 0.0).astype(BF16)
        part = dot_nn(pick, source[...])
        total = part if total is None else total + part
    return total.astype(BF16)


def slot_places(capp, seq):
    return lax.broadcasted_iota(jnp.int32, (capp, seq), 0).astype(F32)


def route_kernel(exp_dev, me_ref, routes_ref, gates_ref, cot_ref, info_ref, slot_col_ref, gate_col_ref, *rest):
    out_refs, scratch = rest[:-1], rest[-1]
    n_img, seq, width = cot_ref.shape
    experts = info_ref.shape[2]
    capp = out_refs[0].shape[1]
    me = me_ref[0]
    expert = lax.broadcasted_iota(jnp.int32, (experts, seq), 0)
    expert = ((expert // exp_dev) ^ me) * exp_dev + expert % exp_dev
    earlier = lax.broadcasted_iota(jnp.int32, (seq, seq), 0)
    later = lax.broadcasted_iota(jnp.int32, (seq, seq), 1)
    tri = jnp.where(earlier < later, 1.0, 0.0).astype(BF16)
    carry = jnp.zeros((experts, 1), F32)
    slots, gate_rows = [], []
    for i in range(n_img):
        hit0 = expert == routes_ref[i, 0:1, :]
        hit1 = expert == routes_ref[i, 1:2, :]
        member = jnp.where(hit0 | hit1, 1.0, 0.0)
        slot = jnp.where(member > 0.5, dot_nn(member.astype(BF16), tri) + carry, -1.0)
        gate = jnp.where(hit0, gates_ref[i, 0:1, :], jnp.where(hit1, gates_ref[i, 1:2, :], 0.0))
        carry = carry + jnp.sum(member, axis=1, keepdims=True)
        slots.append(slot)
        gate_rows.append(gate)
        info_ref[0, i] = slot
        info_ref[1, i] = gate
        scratch[0, 0:experts, 0:seq] = slot
        scratch[1, 0:experts, 0:seq] = gate
        slot_col_ref[i] = jnp.transpose(scratch[0])[:seq, :experts]
        gate_col_ref[i] = jnp.transpose(scratch[1])[:seq, :experts]
    place = slot_places(capp, seq)
    sources = [cot_ref.at[i] for i in range(n_img)]
    for e in range(len(out_refs) * exp_dev):
        out_refs[e // exp_dev][e % exp_dev] = dispatch_rows(place, slots, gate_rows, sources, e)


def route_call(me, routes, gates, cotangent, ep_size, exp_dev, capp):
    n_img, seq, width = cotangent.shape
    experts = ep_size * exp_dev
    seq_pad = -(-seq // 128) * 128
    chunk = jax.ShapeDtypeStruct((exp_dev, capp, width), BF16)
    return pl.pallas_call(
        functools.partial(route_kernel, exp_dev),
        in_specs=[pl.BlockSpec(memory_space=pltpu.SMEM)] + [pl.BlockSpec(memory_space=pltpu.VMEM)] * 3,
        out_specs=[pl.BlockSpec(memory_space=pltpu.VMEM)] * (3 + ep_size // 2),
        out_shape=[
            jax.ShapeDtypeStruct((2, n_img, experts, seq), F32),
            jax.ShapeDtypeStruct((n_img, seq, experts), F32),
            jax.ShapeDtypeStruct((n_img, seq, experts), F32),
        ]
        + [chunk] * (ep_size // 2),
        scratch_shapes=[pltpu.VMEM((2, 128, seq_pad), F32)],
        compiler_params=params(16),
        cost_estimate=cost(4),
        name="route_and_dispatch_cotangent",
    )(me, routes.transpose(0, 2, 1), gates.transpose(0, 2, 1), cotangent)


def gateway_kernel(exp_dev, info_ref, cot_ref, *out_refs):
    n_img, seq, width = cot_ref.shape
    capp = out_refs[0].shape[1]
    place = slot_places(capp, seq)
    slots = [info_ref[0, i] for i in range(n_img)]
    gate_rows = [info_ref[1, i] for i in range(n_img)]
    sources = [cot_ref.at[i] for i in range(n_img)]
    half = len(out_refs)
    for j in range(half):
        for k in range(exp_dev):
            out_refs[j][k] = dispatch_rows(place, slots, gate_rows, sources, (half ^ j) * exp_dev + k)


def gateway_call(info, cotangent, ep_size, exp_dev, capp):
    chunk = jax.ShapeDtypeStruct((exp_dev, capp, cotangent.shape[2]), BF16)
    return pl.pallas_call(
        functools.partial(gateway_kernel, exp_dev),
        in_specs=[pl.BlockSpec(memory_space=pltpu.VMEM)] * 2,
        out_specs=[pl.BlockSpec(memory_space=pltpu.VMEM)] * (ep_size // 2),
        out_shape=[chunk] * (ep_size // 2),
        compiler_params=params(16),
        cost_estimate=cost(3),
        name="dispatch_far_cotangent",
    )(info, cotangent)


def attention_kernel(
    heads, tok_ref, w_qkv_ref, w_out_ref, vec_ref, info_ref, qkv_ref, att_ref, lse_ref, resid_ref, *rest
):
    out_refs, second_ref = rest[:-1], rest[-1]
    img = pl.program_id(0)
    seq, width = tok_ref.shape[1:]
    exp_dev, capp = out_refs[0].shape[:2]
    inputs = tok_ref[0].astype(F32)
    norm_first, _ = norm_parts(inputs)
    first = (norm_first * vec_ref[0:1, :] + vec_ref[1:2, :]).astype(BF16)
    qkv = dot_nn(first, w_qkv_ref[...]).astype(BF16)
    qkv_ref[0] = qkv
    low = lax.broadcasted_iota(jnp.int32, (seq, 2 * HD), 1) < HD
    nothing = jnp.zeros((seq, 2 * HD), BF16)
    lane = lax.broadcasted_iota(jnp.int32, (seq, 128), 1)
    lse_all = jnp.zeros((seq, 128), F32)
    pieces = []
    for pair in range(heads // 2):
        at = pair * 2 * HD
        query = qkv[:, at : at + 2 * HD] * jnp.asarray(HD ** (-0.5), BF16)
        key = qkv[:, width + at : width + at + 2 * HD]
        value = qkv[:, 2 * width + at : 2 * width + at + 2 * HD]
        halves = []
        for half in range(2):
            mine = low if half == 0 else jnp.logical_not(low)
            scores = dot_nt(jnp.where(mine, query, nothing), key)
            top = jnp.max(scores, axis=-1, keepdims=True)
            weight = jnp.exp(scores - top)
            total = jnp.sum(weight, axis=-1, keepdims=True)
            prob = (weight * (1.0 / total)).astype(BF16)
            halves.append(dot_nn(prob, value))
            lse_all = jnp.where(lane == 2 * pair + half, top + jnp.log(total), lse_all)
        pieces.append(jnp.where(low, halves[0], halves[1]).astype(BF16))
    lse_ref[0] = lse_all
    attended = jnp.concatenate(pieces, axis=1)
    att_ref[0] = attended
    resid = inputs + dot_nn(attended, w_out_ref[...]) + vec_ref[2:3, :]
    resid_ref[0] = resid
    norm_second, _ = norm_parts(resid)
    second_ref[img] = (norm_second * vec_ref[3:4, :] + vec_ref[4:5, :]).astype(BF16)

    @pl.when(img == pl.num_programs(0) - 1)
    def _():
        n_img = second_ref.shape[0]
        place = slot_places(capp, seq)
        slots = [info_ref[0, i] for i in range(n_img)]
        sources = [second_ref.at[i] for i in range(n_img)]
        for e in range(len(out_refs) * exp_dev):
            out_refs[e // exp_dev][e % exp_dev] = dispatch_rows(place, slots, None, sources, e)


def attention_call(tokens, w_qkv, w_out, vecs, info, ep_size, exp_dev, capp):
    n_img, seq, width = tokens.shape
    chunk = jax.ShapeDtypeStruct((exp_dev, capp, width), BF16)
    image = lambda *tail: pl.BlockSpec((1,) + tail, lambda i: (i, 0, 0))
    return pl.pallas_call(
        functools.partial(attention_kernel, width // HD),
        grid=(n_img,),
        in_specs=[image(seq, width), whole(w_qkv.shape), whole(w_out.shape), whole(vecs.shape), whole(info.shape)],
        out_specs=[image(seq, 3 * width), image(seq, width), image(seq, 128), image(seq, width)]
        + [whole(chunk.shape)] * ep_size,
        out_shape=[
            pltpu.HBM((n_img, seq, 3 * width), BF16),
            pltpu.HBM((n_img, seq, width), BF16),
            pltpu.HBM((n_img, seq, 128), F32),
            pltpu.HBM((n_img, seq, width), F32),
        ]
        + [chunk] * ep_size,
        scratch_shapes=[pltpu.VMEM((n_img, seq, width), BF16)],
        compiler_params=params(32, "arbitrary"),
        cost_estimate=cost(14),
        name="attention_forward_and_dispatch",
    )(tokens, w_qkv, w_out, vecs, info)


def expert_kernel(count, carried, blocks, tile, sel_ref, *refs):
    x_refs, g_refs = refs[:count], refs[count : 2 * count]
    w_in_ref, w_back_ref, b_in_ref, b_back_ref = refs[2 * count : 2 * count + 4]
    before = refs[2 * count + 4 : 2 * count + 4 + carried]
    outs = refs[2 * count + 4 + carried :]
    out_refs, gdis_refs = outs[:count], outs[count : 2 * count]
    sums, (gb_in_ref, gb_back_ref) = outs[2 * count : 2 * count + 4], outs[2 * count + 4 : 2 * count + 6]
    acc_out, acc_dis = outs[2 * count + 6 :]
    exp_dev, _, hidden = w_in_ref.shape
    block = hidden // blocks
    for l in range(exp_dev):
        e = sel_ref[0] ^ l
        own = pl.ds(e, 1)
        for t in range(hidden // tile):
            span = slice(t * tile, (t + 1) * tile)
            w_in, w_back = w_in_ref[e, :, span], w_back_ref[e, span, :]
            gw_back = gw_in = gb_in = None
            for n in range(count):
                x, g = x_refs[n][e], g_refs[n][e]
                pre = dot_nn(x, w_in) + b_in_ref[own, span]
                square = pre * pre
                bent = jnp.tanh(pre * (GELU_C + (GELU_C * 0.044715) * square))
                half = 0.5 + 0.5 * bent
                value = pre * half
                act = value.astype(BF16)
                slope = half + (value - value * half) * (2 * GELU_C + (6 * GELU_C * 0.044715) * square)
                gpre = (dot_nt(g, w_back) * slope).astype(BF16)
                part_dis, part_out = dot_nt(gpre, w_in), dot_nn(act, w_back)
                if t == 0:
                    part_out = part_out + b_back_ref[own, :]
                else:
                    part_dis, part_out = part_dis + acc_dis[n], part_out + acc_out[n]
                if span.stop == hidden:
                    gdis_refs[n][e] = part_dis.astype(BF16)
                    out_refs[n][e] = part_out.astype(BF16)
                else:
                    acc_dis[n] = part_dis
                    acc_out[n] = part_out
                one = (dot_tn(act, g), dot_tn(x, gpre), jnp.sum(gpre.astype(F32), axis=0, keepdims=True))
                gw_back = one[0] if n == 0 else gw_back + one[0]
                gw_in = one[1] if n == 0 else gw_in + one[1]
                gb_in = one[2] if n == 0 else gb_in + one[2]
            gb_in_ref[own, span] = gb_in
            for b in range(t * tile // block, (t + 1) * tile // block):
                at = slice(b * block - t * tile, (b + 1) * block - t * tile)
                at_back, at_in = b ^ sel_ref[1], b ^ sel_ref[2]
                back, into = gw_back[at, :], gw_in[:, at]
                if carried:
                    back = back + before[2 * l][at_back].astype(F32)
                    into = into + before[2 * l + 1][at_in].astype(F32)
                sums[2 * l][at_back] = back.astype(BF16)
                sums[2 * l + 1][at_in] = into.astype(BF16)
        total = jnp.sum(g_refs[0][e].astype(F32), axis=0, keepdims=True)
        for n in range(1, count):
            total = total + jnp.sum(g_refs[n][e].astype(F32), axis=0, keepdims=True)
        gb_back_ref[own, :] = total


def expert_call(xs, gs, w_in, w_back, b_in, b_back, place, blocks, before, microseconds):
    count = len(xs)
    exp_dev, capp, width = xs[0].shape
    hidden = w_in.shape[2]
    block = hidden // blocks
    tile = max(block, min(hidden, 1024))
    narrow = jax.ShapeDtypeStruct((exp_dev, capp, width), BF16)
    shapes = [jax.ShapeDtypeStruct((blocks, block, width), BF16), jax.ShapeDtypeStruct((blocks, width, block), BF16)] * 2
    held = pl.BlockSpec(memory_space=pltpu.VMEM)
    first = 1 + 2 * count + 4
    res = pl.pallas_call(
        functools.partial(expert_kernel, count, len(before), blocks, tile),
        in_specs=[pl.BlockSpec(memory_space=pltpu.SMEM)] + [held] * (2 * count + 4 + len(before)),
        out_specs=[held] * (2 * count + 6),
        out_shape=[narrow] * (2 * count)
        + shapes
        + [jax.ShapeDtypeStruct(b_in.shape, F32), jax.ShapeDtypeStruct(b_back.shape, F32)],
        scratch_shapes=[pltpu.VMEM((count, capp, width), F32)] * 2,
        input_output_aliases={first + k: 2 * count + k for k in range(len(before))},
        compiler_params=params(30),
        cost_estimate=cost(microseconds),
        name="experts",
    )(place, *xs, *gs, w_in, w_back, b_in, b_back, *before)
    return res[:count], res[count : 2 * count], res[2 * count : 2 * count + 4], res[2 * count + 4 :]


def gather_rows(slot_col, value_col, chunk_refs, capp):
    seq = slot_col.shape[0]
    exp_dev = chunk_refs[0].shape[0]
    place = lax.broadcasted_iota(jnp.int32, (seq, capp), 1).astype(F32)
    total = None
    for e in range(len(chunk_refs) * exp_dev):
        value = 1.0 if value_col is None else value_col[:, e : e + 1]
        pick = jnp.where(place == slot_col[:, e : e + 1], value, 0.0).astype(BF16)
        part = dot_nn(pick, chunk_refs[e // exp_dev][e % exp_dev])
        total = part if total is None else total + part
    return total


def backward_kernel(
    heads, ep_size, pack_blocks, place_ref, bias_ref, tok_ref, cot_ref, resid_ref, qkv_ref, att_ref, lse_ref, slot_col_ref, w_qkv_ref, w_out_ref, vec_ref, *rest
):
    chunk_refs = rest[:ep_size]
    packed = 1 if pack_blocks else 0
    gtok_ref = rest[ep_size]
    pack_refs = rest[ep_size + 1 : ep_size + 1 + packed]
    gw_qkv_ref, gw_out_ref, gvec_ref, gqkv_ref = rest[ep_size + 1 + packed : ep_size + 5 + packed]
    img = pl.program_id(0)
    seq, width = tok_ref.shape[1:]
    capp = chunk_refs[0].shape[1]
    grad_second = gather_rows(slot_col_ref[0], None, chunk_refs, capp)
    norm_second, inv_second = norm_parts(resid_ref[0])
    grad_resid = cot_ref[0].astype(F32) + norm_back(grad_second, norm_second, inv_second, vec_ref[3:4, :])
    grad_branch = grad_resid.astype(BF16)
    grad_att = dot_nt(grad_branch, w_out_ref[...]).astype(BF16)
    gw_out = dot_tn(att_ref[0], grad_branch)
    low = lax.broadcasted_iota(jnp.int32, (seq, 2 * HD), 1) < HD
    nothing = jnp.zeros((seq, 2 * HD), BF16)
    scale = jnp.asarray(HD ** (-0.5), BF16)
    for pair in range(heads // 2):
        at = pair * 2 * HD
        query = qkv_ref[0, :, at : at + 2 * HD] * scale
        key = qkv_ref[0, :, width + at : width + at + 2 * HD]
        value = qkv_ref[0, :, 2 * width + at : 2 * width + at + 2 * HD]
        gatt = grad_att[:, at : at + 2 * HD]
        grad_q = grad_k = grad_v = None
        for half in range(2):
            mine = low if half == 0 else jnp.logical_not(low)
            head = 2 * pair + half
            query_h = jnp.where(mine, query, nothing)
            gatt_h = jnp.where(mine, gatt, nothing)
            key_h = jnp.where(mine, key, nothing) * scale
            prob = jnp.exp(dot_nt(query_h, key) - lse_ref[0, :, head : head + 1])
            grad_prob = dot_nt(gatt_h, value)
            mean = jnp.sum(grad_prob * prob, axis=-1, keepdims=True)
            grad_scores = (prob * (grad_prob - mean)).astype(BF16)
            part_v = dot_tn(prob.astype(BF16), gatt_h)
            part_q = dot_nn(grad_scores, key_h)
            part_k = dot_tn(grad_scores, query_h)
            grad_q = part_q if grad_q is None else grad_q + part_q
            grad_k = part_k if grad_k is None else grad_k + part_k
            grad_v = part_v if grad_v is None else grad_v + part_v
        gqkv_ref[:, at : at + 2 * HD] = grad_q.astype(BF16)
        gqkv_ref[:, width + at : width + at + 2 * HD] = grad_k.astype(BF16)
        gqkv_ref[:, 2 * width + at : 2 * width + at + 2 * HD] = grad_v.astype(BF16)
    grad_qkv = gqkv_ref[...]
    norm_first, inv_first = norm_parts(tok_ref[0].astype(F32))
    first = (norm_first * vec_ref[0:1, :] + vec_ref[1:2, :]).astype(BF16)
    gw_qkv = dot_tn(first, grad_qkv)
    grad_first = dot_nt(grad_qkv, w_qkv_ref[...])
    gtok_ref[0] = (grad_resid + norm_back(grad_first, norm_first, inv_first, vec_ref[0:1, :])).astype(BF16)
    sums = [
        grad_first * norm_first,
        grad_first,
        grad_branch.astype(F32),
        grad_second * norm_second,
        grad_second,
    ]
    gvec = jnp.concatenate([jnp.sum(v, axis=0, keepdims=True) for v in sums] + [jnp.zeros((3, width), F32)], axis=0)

    @pl.when(img == 0)
    def _():
        gw_out_ref[...] = gw_out
        gw_qkv_ref[...] = gw_qkv
        gvec_ref[...] = gvec

    @pl.when(img > 0)
    def _():
        gw_out_ref[...] += gw_out
        gw_qkv_ref[...] += gw_qkv
        gvec_ref[...] += gvec

    if not packed:
        return

    @pl.when(img == pl.num_programs(0) - 1)
    def _():
        small_ref = rest[-1]
        blocks, _, rows = pack_refs[0].shape[:3]
        per_ep = width // ep_size
        biases = bias_ref.shape[0]
        small_ref[...] = jnp.zeros(small_ref.shape, F32)
        for j in range(ep_size):
            owner = place_ref[0] ^ j
            small_ref[0:8, :] = gvec_ref[:, pl.ds(pl.multiple_of(owner * per_ep, per_ep), per_ep)]
            small_ref[8 : 8 + biases, :] = bias_ref[...] if j == 0 else jnp.zeros(bias_ref.shape, F32)
            for r in range(blocks):
                block = pack_blocks[r] ^ place_ref[1]
                start = pl.multiple_of(owner * per_ep + block * rows, rows)
                into = pack_refs[0]
                into[r, j, :, 0 : 3 * width] = gw_qkv_ref[pl.ds(start, rows), :].astype(BF16)
                into[r, j, :, 3 * width : 4 * width] = gw_out_ref[pl.ds(start, rows), :].astype(BF16)
                small = small_ref[pl.ds(pl.multiple_of(block * rows, rows), rows), :]
                into[r, j, :, 4 * width :] = small.astype(BF16)


def backward_call(tokens, cotangent, resid, qkv, attended, lse, slot_col, w_qkv, w_out, vecs, chunks, place, biases, pack_blocks):
    n_img, seq, width = tokens.shape
    ep_size = len(chunks)
    packed = 1 if pack_blocks else 0
    image = lambda arr: pl.BlockSpec((1,) + arr.shape[1:], lambda i: (i, 0, 0))
    sums = [
        jax.ShapeDtypeStruct(w_qkv.shape, F32),
        jax.ShapeDtypeStruct(w_out.shape, F32),
        jax.ShapeDtypeStruct((8, width), F32),
    ]
    scratch = [pltpu.VMEM((seq, 3 * width), BF16)]
    if packed:
        grp_size = len(pack_blocks)
        pack = (grp_size, ep_size, width // (ep_size * grp_size), 4 * width + 128)
        outs = [jax.ShapeDtypeStruct(pack, BF16)]
        scratch = [pltpu.VMEM(v.shape, F32) for v in sums] + scratch + [pltpu.VMEM((width // ep_size, 128), F32)]
    else:
        outs = sums
        place, biases = jnp.zeros((2,), jnp.int32), jnp.zeros((8, 128), F32)
    return pl.pallas_call(
        functools.partial(backward_kernel, width // HD, ep_size, pack_blocks),
        grid=(n_img,),
        in_specs=[pl.BlockSpec(memory_space=pltpu.SMEM), whole(biases.shape)]
        + [image(a) for a in (tokens, cotangent, resid, qkv, attended, lse, slot_col)]
        + [whole(a.shape) for a in (w_qkv, w_out, vecs, *chunks)],
        out_specs=[image(tokens)] + [whole(v.shape) for v in outs],
        out_shape=[jax.ShapeDtypeStruct(tokens.shape, BF16)] + outs,
        scratch_shapes=scratch,
        compiler_params=params(40, "arbitrary"),
        cost_estimate=cost(25),
        name="attention_backward",
    )(place, biases, tokens, cotangent, *(pltpu.with_memory_space_constraint(a, pltpu.HBM) for a in (resid, qkv, attended, lse)), slot_col, w_qkv, w_out, vecs, *chunks)


def combine_kernel(ep_size, resid_ref, slot_col_ref, gate_col_ref, *rest):
    chunk_refs, out_ref = rest[:ep_size], rest[ep_size]
    mixed = gather_rows(slot_col_ref[0], gate_col_ref[0], chunk_refs, chunk_refs[0].shape[1])
    out_ref[0] = (resid_ref[0] + mixed).astype(BF16)


def combine_call(resid, slot_col, gate_col, chunks):
    n_img, seq, width = resid.shape
    image = lambda arr: pl.BlockSpec((1,) + arr.shape[1:], lambda i: (i, 0, 0))
    return pl.pallas_call(
        functools.partial(combine_kernel, len(chunks)),
        grid=(n_img,),
        in_specs=[image(a) for a in (resid, slot_col, gate_col)] + [whole(c.shape) for c in chunks],
        out_specs=image(resid),
        out_shape=jax.ShapeDtypeStruct(resid.shape, BF16),
        compiler_params=params(16, "arbitrary"),
        cost_estimate=cost(5),
        name="combine_output",
    )(resid, slot_col, gate_col, *chunks)


def swap(array, axis, size, distance):
    return lax.ppermute(array, axis, [(i, i ^ distance) for i in range(size)])


def digits(index, bits):
    number = jnp.zeros((), jnp.int32)
    for bit in bits:
        number = number * 2 + (index >> bit) % 2
    return number


def scatter_step(arrays, bits, size):
    halves = [a.shape[0] // 2 for a in arrays]
    came = [swap(a[h:], "grp", size, 1 << bit) for a, h, bit in zip(arrays, halves, bits)]
    return [a[:h] + c for a, h, c in zip(arrays, halves, came)]


def gather_sums(block, order, size):
    pieces = [block]
    for bit in reversed(order):
        held = pieces[0] if len(pieces) == 1 else jnp.concatenate(pieces)
        pieces = pieces + [swap(held, "grp", size, 1 << bit)]
    return pieces


def widen_kernel(starts, place_ref, *refs):
    piece_refs, out_ref = refs[: len(starts)], refs[-1]
    for start, piece_ref in zip(starts, piece_refs):
        for k in range(piece_ref.shape[0]):
            @pl.when(pl.program_id(0) == start + k)
            def _():
                out_ref[0] = piece_ref[k].astype(F32)


def widen_call(pieces, expert, first, axis, shape, base):
    starts = [sum(p.shape[0] for p in pieces[:k]) for k in range(len(pieces))]
    count = sum(p.shape[0] for p in pieces)
    _, m, n = pieces[0].shape
    at = (lambda r, s: (s[0], r ^ s[1], 0)) if axis == 0 else (lambda r, s: (s[0], 0, r ^ s[1]))
    extra = [] if base is None else [base]
    return pl.pallas_call(
        functools.partial(widen_kernel, starts),
        grid_spec=pltpu.PrefetchScalarGridSpec(
            num_scalar_prefetch=1,
            grid=(count,),
            in_specs=[whole(p.shape) for p in pieces] + [pl.BlockSpec(memory_space=pl.ANY)] * len(extra),
            out_specs=pl.BlockSpec((1, m, n), at),
        ),
        out_shape=jax.ShapeDtypeStruct(shape, F32),
        input_output_aliases={1 + len(pieces): 0} if extra else {},
        compiler_params=params(16, "arbitrary"),
        cost_estimate=cost(4),
        name="expert_gradient_result",
    )(jnp.stack([expert, first]), *pieces, *extra)


def unpack_kernel(width, exp_dev, hidden, offsets, place_ref, *refs):
    piece_refs = refs[: len(offsets)]
    gw_qkv_ref, gw_out_ref, vec_ref, b_in_ref, b_back_ref, small_ref = refs[len(offsets) :]
    rows = piece_refs[0].shape[0]
    for piece_ref, offset in zip(piece_refs, offsets):
        at = pl.ds(pl.multiple_of((place_ref[0] ^ offset) * rows, rows), rows)
        gw_qkv_ref[at, :] = piece_ref[:, 0 : 3 * width].astype(F32)
        gw_out_ref[at, :] = piece_ref[:, 3 * width : 4 * width].astype(F32)
        small_ref[at, :] = piece_ref[:, 4 * width :].astype(F32)
    vec_ref[...] = small_ref[0:8, :]
    row = 8
    for ref, length in ((b_in_ref, hidden), (b_back_ref, width)):
        for e in range(exp_dev):
            for at in range(0, length, 128):
                ref[e : e + 1, at : at + 128] = small_ref[row : row + 1, :]
                row += 1


def unpack_call(pieces, offsets, place, width, exp_dev, hidden):
    rows = pieces[0].shape[0] * len(pieces)
    shapes = [(rows, 3 * width), (rows, width), (8, 128), (exp_dev, hidden), (exp_dev, width)]
    return pl.pallas_call(
        functools.partial(unpack_kernel, width, exp_dev, hidden, offsets),
        in_specs=[pl.BlockSpec(memory_space=pltpu.SMEM)] + [pl.BlockSpec(memory_space=pltpu.VMEM)] * len(pieces),
        out_specs=[pl.BlockSpec(memory_space=pltpu.VMEM)] * len(shapes),
        out_shape=[jax.ShapeDtypeStruct(v, F32) for v in shapes],
        scratch_shapes=[pltpu.VMEM((rows, 128), F32)],
        compiler_params=params(16),
        cost_estimate=cost(5),
        name="parameter_gradient_results",
    )(place, *pieces)


def after(arrays, *others):
    return lax.optimization_barrier((list(arrays), others))[0]


def local(
    tokens,
    routes,
    gates,
    ln1_gain,
    ln1_bias,
    w_qkv,
    w_out,
    out_bias,
    ln2_gain,
    ln2_bias,
    w_in,
    in_bias,
    w_back,
    back_bias,
    cotangent,
):
    images, seq_len, width = tokens.shape
    ep_size = lax.axis_size("ep")
    exp_dev = w_in.shape[0]
    experts = exp_dev * ep_size
    capacity = (images * seq_len * 10 + 4 * experts - 1) // (4 * experts)
    capp = -(-capacity // 8) * 8
    me = lax.axis_index("ep").astype(jnp.int32).reshape(1)
    vecs = jnp.stack([ln1_gain, ln1_bias, out_bias, ln2_gain, ln2_bias] + [jnp.zeros_like(ln1_gain)] * 3)

    grp_size = lax.axis_size("grp")
    grp = lax.axis_index("grp").astype(jnp.int32)
    bits = list(range(grp_size.bit_length() - 1))
    order_a, order_b = bits[1:], bits[:0:-1]
    blocks = grp_size // 2
    core = grp % 2
    block_a, block_b = digits(grp, order_a), digits(grp, order_b)
    half = ep_size // 2

    def over_ep(array, distance):
        return swap(array, "ep", ep_size, distance)

    cot_far = over_ep(cotangent, half)
    info, slot_col, gate_col, *g_all = route_call(me, routes, gates, cotangent, ep_size, exp_dev, capp)
    info_far = over_ep(info, half)
    g_all = [g_all[0]] + [over_ep(g_all[d], d) for d in range(1, half)]
    qkv, attended, lse, resid, *x_send = attention_call(tokens, w_qkv, w_out, vecs, info, ep_size, exp_dev, capp)
    place_e = jnp.stack([1 - core, block_a, block_b])
    x_all = [x_send[0]] + [over_ep(x_send[d], d) for d in range(1, half + 1)]
    groups = [[0]] + [list(range(d, min(d + 2, half + 1))) for d in range(1, half + 1, 2)] + [[d] for d in range(half + 1, ep_size)]
    outs, gdis, gdis_back, sums, bias_sums = [], [], [], (), None
    for number, group in enumerate(groups):
        if number == 1:
            info_far, = after([info_far], sums[0])
            far = gateway_call(info_far, cot_far, ep_size, exp_dev, capp)
            g_all = g_all + [far[0]] + [over_ep(far[j], j) for j in range(1, half)]
            for d in range(half + 1, ep_size):
                send, = after([x_send[d]], *far, *x_all[1:d])
                x_all.append(over_ep(send, d))
        xs, gs = [x_all[d] for d in group], [g_all[d] for d in group]
        if number == 0:
            xs = after(xs, *g_all[1:])
        o, g, sums, sums_b = expert_call(xs, gs, w_in, w_back, in_bias, back_bias, place_e, blocks, tuple(sums), 10 * len(group))
        outs, gdis = outs + list(o), gdis + list(g)
        for d in group:
            send, = after([gdis[d]], *([x_all[-1]] if d >= half else []))
            gdis_back.append(over_ep(send, d) if d else send)
        bias_sums = sums_b if number == 0 else [a + b for a, b in zip(bias_sums, sums_b)]
    gb_in, gb_back = bias_sums
    far_b, far_i, near_b, near_i = sums
    state = [near_b + swap(far_b, "grp", grp_size, 1), near_i + swap(far_i, "grp", grp_size, 1)]
    stages = [state]
    for step in range(len(order_a)):
        state = scatter_step(state, [order_a[step], order_b[step]], grp_size)
        stages.append(state)
    sum_b, sum_i = state
    early = stages[len(stages) // 2]
    resid_late, = after([resid], *early)
    all_b, all_i = gather_sums(sum_b, order_a, grp_size), gather_sums(sum_i, order_b, grp_size)
    hidden = w_in.shape[2]
    packed = width // ep_size == 128 and 128 % (16 * grp_size) == 0
    place, biases, pack_blocks = None, None, ()
    if packed:
        pack_blocks = tuple(range(0, grp_size, 2)) + tuple(range(1, grp_size, 2))
        place = jnp.stack([me[0], grp])
        biases = jnp.concatenate([gb_in.reshape(-1, 128), gb_back.reshape(-1, 128)])
    grad_tokens, *grads = backward_call(
        tokens, cotangent, resid_late, qkv, attended, lse, slot_col, w_qkv, w_out, vecs, gdis_back, place, biases, pack_blocks
    )
    outs_back = [outs[0]]
    for d in range(1, ep_size):
        send, = after([outs[d]], *early, *gdis_back, *([outs_back[-1]] if d > half else []))
        outs_back.append(over_ep(send, d))
    output = combine_call(resid, slot_col, gate_col, outs_back)
    grads = after(grads, sum_b, sum_i, *outs_back[: half + 1])
    if packed:
        chips = grp_size // 2
        pack = grads[0][:chips] + swap(grads[0][chips:], "grp", grp_size, 1)
        pack, = after([pack], all_b[1], all_i[1])
        share = pack[0].astype(F32)
        for c in range(1, chips):
            share = share + swap(pack[c], "grp", grp_size, 2 * c).astype(F32)
        share, *_ = after([share.astype(BF16)], *outs_back)
        total = share[0].astype(F32)
        for d in range(1, ep_size):
            total = total + over_ep(share[d], d).astype(F32)
        total, *_ = after([total.astype(BF16)], all_b[-1], all_i[-1])
        late = total
        pieces = [total] + [swap(total, "grp", grp_size, 2 * c) for c in range(1, chips)]
        offsets = tuple(range(0, grp_size, 2)) + tuple(range(1, grp_size, 2))
        pieces = pieces + [swap(p, "grp", grp_size, 1) for p in pieces]
        gw_qkv, gw_out, gvec, gb_in, gb_back = unpack_call(pieces, offsets, grp.reshape(1), width, exp_dev, hidden)
        gvec = [gvec[k] for k in range(5)]
    else:
        def over_grp(v):
            return lax.psum(v.astype(BF16), "grp").astype(F32)

        def over_all(v):
            return over_grp(lax.psum_scatter(v.astype(BF16), "ep", scatter_dimension=0, tiled=True))

        gw_qkv, gw_out, gvec = grads
        late = gw_qkv
        gw_qkv, gw_out, gb_in, gb_back = over_all(gw_qkv), over_all(gw_out), over_grp(gb_in), over_grp(gb_back)
        gvec = [over_all(gvec[k]) for k in range(5)]
    oth_b = [swap(p, "grp", grp_size, 1) for p in after(all_b, late)]
    oth_i = [swap(p, "grp", grp_size, 1) for p in after(all_i, late)]
    gw_back = widen_call(all_b, core, block_a, 0, w_back.shape, None)
    gw_in = widen_call(all_i, core, block_b, 1, w_in.shape, None)
    gw_back = widen_call(oth_b, 1 - core, block_a, 0, w_back.shape, gw_back)
    gw_in = widen_call(oth_i, 1 - core, block_b, 1, w_in.shape, gw_in)
    return (output, grad_tokens, gvec[0], gvec[1], gw_qkv, gw_out, gvec[2], gvec[3], gvec[4], gw_in, gb_in, gw_back, gb_back)


def solution(mesh):
    rows = P(("grp", "ep"), None, None)
    return jax.shard_map(
        local,
        mesh=mesh,
        in_specs=(rows, rows, rows)
        + (P(),) * 7
        + (P("ep", None, None), P("ep", None), P("ep", None, None), P("ep", None), rows),
        out_specs=(rows, rows)
        + (P("ep"), P("ep"), P("ep", None), P("ep", None), P("ep"), P("ep"), P("ep"))
        + (P("ep", None, None), P("ep", None), P("ep", None, None), P("ep", None)),
        check_vma=False,
    )
```

```python
import functools

import jax
import jax.numpy as jnp
from jax import lax
from jax.experimental import pallas as pl
from jax.experimental.pallas import tpu as pltpu
from jax.sharding import PartitionSpec as P

HD = 64
NORM_EPS = 1e-06
BF16 = jnp.bfloat16
F32 = jnp.float32
MIB = 1024 * 1024
GELU_C = 0.7978845608028654


def cost(microseconds):
    return pl.CostEstimate(flops=int(microseconds * 10**9), bytes_accessed=2**12, transcendentals=0)


def dot_nn(a, b):
    return jnp.dot(a, b, preferred_element_type=F32)


def dot_nt(a, b):
    return lax.dot_general(a, b, (((1,), (1,)), ((), ())), preferred_element_type=F32)


def dot_tn(a, b):
    return lax.dot_general(a, b, (((0,), (0,)), ((), ())), preferred_element_type=F32)


def norm_parts(values):
    average = jnp.mean(values, axis=-1, keepdims=True)
    centred = values - average
    inv_std = lax.rsqrt(jnp.mean(centred * centred, axis=-1, keepdims=True) + NORM_EPS)
    return centred * inv_std, inv_std


def norm_back(grad_norm, normed, inv_std, gain):
    scaled = grad_norm * gain
    return inv_std * (
        scaled
        - jnp.mean(scaled, axis=-1, keepdims=True)
        - normed * jnp.mean(scaled * normed, axis=-1, keepdims=True)
    )


def whole(shape):
    zeros = (0,) * len(shape)
    return pl.BlockSpec(tuple(shape), lambda *_: zeros)


def params(mebibytes, *semantics):
    return pltpu.CompilerParams(dimension_semantics=semantics or None, vmem_limit_bytes=mebibytes * MIB)


def dispatch_rows(place, slots, values, source_refs, e):
    total = None
    for i, source in enumerate(source_refs):
        value = 1.0 if values is None else values[i][e : e + 1, :]
        pick = jnp.where(place == slots[i][e : e + 1, :], value, 0.0).astype(BF16)
        part = dot_nn(pick, source[...])
        total = part if total is None else total + part
    return total.astype(BF16)


def slot_places(capp, seq):
    return lax.broadcasted_iota(jnp.int32, (capp, seq), 0).astype(F32)


def route_kernel(exp_dev, me_ref, routes_ref, gates_ref, cot_ref, info_ref, slot_col_ref, gate_col_ref, *rest):
    out_refs, scratch = rest[:-1], rest[-1]
    n_img, seq, width = cot_ref.shape
    experts = info_ref.shape[2]
    capp = out_refs[0].shape[1]
    me = me_ref[0]
    expert = lax.broadcasted_iota(jnp.int32, (experts, seq), 0)
    expert = ((expert // exp_dev) ^ me) * exp_dev + expert % exp_dev
    earlier = lax.broadcasted_iota(jnp.int32, (seq, seq), 0)
    later = lax.broadcasted_iota(jnp.int32, (seq, seq), 1)
    tri = jnp.where(earlier < later, 1.0, 0.0).astype(BF16)
    carry = jnp.zeros((experts, 1), F32)
    slots, gate_rows = [], []
    for i in range(n_img):
        hit0 = expert == routes_ref[i, 0:1, :]
        hit1 = expert == routes_ref[i, 1:2, :]
        member = jnp.where(hit0 | hit1, 1.0, 0.0)
        slot = jnp.where(member > 0.5, dot_nn(member.astype(BF16), tri) + carry, -1.0)
        gate = jnp.where(hit0, gates_ref[i, 0:1, :], jnp.where(hit1, gates_ref[i, 1:2, :], 0.0))
        carry = carry + jnp.sum(member, axis=1, keepdims=True)
        slots.append(slot)
        gate_rows.append(gate)
        info_ref[0, i] = slot
        info_ref[1, i] = gate
        scratch[0, 0:experts, 0:seq] = slot
        scratch[1, 0:experts, 0:seq] = gate
        slot_col_ref[i] = jnp.transpose(scratch[0])[:seq, :experts]
        gate_col_ref[i] = jnp.transpose(scratch[1])[:seq, :experts]
    place = slot_places(capp, seq)
    sources = [cot_ref.at[i] for i in range(n_img)]
    for e in range(len(out_refs) * exp_dev):
        out_refs[e // exp_dev][e % exp_dev] = dispatch_rows(place, slots, gate_rows, sources, e)


def route_call(me, routes, gates, cotangent, ep_size, exp_dev, capp):
    n_img, seq, width = cotangent.shape
    experts = ep_size * exp_dev
    seq_pad = -(-seq // 128) * 128
    chunk = jax.ShapeDtypeStruct((exp_dev, capp, width), BF16)
    return pl.pallas_call(
        functools.partial(route_kernel, exp_dev),
        in_specs=[pl.BlockSpec(memory_space=pltpu.SMEM)] + [pl.BlockSpec(memory_space=pltpu.VMEM)] * 3,
        out_specs=[pl.BlockSpec(memory_space=pltpu.VMEM)] * (3 + ep_size // 2),
        out_shape=[
            jax.ShapeDtypeStruct((2, n_img, experts, seq), F32),
            jax.ShapeDtypeStruct((n_img, seq, experts), F32),
            jax.ShapeDtypeStruct((n_img, seq, experts), F32),
        ]
        + [chunk] * (ep_size // 2),
        scratch_shapes=[pltpu.VMEM((2, 128, seq_pad), F32)],
        compiler_params=params(16),
        cost_estimate=cost(4),
        name="route_and_dispatch_cotangent",
    )(me, routes.transpose(0, 2, 1), gates.transpose(0, 2, 1), cotangent)


def gateway_kernel(exp_dev, info_ref, cot_ref, *out_refs):
    n_img, seq, width = cot_ref.shape
    capp = out_refs[0].shape[1]
    place = slot_places(capp, seq)
    slots = [info_ref[0, i] for i in range(n_img)]
    gate_rows = [info_ref[1, i] for i in range(n_img)]
    sources = [cot_ref.at[i] for i in range(n_img)]
    half = len(out_refs)
    for j in range(half):
        for k in range(exp_dev):
            out_refs[j][k] = dispatch_rows(place, slots, gate_rows, sources, (half ^ j) * exp_dev + k)


def gateway_call(info, cotangent, ep_size, exp_dev, capp):
    chunk = jax.ShapeDtypeStruct((exp_dev, capp, cotangent.shape[2]), BF16)
    return pl.pallas_call(
        functools.partial(gateway_kernel, exp_dev),
        in_specs=[pl.BlockSpec(memory_space=pltpu.VMEM)] * 2,
        out_specs=[pl.BlockSpec(memory_space=pltpu.VMEM)] * (ep_size // 2),
        out_shape=[chunk] * (ep_size // 2),
        compiler_params=params(16),
        cost_estimate=cost(3),
        name="dispatch_far_cotangent",
    )(info, cotangent)


def attention_kernel(
    heads, tok_ref, w_qkv_ref, w_out_ref, vec_ref, info_ref, qkv_ref, att_ref, lse_ref, resid_ref, *rest
):
    out_refs, second_ref = rest[:-1], rest[-1]
    img = pl.program_id(0)
    seq, width = tok_ref.shape[1:]
    exp_dev, capp = out_refs[0].shape[:2]
    inputs = tok_ref[0].astype(F32)
    norm_first, _ = norm_parts(inputs)
    first = (norm_first * vec_ref[0:1, :] + vec_ref[1:2, :]).astype(BF16)
    qkv = dot_nn(first, w_qkv_ref[...]).astype(BF16)
    qkv_ref[0] = qkv
    low = lax.broadcasted_iota(jnp.int32, (seq, 2 * HD), 1) < HD
    nothing = jnp.zeros((seq, 2 * HD), BF16)
    lane = lax.broadcasted_iota(jnp.int32, (seq, 128), 1)
    lse_all = jnp.zeros((seq, 128), F32)
    pieces = []
    for pair in range(heads // 2):
        at = pair * 2 * HD
        query = qkv[:, at : at + 2 * HD] * jnp.asarray(HD ** (-0.5), BF16)
        key = qkv[:, width + at : width + at + 2 * HD]
        value = qkv[:, 2 * width + at : 2 * width + at + 2 * HD]
        halves = []
        for half in range(2):
            mine = low if half == 0 else jnp.logical_not(low)
            scores = dot_nt(jnp.where(mine, query, nothing), key)
            top = jnp.max(scores, axis=-1, keepdims=True)
            weight = jnp.exp(scores - top)
            total = jnp.sum(weight, axis=-1, keepdims=True)
            prob = (weight * (1.0 / total)).astype(BF16)
            halves.append(dot_nn(prob, value))
            lse_all = jnp.where(lane == 2 * pair + half, top + jnp.log(total), lse_all)
        pieces.append(jnp.where(low, halves[0], halves[1]).astype(BF16))
    lse_ref[0] = lse_all
    attended = jnp.concatenate(pieces, axis=1)
    att_ref[0] = attended
    resid = inputs + dot_nn(attended, w_out_ref[...]) + vec_ref[2:3, :]
    resid_ref[0] = resid
    norm_second, _ = norm_parts(resid)
    second_ref[img] = (norm_second * vec_ref[3:4, :] + vec_ref[4:5, :]).astype(BF16)

    @pl.when(img == pl.num_programs(0) - 1)
    def _():
        n_img = second_ref.shape[0]
        place = slot_places(capp, seq)
        slots = [info_ref[0, i] for i in range(n_img)]
        sources = [second_ref.at[i] for i in range(n_img)]
        for e in range(len(out_refs) * exp_dev):
            out_refs[e // exp_dev][e % exp_dev] = dispatch_rows(place, slots, None, sources, e)


def attention_call(tokens, w_qkv, w_out, vecs, info, ep_size, exp_dev, capp):
    n_img, seq, width = tokens.shape
    chunk = jax.ShapeDtypeStruct((exp_dev, capp, width), BF16)
    image = lambda *tail: pl.BlockSpec((1,) + tail, lambda i: (i, 0, 0))
    return pl.pallas_call(
        functools.partial(attention_kernel, width // HD),
        grid=(n_img,),
        in_specs=[image(seq, width), whole(w_qkv.shape), whole(w_out.shape), whole(vecs.shape), whole(info.shape)],
        out_specs=[image(seq, 3 * width), image(seq, width), image(seq, 128), image(seq, width)]
        + [whole(chunk.shape)] * ep_size,
        out_shape=[
            pltpu.HBM((n_img, seq, 3 * width), BF16),
            pltpu.HBM((n_img, seq, width), BF16),
            pltpu.HBM((n_img, seq, 128), F32),
            pltpu.HBM((n_img, seq, width), F32),
        ]
        + [chunk] * ep_size,
        scratch_shapes=[pltpu.VMEM((n_img, seq, width), BF16)],
        compiler_params=params(32, "arbitrary"),
        cost_estimate=cost(14),
        name="attention_forward_and_dispatch",
    )(tokens, w_qkv, w_out, vecs, info)


def expert_kernel(count, carried, blocks, tile, sel_ref, *refs):
    x_refs, g_refs = refs[:count], refs[count : 2 * count]
    w_in_ref, w_back_ref, b_in_ref, b_back_ref = refs[2 * count : 2 * count + 4]
    before = refs[2 * count + 4 : 2 * count + 4 + carried]
    outs = refs[2 * count + 4 + carried :]
    out_refs, gdis_refs = outs[:count], outs[count : 2 * count]
    sums, (gb_in_ref, gb_back_ref) = outs[2 * count : 2 * count + 4], outs[2 * count + 4 : 2 * count + 6]
    acc_out, acc_dis = outs[2 * count + 6 :]
    exp_dev, _, hidden = w_in_ref.shape
    block = hidden // blocks
    for l in range(exp_dev):
        e = sel_ref[0] ^ l
        own = pl.ds(e, 1)
        for t in range(hidden // tile):
            span = slice(t * tile, (t + 1) * tile)
            w_in, w_back = w_in_ref[e, :, span], w_back_ref[e, span, :]
            gw_back = gw_in = gb_in = None
            for n in range(count):
                x, g = x_refs[n][e], g_refs[n][e]
                pre = dot_nn(x, w_in) + b_in_ref[own, span]
                square = pre * pre
                bent = jnp.tanh(pre * (GELU_C + (GELU_C * 0.044715) * square))
                half = 0.5 + 0.5 * bent
                value = pre * half
                act = value.astype(BF16)
                slope = half + (value - value * half) * (2 * GELU_C + (6 * GELU_C * 0.044715) * square)
                gpre = (dot_nt(g, w_back) * slope).astype(BF16)
                part_dis, part_out = dot_nt(gpre, w_in), dot_nn(act, w_back)
                if t == 0:
                    part_out = part_out + b_back_ref[own, :]
                else:
                    part_dis, part_out = part_dis + acc_dis[n], part_out + acc_out[n]
                if span.stop == hidden:
                    gdis_refs[n][e] = part_dis.astype(BF16)
                    out_refs[n][e] = part_out.astype(BF16)
                else:
                    acc_dis[n] = part_dis
                    acc_out[n] = part_out
                one = (dot_tn(act, g), dot_tn(x, gpre), jnp.sum(gpre.astype(F32), axis=0, keepdims=True))
                gw_back = one[0] if n == 0 else gw_back + one[0]
                gw_in = one[1] if n == 0 else gw_in + one[1]
                gb_in = one[2] if n == 0 else gb_in + one[2]
            gb_in_ref[own, span] = gb_in
            for b in range(t * tile // block, (t + 1) * tile // block):
                at = slice(b * block - t * tile, (b + 1) * block - t * tile)
                at_back, at_in = b ^ sel_ref[1], b ^ sel_ref[2]
                back, into = gw_back[at, :], gw_in[:, at]
                if carried:
                    back = back + before[2 * l][at_back].astype(F32)
                    into = into + before[2 * l + 1][at_in].astype(F32)
                sums[2 * l][at_back] = back.astype(BF16)
                sums[2 * l + 1][at_in] = into.astype(BF16)
        total = jnp.sum(g_refs[0][e].astype(F32), axis=0, keepdims=True)
        for n in range(1, count):
            total = total + jnp.sum(g_refs[n][e].astype(F32), axis=0, keepdims=True)
        gb_back_ref[own, :] = total


def expert_call(xs, gs, w_in, w_back, b_in, b_back, place, blocks, before, microseconds):
    count = len(xs)
    exp_dev, capp, width = xs[0].shape
    hidden = w_in.shape[2]
    block = hidden // blocks
    tile = max(block, min(hidden, 1024))
    narrow = jax.ShapeDtypeStruct((exp_dev, capp, width), BF16)
    shapes = [jax.ShapeDtypeStruct((blocks, block, width), BF16), jax.ShapeDtypeStruct((blocks, width, block), BF16)] * 2
    held = pl.BlockSpec(memory_space=pltpu.VMEM)
    first = 1 + 2 * count + 4
    res = pl.pallas_call(
        functools.partial(expert_kernel, count, len(before), blocks, tile),
        in_specs=[pl.BlockSpec(memory_space=pltpu.SMEM)] + [held] * (2 * count + 4 + len(before)),
        out_specs=[held] * (2 * count + 6),
        out_shape=[narrow] * (2 * count)
        + shapes
        + [jax.ShapeDtypeStruct(b_in.shape, F32), jax.ShapeDtypeStruct(b_back.shape, F32)],
        scratch_shapes=[pltpu.VMEM((count, capp, width), F32)] * 2,
        input_output_aliases={first + k: 2 * count + k for k in range(len(before))},
        compiler_params=params(30),
        cost_estimate=cost(microseconds),
        name="experts",
    )(place, *xs, *gs, w_in, w_back, b_in, b_back, *before)
    return res[:count], res[count : 2 * count], res[2 * count : 2 * count + 4], res[2 * count + 4 :]


def gather_rows(slot_col, value_col, chunk_refs, capp):
    seq = slot_col.shape[0]
    exp_dev = chunk_refs[0].shape[0]
    place = lax.broadcasted_iota(jnp.int32, (seq, capp), 1).astype(F32)
    total = None
    for e in range(len(chunk_refs) * exp_dev):
        value = 1.0 if value_col is None else value_col[:, e : e + 1]
        pick = jnp.where(place == slot_col[:, e : e + 1], value, 0.0).astype(BF16)
        part = dot_nn(pick, chunk_refs[e // exp_dev][e % exp_dev])
        total = part if total is None else total + part
    return total


def backward_kernel(
    heads, ep_size, pack_blocks, place_ref, bias_ref, tok_ref, cot_ref, resid_ref, qkv_ref, att_ref, lse_ref, slot_col_ref, w_qkv_ref, w_out_ref, vec_ref, *rest
):
    chunk_refs = rest[:ep_size]
    packed = 1 if pack_blocks else 0
    gtok_ref = rest[ep_size]
    pack_refs = rest[ep_size + 1 : ep_size + 1 + packed]
    gw_qkv_ref, gw_out_ref, gvec_ref, gqkv_ref = rest[ep_size + 1 + packed : ep_size + 5 + packed]
    img = pl.program_id(0)
    seq, width = tok_ref.shape[1:]
    capp = chunk_refs[0].shape[1]
    grad_second = gather_rows(slot_col_ref[0], None, chunk_refs, capp)
    norm_second, inv_second = norm_parts(resid_ref[0])
    grad_resid = cot_ref[0].astype(F32) + norm_back(grad_second, norm_second, inv_second, vec_ref[3:4, :])
    grad_branch = grad_resid.astype(BF16)
    grad_att = dot_nt(grad_branch, w_out_ref[...]).astype(BF16)
    gw_out = dot_tn(att_ref[0], grad_branch)
    low = lax.broadcasted_iota(jnp.int32, (seq, 2 * HD), 1) < HD
    nothing = jnp.zeros((seq, 2 * HD), BF16)
    scale = jnp.asarray(HD ** (-0.5), BF16)
    for pair in range(heads // 2):
        at = pair * 2 * HD
        query = qkv_ref[0, :, at : at + 2 * HD] * scale
        key = qkv_ref[0, :, width + at : width + at + 2 * HD]
        value = qkv_ref[0, :, 2 * width + at : 2 * width + at + 2 * HD]
        gatt = grad_att[:, at : at + 2 * HD]
        grad_q = grad_k = grad_v = None
        for half in range(2):
            mine = low if half == 0 else jnp.logical_not(low)
            head = 2 * pair + half
            query_h = jnp.where(mine, query, nothing)
            gatt_h = jnp.where(mine, gatt, nothing)
            key_h = jnp.where(mine, key, nothing) * scale
            prob = jnp.exp(dot_nt(query_h, key) - lse_ref[0, :, head : head + 1])
            grad_prob = dot_nt(gatt_h, value)
            mean = jnp.sum(grad_prob * prob, axis=-1, keepdims=True)
            grad_scores = (prob * (grad_prob - mean)).astype(BF16)
            part_v = dot_tn(prob.astype(BF16), gatt_h)
            part_q = dot_nn(grad_scores, key_h)
            part_k = dot_tn(grad_scores, query_h)
            grad_q = part_q if grad_q is None else grad_q + part_q
            grad_k = part_k if grad_k is None else grad_k + part_k
            grad_v = part_v if grad_v is None else grad_v + part_v
        gqkv_ref[:, at : at + 2 * HD] = grad_q.astype(BF16)
        gqkv_ref[:, width + at : width + at + 2 * HD] = grad_k.astype(BF16)
        gqkv_ref[:, 2 * width + at : 2 * width + at + 2 * HD] = grad_v.astype(BF16)
    grad_qkv = gqkv_ref[...]
    norm_first, inv_first = norm_parts(tok_ref[0].astype(F32))
    first = (norm_first * vec_ref[0:1, :] + vec_ref[1:2, :]).astype(BF16)
    gw_qkv = dot_tn(first, grad_qkv)
    grad_first = dot_nt(grad_qkv, w_qkv_ref[...])
    gtok_ref[0] = (grad_resid + norm_back(grad_first, norm_first, inv_first, vec_ref[0:1, :])).astype(BF16)
    sums = [
        grad_first * norm_first,
        grad_first,
        grad_branch.astype(F32),
        grad_second * norm_second,
        grad_second,
    ]
    gvec = jnp.concatenate([jnp.sum(v, axis=0, keepdims=True) for v in sums] + [jnp.zeros((3, width), F32)], axis=0)

    @pl.when(img == 0)
    def _():
        gw_out_ref[...] = gw_out
        gw_qkv_ref[...] = gw_qkv
        gvec_ref[...] = gvec

    @pl.when(img > 0)
    def _():
        gw_out_ref[...] += gw_out
        gw_qkv_ref[...] += gw_qkv
        gvec_ref[...] += gvec

    if not packed:
        return

    @pl.when(img == pl.num_programs(0) - 1)
    def _():
        small_ref = rest[-1]
        blocks, _, rows = pack_refs[0].shape[:3]
        per_ep = width // ep_size
        biases = bias_ref.shape[0]
        small_ref[...] = jnp.zeros(small_ref.shape, F32)
        for j in range(ep_size):
            owner = place_ref[0] ^ j
            small_ref[0:8, :] = gvec_ref[:, pl.ds(pl.multiple_of(owner * per_ep, per_ep), per_ep)]
            small_ref[8 : 8 + biases, :] = bias_ref[...] if j == 0 else jnp.zeros(bias_ref.shape, F32)
            for r in range(blocks):
                block = pack_blocks[r] ^ place_ref[1]
                start = pl.multiple_of(owner * per_ep + block * rows, rows)
                into = pack_refs[0]
                into[r, j, :, 0 : 3 * width] = gw_qkv_ref[pl.ds(start, rows), :].astype(BF16)
                into[r, j, :, 3 * width : 4 * width] = gw_out_ref[pl.ds(start, rows), :].astype(BF16)
                small = small_ref[pl.ds(pl.multiple_of(block * rows, rows), rows), :]
                into[r, j, :, 4 * width :] = small.astype(BF16)


def backward_call(tokens, cotangent, resid, qkv, attended, lse, slot_col, w_qkv, w_out, vecs, chunks, place, biases, pack_blocks):
    n_img, seq, width = tokens.shape
    ep_size = len(chunks)
    packed = 1 if pack_blocks else 0
    image = lambda arr: pl.BlockSpec((1,) + arr.shape[1:], lambda i: (i, 0, 0))
    sums = [
        jax.ShapeDtypeStruct(w_qkv.shape, F32),
        jax.ShapeDtypeStruct(w_out.shape, F32),
        jax.ShapeDtypeStruct((8, width), F32),
    ]
    scratch = [pltpu.VMEM((seq, 3 * width), BF16)]
    if packed:
        grp_size = len(pack_blocks)
        pack = (grp_size, ep_size, width // (ep_size * grp_size), 4 * width + 128)
        outs = [jax.ShapeDtypeStruct(pack, BF16)]
        scratch = [pltpu.VMEM(v.shape, F32) for v in sums] + scratch + [pltpu.VMEM((width // ep_size, 128), F32)]
    else:
        outs = sums
        place, biases = jnp.zeros((2,), jnp.int32), jnp.zeros((8, 128), F32)
    return pl.pallas_call(
        functools.partial(backward_kernel, width // HD, ep_size, pack_blocks),
        grid=(n_img,),
        in_specs=[pl.BlockSpec(memory_space=pltpu.SMEM), whole(biases.shape)]
        + [image(a) for a in (tokens, cotangent, resid, qkv, attended, lse, slot_col)]
        + [whole(a.shape) for a in (w_qkv, w_out, vecs, *chunks)],
        out_specs=[image(tokens)] + [whole(v.shape) for v in outs],
        out_shape=[jax.ShapeDtypeStruct(tokens.shape, BF16)] + outs,
        scratch_shapes=scratch,
        compiler_params=params(40, "arbitrary"),
        cost_estimate=cost(25),
        name="attention_backward",
    )(place, biases, tokens, cotangent, *(pltpu.with_memory_space_constraint(a, pltpu.HBM) for a in (resid, qkv, attended, lse)), slot_col, w_qkv, w_out, vecs, *chunks)


def combine_kernel(ep_size, resid_ref, slot_col_ref, gate_col_ref, *rest):
    chunk_refs, out_ref = rest[:ep_size], rest[ep_size]
    mixed = gather_rows(slot_col_ref[0], gate_col_ref[0], chunk_refs, chunk_refs[0].shape[1])
    out_ref[0] = (resid_ref[0] + mixed).astype(BF16)


def combine_call(resid, slot_col, gate_col, chunks):
    n_img, seq, width = resid.shape
    image = lambda arr: pl.BlockSpec((1,) + arr.shape[1:], lambda i: (i, 0, 0))
    return pl.pallas_call(
        functools.partial(combine_kernel, len(chunks)),
        grid=(n_img,),
        in_specs=[image(a) for a in (resid, slot_col, gate_col)] + [whole(c.shape) for c in chunks],
        out_specs=image(resid),
        out_shape=jax.ShapeDtypeStruct(resid.shape, BF16),
        compiler_params=params(16, "arbitrary"),
        cost_estimate=cost(5),
        name="combine_output",
    )(resid, slot_col, gate_col, *chunks)


def swap(array, axis, size, distance):
    return lax.ppermute(array, axis, [(i, i ^ distance) for i in range(size)])


def digits(index, bits):
    number = jnp.zeros((), jnp.int32)
    for bit in bits:
        number = number * 2 + (index >> bit) % 2
    return number


def scatter_step(arrays, bits, size):
    halves = [a.shape[0] // 2 for a in arrays]
    came = [swap(a[h:], "grp", size, 1 << bit) for a, h, bit in zip(arrays, halves, bits)]
    return [a[:h] + c for a, h, c in zip(arrays, halves, came)]


def gather_sums(block, order, size):
    pieces = [block]
    for bit in reversed(order):
        held = pieces[0] if len(pieces) == 1 else jnp.concatenate(pieces)
        pieces = pieces + [swap(held, "grp", size, 1 << bit)]
    return pieces


def widen_kernel(starts, place_ref, *refs):
    piece_refs, out_ref = refs[: len(starts)], refs[-1]
    for start, piece_ref in zip(starts, piece_refs):
        for k in range(piece_ref.shape[0]):
            @pl.when(pl.program_id(0) == start + k)
            def _():
                out_ref[0] = piece_ref[k].astype(F32)


def widen_call(pieces, expert, first, axis, shape, base):
    starts = [sum(p.shape[0] for p in pieces[:k]) for k in range(len(pieces))]
    count = sum(p.shape[0] for p in pieces)
    _, m, n = pieces[0].shape
    at = (lambda r, s: (s[0], r ^ s[1], 0)) if axis == 0 else (lambda r, s: (s[0], 0, r ^ s[1]))
    extra = [] if base is None else [base]
    return pl.pallas_call(
        functools.partial(widen_kernel, starts),
        grid_spec=pltpu.PrefetchScalarGridSpec(
            num_scalar_prefetch=1,
            grid=(count,),
            in_specs=[whole(p.shape) for p in pieces] + [pl.BlockSpec(memory_space=pl.ANY)] * len(extra),
            out_specs=pl.BlockSpec((1, m, n), at),
        ),
        out_shape=jax.ShapeDtypeStruct(shape, F32),
        input_output_aliases={1 + len(pieces): 0} if extra else {},
        compiler_params=params(16, "arbitrary"),
        cost_estimate=cost(4),
        name="expert_gradient_result",
    )(jnp.stack([expert, first]), *pieces, *extra)


def unpack_kernel(width, exp_dev, hidden, offsets, place_ref, *refs):
    piece_refs = refs[: len(offsets)]
    gw_qkv_ref, gw_out_ref, vec_ref, b_in_ref, b_back_ref, small_ref = refs[len(offsets) :]
    rows = piece_refs[0].shape[0]
    for piece_ref, offset in zip(piece_refs, offsets):
        at = pl.ds(pl.multiple_of((place_ref[0] ^ offset) * rows, rows), rows)
        gw_qkv_ref[at, :] = piece_ref[:, 0 : 3 * width].astype(F32)
        gw_out_ref[at, :] = piece_ref[:, 3 * width : 4 * width].astype(F32)
        small_ref[at, :] = piece_ref[:, 4 * width :].astype(F32)
    vec_ref[...] = small_ref[0:8, :]
    row = 8
    for ref, length in ((b_in_ref, hidden), (b_back_ref, width)):
        for e in range(exp_dev):
            for at in range(0, length, 128):
                ref[e : e + 1, at : at + 128] = small_ref[row : row + 1, :]
                row += 1


def unpack_call(pieces, offsets, place, width, exp_dev, hidden):
    rows = pieces[0].shape[0] * len(pieces)
    shapes = [(rows, 3 * width), (rows, width), (8, 128), (exp_dev, hidden), (exp_dev, width)]
    return pl.pallas_call(
        functools.partial(unpack_kernel, width, exp_dev, hidden, offsets),
        in_specs=[pl.BlockSpec(memory_space=pltpu.SMEM)] + [pl.BlockSpec(memory_space=pltpu.VMEM)] * len(pieces),
        out_specs=[pl.BlockSpec(memory_space=pltpu.VMEM)] * len(shapes),
        out_shape=[jax.ShapeDtypeStruct(v, F32) for v in shapes],
        scratch_shapes=[pltpu.VMEM((rows, 128), F32)],
        compiler_params=params(16),
        cost_estimate=cost(5),
        name="parameter_gradient_results",
    )(place, *pieces)


def after(arrays, *others):
    return lax.optimization_barrier((list(arrays), others))[0]


def local(
    tokens,
    routes,
    gates,
    ln1_gain,
    ln1_bias,
    w_qkv,
    w_out,
    out_bias,
    ln2_gain,
    ln2_bias,
    w_in,
    in_bias,
    w_back,
    back_bias,
    cotangent,
):
    images, seq_len, width = tokens.shape
    ep_size = lax.axis_size("ep")
    exp_dev = w_in.shape[0]
    experts = exp_dev * ep_size
    capacity = (images * seq_len * 10 + 4 * experts - 1) // (4 * experts)
    capp = -(-capacity // 8) * 8
    me = lax.axis_index("ep").astype(jnp.int32).reshape(1)
    vecs = jnp.stack([ln1_gain, ln1_bias, out_bias, ln2_gain, ln2_bias] + [jnp.zeros_like(ln1_gain)] * 3)

    grp_size = lax.axis_size("grp")
    grp = lax.axis_index("grp").astype(jnp.int32)
    bits = list(range(grp_size.bit_length() - 1))
    order_a, order_b = bits[1:], bits[:0:-1]
    blocks = grp_size // 2
    core = grp % 2
    block_a, block_b = digits(grp, order_a), digits(grp, order_b)
    half = ep_size // 2

    def over_ep(array, distance):
        return swap(array, "ep", ep_size, distance)

    cot_far = over_ep(cotangent, half)
    info, slot_col, gate_col, *g_all = route_call(me, routes, gates, cotangent, ep_size, exp_dev, capp)
    info_far = over_ep(info, half)
    g_all = [g_all[0]] + [over_ep(g_all[d], d) for d in range(1, half)]
    qkv, attended, lse, resid, *x_send = attention_call(tokens, w_qkv, w_out, vecs, info, ep_size, exp_dev, capp)
    place_e = jnp.stack([1 - core, block_a, block_b])
    x_all = [x_send[0]] + [over_ep(x_send[d], d) for d in range(1, half + 1)]
    groups = [[0]] + [list(range(d, min(d + 2, half + 1))) for d in range(1, half + 1, 2)] + [[d] for d in range(half + 1, ep_size)]
    outs, gdis, gdis_back, sums, bias_sums = [], [], [], (), None
    for number, group in enumerate(groups):
        if number == 1:
            info_far, = after([info_far], sums[0])
            far = gateway_call(info_far, cot_far, ep_size, exp_dev, capp)
            g_all = g_all + [far[0]] + [over_ep(far[j], j) for j in range(1, half)]
            for d in range(half + 1, ep_size):
                send, = after([x_send[d]], *far, *x_all[1:d])
                x_all.append(over_ep(send, d))
        xs, gs = [x_all[d] for d in group], [g_all[d] for d in group]
        if number == 0:
            xs = after(xs, *g_all[1:])
        o, g, sums, sums_b = expert_call(xs, gs, w_in, w_back, in_bias, back_bias, place_e, blocks, tuple(sums), 10 * len(group))
        outs, gdis = outs + list(o), gdis + list(g)
        for d in group:
            send, = after([gdis[d]], *([x_all[-1]] if d >= half else []))
            gdis_back.append(over_ep(send, d) if d else send)
        bias_sums = sums_b if number == 0 else [a + b for a, b in zip(bias_sums, sums_b)]
    gb_in, gb_back = bias_sums
    far_b, far_i, near_b, near_i = sums
    state = [near_b + swap(far_b, "grp", grp_size, 1), near_i + swap(far_i, "grp", grp_size, 1)]
    stages = [state]
    for step in range(len(order_a)):
        state = scatter_step(state, [order_a[step], order_b[step]], grp_size)
        stages.append(state)
    sum_b, sum_i = state
    early = stages[len(stages) // 2]
    resid_late, = after([resid], *early)
    all_b, all_i = gather_sums(sum_b, order_a, grp_size), gather_sums(sum_i, order_b, grp_size)
    hidden = w_in.shape[2]
    packed = width // ep_size == 128 and 128 % (16 * grp_size) == 0
    place, biases, pack_blocks = None, None, ()
    if packed:
        pack_blocks = tuple(range(0, grp_size, 2)) + tuple(range(1, grp_size, 2))
        place = jnp.stack([me[0], grp])
        biases = jnp.concatenate([gb_in.reshape(-1, 128), gb_back.reshape(-1, 128)])
    grad_tokens, *grads = backward_call(
        tokens, cotangent, resid_late, qkv, attended, lse, slot_col, w_qkv, w_out, vecs, gdis_back, place, biases, pack_blocks
    )
    outs_back = [outs[0]]
    for d in range(1, ep_size):
        send, = after([outs[d]], *early, *gdis_back, *([outs_back[-1]] if d > half else []))
        outs_back.append(over_ep(send, d))
    output = combine_call(resid, slot_col, gate_col, outs_back)
    grads = after(grads, sum_b, sum_i, *outs_back[: half + 1])
    if packed:
        chips = grp_size // 2
        pack = grads[0][:chips] + swap(grads[0][chips:], "grp", grp_size, 1)
        pack, = after([pack], all_b[1], all_i[1])
        share = pack[0].astype(F32)
        for c in range(1, chips):
            share = share + swap(pack[c], "grp", grp_size, 2 * c).astype(F32)
        share, *_ = after([share.astype(BF16)], *outs_back[: half + 1])
        total = share[0].astype(F32)
        for d in range(1, ep_size):
            total = total + over_ep(share[d], d).astype(F32)
        total, *_ = after([total.astype(BF16)], all_b[-1], all_i[-1])
        late = total
        pieces = [total] + [swap(total, "grp", grp_size, 2 * c) for c in range(1, chips)]
        offsets = tuple(range(0, grp_size, 2)) + tuple(range(1, grp_size, 2))
        pieces = pieces + [swap(p, "grp", grp_size, 1) for p in pieces]
        gw_qkv, gw_out, gvec, gb_in, gb_back = unpack_call(pieces, offsets, grp.reshape(1), width, exp_dev, hidden)
        gvec = [gvec[k] for k in range(5)]
    else:
        def over_grp(v):
            return lax.psum(v.astype(BF16), "grp").astype(F32)

        def over_all(v):
            return over_grp(lax.psum_scatter(v.astype(BF16), "ep", scatter_dimension=0, tiled=True))

        gw_qkv, gw_out, gvec = grads
        late = gw_qkv
        gw_qkv, gw_out, gb_in, gb_back = over_all(gw_qkv), over_all(gw_out), over_grp(gb_in), over_grp(gb_back)
        gvec = [over_all(gvec[k]) for k in range(5)]
    oth_b = [swap(p, "grp", grp_size, 1) for p in after(all_b, late)]
    oth_i = [swap(p, "grp", grp_size, 1) for p in after(all_i, late)]
    gw_back = widen_call(all_b, core, block_a, 0, w_back.shape, None)
    gw_in = widen_call(all_i, core, block_b, 1, w_in.shape, None)
    gw_back = widen_call(oth_b, 1 - core, block_a, 0, w_back.shape, gw_back)
    gw_in = widen_call(oth_i, 1 - core, block_b, 1, w_in.shape, gw_in)
    return (output, grad_tokens, gvec[0], gvec[1], gw_qkv, gw_out, gvec[2], gvec[3], gvec[4], gw_in, gb_in, gw_back, gb_back)


def solution(mesh):
    rows = P(("grp", "ep"), None, None)
    return jax.shard_map(
        local,
        mesh=mesh,
        in_specs=(rows, rows, rows)
        + (P(),) * 7
        + (P("ep", None, None), P("ep", None), P("ep", None, None), P("ep", None), rows),
        out_specs=(rows, rows)
        + (P("ep"), P("ep"), P("ep", None), P("ep", None), P("ep"), P("ep"), P("ep"))
        + (P("ep", None, None), P("ep", None), P("ep", None, None), P("ep", None)),
        check_vma=False,
    )
```
